32 devices in a mesh: dp: 8 (over z, y), pipe: 4 (over x, core).
Axes of the slice: x: 2, y: 2, z: 4, core: 2. Of those that a mesh axis runs over, the one named last changes fastest.
Arguments:
- inputs: bfloat16 [4, 32, 196, 384], P(None, 'dp'), may hold values from -6 to 6
- patch_masks: int32 [4, 32, 2, 196], P(None, 'dp'), may hold values 0 or 1
- out_grad: bfloat16 [4, 32, 196, 384], P(None, 'dp'), may hold values from -6 to 6
- cross_aff_scale: float32 [2, 384], replicated, may hold values from 0.5 to 2
- cross_aff_shift: float32 [2, 384], replicated, may hold values from -3 to 3
- cross_weight: bfloat16 [2, 196, 196], replicated, may hold values from -0.4375 to 0.4375
- cross_bias: float32 [2, 196], replicated, may hold values from -3 to 3
- cross_scale: float32 [2, 384], replicated, may hold values from 0.3 to 1.5
- mixer_aff_scale: float32 [2, 384], replicated, may hold values from 0.5 to 2
- mixer_aff_shift: float32 [2, 384], replicated, may hold values from -3 to 3
- mixer_in: bfloat16 [2, 384, 1536], replicated, may hold values from -0.3125 to 0.3125
- mixer_in_bias: float32 [2, 1536], replicated, may hold values from -3 to 3
- mixer_out: bfloat16 [2, 1536, 384], replicated, may hold values from -0.21875 to 0.21875
- mixer_out_bias: float32 [2, 384], replicated, may hold values from -3 to 3
- mixer_scale: float32 [2, 384], replicated, may hold values from 0.3 to 1.5
Outputs:
- output: bfloat16 [4, 32, 196, 384], P('pipe', 'dp')
- input_grad: bfloat16 [4, 32, 196, 384], P('pipe', 'dp')
- cross_aff_scale_grad: float32 [2, 384], replicated
- cross_aff_shift_grad: float32 [2, 384], replicated
- cross_weight_grad: float32 [2, 196, 196], replicated
- cross_bias_grad: float32 [2, 196], replicated
- cross_scale_grad: float32 [2, 384], replicated
- mixer_aff_scale_grad: float32 [2, 384], replicated
- mixer_aff_shift_grad: float32 [2, 384], replicated
- mixer_in_grad: float32 [2, 384, 1536], replicated
- mixer_in_bias_grad: float32 [2, 1536], replicated
- mixer_out_grad: float32 [2, 1536, 384], replicated
- mixer_out_bias_grad: float32 [2, 384], replicated
- mixer_scale_grad: float32 [2, 384], replicated
- magnitudes: float32 [2, 2, 2], replicated
The draws below stay inside these ranges and needn't reach their ends.
Inputs may be any that keep to these rules, and one draw needn't show every extreme that they name: `patch_masks`: 1 keeps a patch row, 0 zeroes it.
All inputs are finite; a program needn't handle non-finite values. No bound on the sum of `patch_masks` on one device may be relied on, other than what follows from the above.
Results may differ from the reference program's by a relative error of at most 0.018.
The reference program's roundings to bfloat16 on the way count: a program that leaves them out, or rounds other values in their place, can miss the bound.
Values may be sent and summed in bfloat16 or wider, within the bound.
No kernel may reach another device: no remote copies, remote signals or barrier semaphores. Data moves between devices by JAX's collectives and lax.ppermute only.
A program may use at most 320 MiB of HBM per device.

```python
import math
import jax
import jax.numpy as jnp
from jax import lax

D = 384
FF = 1536
P_SIZE = 196
LAYERS = 2
MICRO = 4
IMAGES = 32


def touch_ends(entries, key, least, high):
    longest = entries.shape.index(max(entries.shape))
    spots = []
    for shift in (0, 1):
        where = [jax.random.randint(jax.random.fold_in(key, axis), (), 0, length) for axis, length in enumerate(entries.shape)]
        where[longest] = (where[longest] + shift) % entries.shape[longest]
        spots.append(tuple(where))
    return entries.at[spots[0]].set(least).at[spots[1]].set(high)


def level_of(stream_key, extent, cuts, smallest, high):
    level, own = 1.0, jax.random.fold_in(stream_key, 6)
    for axis_at, blocks in cuts:
        draws = jnp.exp(jax.random.uniform(jax.random.fold_in(own, axis_at), (blocks,), jnp.float32, smallest / len(cuts), high / len(cuts)))
        level = level * jnp.repeat(draws, extent[axis_at] // blocks).reshape([-1 if axis == axis_at else 1 for axis in range(len(extent))])
    return level


def scatter_about(own_key, extent, deviation, limit, shards=(), held_as=jnp.bfloat16):
    array = deviation * jax.random.normal(own_key, extent, jnp.float32)
    if shards:
        array = array * level_of(own_key, extent, shards, -0.22, 0.18)
    return jnp.clip(array, -limit, limit).astype(held_as)


def setup_inputs(seed: int = 0) -> dict:
    key_of = jax.random.split(jax.random.key(seed), 16)
    inputs = scatter_about(key_of[0], (MICRO, IMAGES, P_SIZE, D), 1.0, 6.0, ((1, 8),))
    patch_masks = touch_ends((jax.random.randint(key_of[1], (MICRO, IMAGES, LAYERS, P_SIZE), 0, 5) < 4).astype(jnp.int32), jax.random.fold_in(key_of[1], 1), 0, 1)
    out_grad = scatter_about(key_of[2], (MICRO, IMAGES, P_SIZE, D), 1.0, 6.0, ((1, 8),))
    cross_aff_scale = jnp.clip(jnp.exp(jax.random.uniform(key_of[3], (LAYERS, D), jnp.float32, math.log(0.5), math.log(2.0))), 0.5, 2.0)
    cross_aff_shift = scatter_about(key_of[4], (LAYERS, D), 0.5, 3.0, (), jnp.float32)
    cross_weight = scatter_about(key_of[5], (LAYERS, P_SIZE, P_SIZE), P_SIZE ** -0.5, 0.4375)
    cross_bias = scatter_about(key_of[6], (LAYERS, P_SIZE), 0.5, 3.0, (), jnp.float32)
    cross_scale = jnp.clip(jnp.exp(jax.random.uniform(key_of[7], (LAYERS, D), jnp.float32, math.log(0.3), math.log(1.5))), 0.3, 1.5)
    mixer_aff_scale = jnp.clip(jnp.exp(jax.random.uniform(key_of[8], (LAYERS, D), jnp.float32, math.log(0.5), math.log(2.0))), 0.5, 2.0)
    mixer_aff_shift = scatter_about(key_of[9], (LAYERS, D), 0.5, 3.0, (), jnp.float32)
    mixer_in = scatter_about(key_of[10], (LAYERS, D, FF), D ** -0.5, 0.3125)
    mixer_in_bias = scatter_about(key_of[11], (LAYERS, FF), 0.5, 3.0, (), jnp.float32)
    mixer_out = scatter_about(key_of[12], (LAYERS, FF, D), (FF // 2) ** -0.5, 0.21875)
    mixer_out_bias = scatter_about(key_of[13], (LAYERS, D), 0.5, 3.0, (), jnp.float32)
    mixer_scale = jnp.clip(jnp.exp(jax.random.uniform(key_of[14], (LAYERS, D), jnp.float32, math.log(0.3), math.log(1.5))), 0.3, 1.5)
    return dict(inputs=inputs, patch_masks=patch_masks, out_grad=out_grad, cross_aff_scale=cross_aff_scale, cross_aff_shift=cross_aff_shift, cross_weight=cross_weight, cross_bias=cross_bias, cross_scale=cross_scale, mixer_aff_scale=mixer_aff_scale, mixer_aff_shift=mixer_aff_shift, mixer_in=mixer_in, mixer_in_bias=mixer_in_bias, mixer_out=mixer_out, mixer_out_bias=mixer_out_bias, mixer_scale=mixer_scale)


HIGH = lax.Precision.HIGHEST

@jax.custom_vjp
def low(v):
    return lax.optimization_barrier(v.astype(jnp.bfloat16)).astype(jnp.float32)

@jax.custom_vjp
def low_back(v):
    return v

def low_keep(v):
    return (low(v), None)

def low_pass(kept, grad):
    return (grad,)

def back_keep(v):
    return (v, None)

def back_low(kept, grad):
    return (low(grad),)
low.defvjp(low_keep, low_pass)
low_back.defvjp(back_keep, back_low)

def cross_block(stream, keep_rows, aff_scale, aff_shift, weight, offset, layer_scale):
    normed = aff_scale * stream + aff_shift
    masked = low(normed * keep_rows[:, :, None])
    mixing = low_back(jnp.einsum('qp,ipd->iqd', weight, masked, precision=HIGH))
    branch = layer_scale * (mixing + offset[None, :, None])
    return (stream + branch, branch, normed)

def mixer_block(stream, aff_scale, aff_shift, inner_weight, inner_bias, outer_weight, outer_bias, layer_scale):
    normed = aff_scale * stream + aff_shift
    hidden = low_back(jnp.einsum('ipd,dh->iph', low(normed), inner_weight, precision=HIGH)) + inner_bias
    fired = low(jax.nn.gelu(hidden, approximate=False))
    result = low_back(jnp.einsum('iph,hd->ipd', fired, outer_weight, precision=HIGH)) + outer_bias
    branch = layer_scale * result
    return (stream + branch, branch, normed)

def forward(weights, inputs, masks):
    layers = weights[2].shape[0]

    def micro_step(running, element):
        stream, keep_all = element
        pieces = []
        for level in range(layers):
            stream, branch, normed = jax.checkpoint(cross_block)(stream, keep_all[:, level, :], weights[0][level], weights[1][level], weights[2][level], weights[3][level], weights[4][level])
            pieces.append(jnp.stack([jnp.sum(branch * branch), jnp.sum(normed * normed)]))
            stream = low_back(low(stream))
            stream, branch, normed = jax.checkpoint(mixer_block)(stream, weights[5][level], weights[6][level], weights[7][level], weights[8][level], weights[9][level], weights[10][level], weights[11][level])
            pieces.append(jnp.stack([jnp.sum(branch * branch), jnp.sum(normed * normed)]))
            if level + 1 < layers:
                stream = low_back(low(stream))
        return (running + jnp.stack(pieces).reshape(layers, 2, 2), stream)
    totals, outputs = lax.scan(micro_step, jnp.zeros((layers, 2, 2), jnp.float32), (inputs, masks))
    return (outputs, totals)

def reference(inputs, patch_masks, out_grad, cross_aff_scale, cross_aff_shift, cross_weight, cross_bias, cross_scale, mixer_aff_scale, mixer_aff_shift, mixer_in, mixer_in_bias, mixer_out, mixer_out_bias, mixer_scale):
    weights = tuple((w.astype(jnp.float32) for w in (cross_aff_scale, cross_aff_shift, cross_weight, cross_bias, cross_scale, mixer_aff_scale, mixer_aff_shift, mixer_in, mixer_in_bias, mixer_out, mixer_out_bias, mixer_scale)))
    data = inputs.astype(jnp.float32)
    masks = patch_masks.astype(jnp.float32)
    outputs, pullback, totals = jax.vjp(lambda w, x: forward(w, x, masks), weights, data, has_aux=True)
    weight_grads, data_grad = pullback(out_grad.astype(jnp.float32))
    images_all = MICRO * IMAGES
    return (outputs.astype(jnp.bfloat16), data_grad.astype(jnp.bfloat16), weight_grads[0] / images_all, weight_grads[1] / images_all, weight_grads[2] / images_all, weight_grads[3] / images_all, weight_grads[4] / images_all, weight_grads[5] / images_all, weight_grads[6] / images_all, weight_grads[7] / images_all, weight_grads[8] / images_all, weight_grads[9] / images_all, weight_grads[10] / images_all, weight_grads[11] / images_all, jnp.sqrt(totals / (images_all * P_SIZE * D)))
```

```python
import jax
import jax.numpy as jnp
from jax import lax
from jax.sharding import PartitionSpec as P

SQRT_HALF = 0.7071067811865476
INV_ROOT_TAU = 0.3989422804014327


def cross_parts(stream, keep_rows, aff_scale, aff_shift, weight, offset):
    normed = aff_scale * stream + aff_shift
    masked = (normed * keep_rows[:, :, None]).astype(jnp.bfloat16)
    mixing = jnp.einsum("qp,ipd->iqd", weight, masked, preferred_element_type=jnp.float32)
    return (normed, masked, mixing + offset[None, :, None])


def cross_forward(stream, keep_rows, aff_scale, aff_shift, weight, offset, layer_scale):
    normed, masked, shifted = cross_parts(stream, keep_rows, aff_scale, aff_shift, weight, offset)
    branch = layer_scale * shifted
    return (stream + branch, jnp.stack([jnp.sum(branch * branch), jnp.sum(normed * normed)]))


def cross_backward(
    stream, upper_grad, keep_rows, aff_scale, aff_shift, weight, offset, layer_scale
):
    normed, masked, shifted = cross_parts(stream, keep_rows, aff_scale, aff_shift, weight, offset)
    scale_grad = jnp.sum(upper_grad * shifted, axis=(0, 1))
    shifted_grad = upper_grad * layer_scale
    offset_grad = jnp.sum(shifted_grad, axis=(0, 2))
    mixing_low = shifted_grad.astype(jnp.bfloat16)
    weight_grad = jnp.einsum("iqd,ipd->qp", mixing_low, masked, preferred_element_type=jnp.float32)
    masked_grad = jnp.einsum("qp,iqd->ipd", weight, mixing_low, preferred_element_type=jnp.float32)
    normed_grad = masked_grad * keep_rows[:, :, None]
    aff_scale_grad = jnp.sum(normed_grad * stream, axis=(0, 1))
    aff_shift_grad = jnp.sum(normed_grad, axis=(0, 1))
    stream_grad = upper_grad + normed_grad * aff_scale
    return (stream_grad, (aff_scale_grad, aff_shift_grad, weight_grad, offset_grad, scale_grad))


def mixer_parts(stream, aff_scale, aff_shift, inner_weight, inner_bias, outer_weight, outer_bias):
    tokens = stream.reshape(-1, stream.shape[-1])
    normed = aff_scale * tokens + aff_shift
    normed_low = normed.astype(jnp.bfloat16)
    hidden = jnp.dot(normed_low, inner_weight, preferred_element_type=jnp.float32) + inner_bias
    gelu_low = jax.nn.gelu(hidden, approximate=False).astype(jnp.bfloat16)
    result = jnp.dot(gelu_low, outer_weight, preferred_element_type=jnp.float32) + outer_bias
    return (tokens, normed, normed_low, hidden, gelu_low, result)


def mixer_forward(
    stream, aff_scale, aff_shift, inner_weight, inner_bias, outer_weight, outer_bias, layer_scale
):
    tokens, normed, normed_low, hidden, gelu_low, result = mixer_parts(
        stream, aff_scale, aff_shift, inner_weight, inner_bias, outer_weight, outer_bias
    )
    branch = layer_scale * result
    leaving = (tokens + branch).reshape(stream.shape)
    return (leaving, jnp.stack([jnp.sum(branch * branch), jnp.sum(normed * normed)]))


def mixer_backward(
    stream,
    upper_grad,
    aff_scale,
    aff_shift,
    inner_weight,
    inner_bias,
    outer_weight,
    outer_bias,
    layer_scale,
):
    tokens, normed, normed_low, hidden, gelu_low, result = mixer_parts(
        stream, aff_scale, aff_shift, inner_weight, inner_bias, outer_weight, outer_bias
    )
    up_rows = upper_grad.reshape(tokens.shape)
    scale_grad = jnp.sum(up_rows * result, axis=0)
    result_grad = up_rows * layer_scale
    outer_bias_grad = jnp.sum(result_grad, axis=0)
    result_low = result_grad.astype(jnp.bfloat16)
    outer_grad = jnp.einsum("th,td->hd", gelu_low, result_low, preferred_element_type=jnp.float32)
    gelu_grad = jnp.einsum(
        "td,hd->th", result_low, outer_weight, preferred_element_type=jnp.float32
    )
    normal_cdf = 0.5 * (1.0 + lax.erf(hidden * SQRT_HALF))
    density = INV_ROOT_TAU * jnp.exp(-0.5 * hidden * hidden)
    hidden_grad = gelu_grad * (normal_cdf + hidden * density)
    inner_bias_grad = jnp.sum(hidden_grad, axis=0)
    hidden_low = hidden_grad.astype(jnp.bfloat16)
    inner_grad = jnp.einsum("td,th->dh", normed_low, hidden_low, preferred_element_type=jnp.float32)
    normed_grad = jnp.einsum(
        "th,dh->td", hidden_low, inner_weight, preferred_element_type=jnp.float32
    )
    aff_scale_grad = jnp.sum(normed_grad * tokens, axis=0)
    aff_shift_grad = jnp.sum(normed_grad, axis=0)
    stream_grad = (up_rows + normed_grad * aff_scale).reshape(stream.shape)
    return (
        stream_grad,
        (
            aff_scale_grad,
            aff_shift_grad,
            inner_grad,
            inner_bias_grad,
            outer_grad,
            outer_bias_grad,
            scale_grad,
        ),
    )


def on_device(
    inputs,
    patch_masks,
    out_grad,
    *weights,
):
    micros = inputs.shape[0]
    depth_count = weights[2].shape[0]
    own = lax.axis_index("pipe")
    per = micros // lax.axis_size("pipe")
    images = per * inputs.shape[1]

    def mine(array):
        part = lax.dynamic_slice_in_dim(array, own * per, per, 0)
        return part.reshape((images,) + part.shape[2:])

    stream = mine(inputs)
    upper = mine(out_grad)
    keep = mine(patch_masks).astype(jnp.float32)
    saved = []
    squares = []
    for layer in range(depth_count):
        saved.append(stream)
        leaving, sums = cross_forward(
            stream.astype(jnp.float32), keep[:, layer], *(w[layer] for w in weights[:5])
        )
        squares.append(sums)
        stream = leaving.astype(jnp.bfloat16)
        saved.append(stream)
        leaving, sums = mixer_forward(stream.astype(jnp.float32), *(w[layer] for w in weights[5:]))
        squares.append(sums)
        stream = leaving.astype(jnp.bfloat16)
    output = stream
    grads = [None] * depth_count
    for layer in reversed(range(depth_count)):
        upper, mixer_terms = mixer_backward(
            saved[2 * layer + 1].astype(jnp.float32),
            upper.astype(jnp.float32),
            *(w[layer] for w in weights[5:]),
        )
        upper = upper.astype(jnp.bfloat16)
        upper, cross_terms = cross_backward(
            saved[2 * layer].astype(jnp.float32),
            upper.astype(jnp.float32),
            keep[:, layer],
            *(w[layer] for w in weights[:5]),
        )
        upper = upper.astype(jnp.bfloat16)
        grads[layer] = cross_terms + mixer_terms
    gradient = tuple((jnp.stack(parts) for parts in zip(*grads)))
    totals = jnp.stack(squares).reshape(depth_count, 2, 2)
    gradient, totals = lax.psum((gradient, totals), ("dp", "pipe"))
    images_all = micros * inputs.shape[1] * lax.axis_size("dp")
    magnitudes = jnp.sqrt(totals / (images_all * inputs.shape[2] * inputs.shape[3]))
    local = (per,) + inputs.shape[1:]
    return (
        output.reshape(local),
        upper.reshape(local),
        *(part / images_all for part in gradient),
        magnitudes,
    )


def solution(mesh):
    in_specs = (
        P(None, "dp", None, None),
        P(None, "dp", None, None),
        P(None, "dp", None, None),
        P(),
        P(),
        P(),
        P(),
        P(),
        P(),
        P(),
        P(),
        P(),
        P(),
        P(),
        P(),
    )
    out_specs = (
        P("pipe", "dp", None, None),
        P("pipe", "dp", None, None),
        P(),
        P(),
        P(),
        P(),
        P(),
        P(),
        P(),
        P(),
        P(),
        P(),
        P(),
        P(),
        P(),
    )
    return jax.shard_map(
        on_device, mesh=mesh, in_specs=in_specs, out_specs=out_specs, check_vma=False
    )
```

```python
import functools

import jax
import jax.numpy as jnp
from jax import lax
from jax.experimental import pallas as pl
from jax.experimental.pallas import tpu as pltpu
from jax.sharding import PartitionSpec as P

SQRT_HALF = 0.7071067811865476
INV_ROOT_TAU = 0.3989422804014327
AXES = ("dp", "pipe")
BLOCKS = 32
HALF = BLOCKS // 2
SCATTERED = 5
LANES = 384
VECTOR_ROWS = 16
BF = jnp.bfloat16
F32 = jnp.float32
VMEM = pl.BlockSpec(memory_space=pltpu.VMEM)
ANY = pl.BlockSpec(memory_space=pl.ANY)
PARAMS = pltpu.CompilerParams(vmem_limit_bytes=56 * 2**20)

CROSS_AFF_SCALE, CROSS_AFF_SHIFT, CROSS_SCALE, CROSS_BIAS = 0, 1, 2, 3
MIXER_AFF_SCALE, MIXER_AFF_SHIFT, MIXER_OUT_BIAS, MIXER_SCALE = 4, 5, 6, 7
MIXER_IN_BIAS = 8
SQUARES = 12


def dot(a, b, a_dim=1, b_dim=0):
    return lax.dot_general(
        a, b, (((a_dim,), (b_dim,)), ((), ())), preferred_element_type=F32
    )


def row_sum(values):
    return jnp.sum(values, axis=0, keepdims=True)


def phase_bits(mesh_shape):
    pipe_bits = [1 << b for b in range(mesh_shape["pipe"].bit_length() - 1)]
    dp_bits = [mesh_shape["pipe"] << b for b in range(mesh_shape["dp"].bit_length() - 1)]
    even = [pipe_bits[0], *pipe_bits[1:], *dp_bits]
    odd = list(even)
    odd[1], odd[2] = even[2], even[1]
    return even, odd


def exchange(values, mesh_shape, phase):
    even, odd = phase_bits(mesh_shape)
    places = range(mesh_shape["dp"] * mesh_shape["pipe"])
    return lax.ppermute(
        values, AXES, [(i, i ^ (odd if i & 1 else even)[phase]) for i in places]
    )


def block_code(mesh_shape, place):
    even, odd = phase_bits(mesh_shape)
    odd_place = place & 1
    code = jnp.int32(0)
    for even_bit, odd_bit in zip(even[:SCATTERED], odd[:SCATTERED]):
        bit = jnp.where(odd_place == 1, (place & odd_bit) != 0, (place & even_bit) != 0)
        code = 2 * code + bit.astype(jnp.int32)
    return code


def own_codes(mesh_shape):
    place = lax.axis_index("dp") * mesh_shape["pipe"] + lax.axis_index("pipe")
    return block_code(mesh_shape, place), block_code(mesh_shape, place ^ 1)


def kept_block(codes, slot):
    return codes[0] ^ slot


def sent_block(codes, slot):
    return codes[1] ^ slot


def inner_spot(block, rows, columns):
    across = columns // LANES
    row_at = pl.multiple_of((block // across) * rows, rows)
    return row_at, pl.multiple_of((block % across) * LANES, LANES)


def pack_blocks(codes, inner_ref, outer_ref, kept_ref, sent_ref, small_ref=None):
    depth = inner_ref.shape[0] * inner_ref.shape[1] // (BLOCKS * LANES)

    def pack(block, slot, out_ref):
        row_at, column_at = inner_spot(block, depth, inner_ref.shape[1])
        out_ref[slot, 0:depth, :] = inner_ref[pl.ds(row_at, depth), pl.ds(column_at, LANES)]
        outer_at = pl.multiple_of(block * depth, depth)
        out_ref[slot, depth : 2 * depth, :] = outer_ref[pl.ds(outer_at, depth), :]
        if small_ref is not None:
            out_ref[slot, 2 * depth :, :] = small_ref[block]

    @pl.loop(0, HALF)
    def _(slot):
        pack(sent_block(codes, slot), slot, sent_ref)
        pack(kept_block(codes, slot), slot, kept_ref)


def pad_masks(mask_ref, keep_ref, layers):
    keep_ref[...] = jnp.zeros_like(keep_ref)
    patches = mask_ref.shape[-1]
    for image in range(mask_ref.shape[0]):
        keep_ref[image, 0:layers, 0:patches] = mask_ref[image].astype(F32)


def pad_rows(source_ref, padded_ref, patches, padded):
    for image in range(source_ref.shape[0]):
        base = image * padded
        padded_ref[base + padded - 16 : base + padded, :] = jnp.zeros((16, LANES), BF)
        padded_ref[base : base + patches, :] = source_ref[image]


def kept_weight(weight_ref, keep_ref, image, layer):
    keep_row = keep_ref[image, layer : layer + 1, :]
    return (weight_ref[layer].astype(F32) * keep_row).astype(BF)


def cross_forward(
    layer, source_ref, target_ref, vectors_ref, keep_ref, weight_ref, bias_ref,
    aff_scale_ref, aff_shift_ref, scale_ref, patches, padded,
):
    aff_scale = aff_scale_ref[layer : layer + 1, :]
    aff_shift = aff_shift_ref[layer : layer + 1, :]
    scale = scale_ref[layer : layer + 1, :]
    branch_squares = jnp.zeros((1, LANES), F32)
    normed_squares = jnp.zeros((1, LANES), F32)
    for image in range(keep_ref.shape[0]):
        rows = slice(image * padded, (image + 1) * padded)
        stream = source_ref[rows, :].astype(F32)
        normed = aff_scale * stream + aff_shift
        mixing = dot(kept_weight(weight_ref, keep_ref, image, layer), normed.astype(BF))
        branch = scale * (mixing + bias_ref[:, layer : layer + 1])
        target_ref[rows, :] = (stream + branch).astype(BF)
        branch_squares += row_sum(branch[0:patches] * branch[0:patches])
        normed_squares += row_sum(normed[0:patches] * normed[0:patches])
    vectors_ref[layer, SQUARES : SQUARES + 1, :] = branch_squares
    vectors_ref[layer, SQUARES + 1 : SQUARES + 2, :] = normed_squares


def mixer_hidden(
    layer, stream_ref, low_ref, fired_ref, slope_ref, vectors_ref,
    aff_scale_ref, aff_shift_ref, inner_ref, inner_bias_ref, images, patches, padded,
):
    aff_scale = aff_scale_ref[layer : layer + 1, :]
    aff_shift = aff_shift_ref[layer : layer + 1, :]
    squares = jnp.zeros((1, LANES), F32)
    for image in range(images):
        rows = slice(image * padded, (image + 1) * padded)
        normed = aff_scale * stream_ref[rows, :].astype(F32) + aff_shift
        low_ref[rows, :] = normed.astype(BF)
        squares += row_sum(normed[0:patches] * normed[0:patches])
    vectors_ref[layer, SQUARES + 3 : SQUARES + 4, :] = squares
    columns = inner_ref.shape[1]
    step = columns // 2

    @pl.loop(0, 2)
    def _(part):
        at = pl.ds(pl.multiple_of(part * step, step), step)
        for image in range(images):
            rows = slice(image * padded, (image + 1) * padded)
            hidden = dot(low_ref[rows, :], inner_ref[:, at]) + inner_bias_ref[layer : layer + 1, at]
            normal_cdf = 0.5 * (1.0 + lax.erf(hidden * SQRT_HALF))
            density = INV_ROOT_TAU * jnp.exp(-0.5 * hidden * hidden)
            fired_ref[rows, at] = (hidden * normal_cdf).astype(BF)
            slope_ref[rows, at] = (normal_cdf + hidden * density).astype(BF)


def mixer_result(layer, fired_ref, outer_ref, outer_bias_ref, rows):
    return dot(fired_ref[rows, :], outer_ref[...]) + outer_bias_ref[layer : layer + 1, :]


def mixer_backward(
    layer, upper_ref, low_ref, fired_ref, slope_ref, scaled_ref, inner_ref, outer_ref,
    inner_grad_ref, outer_grad_ref, vectors_ref, scale_ref, images, padded,
):
    scale = scale_ref[layer : layer + 1, :]
    bias = jnp.zeros((1, LANES), F32)
    for image in range(images):
        rows = slice(image * padded, (image + 1) * padded)
        result_grad = upper_ref[rows, :].astype(F32) * scale
        bias += row_sum(result_grad)
        scaled_ref[rows, :] = result_grad.astype(BF)
    vectors_ref[layer, MIXER_OUT_BIAS : MIXER_OUT_BIAS + 1, :] = bias
    columns = inner_ref.shape[1]
    step = 2 * LANES
    for part in range(columns // step):
        at = slice(part * step, (part + 1) * step)
        outer_grad_ref[at, :] = dot(fired_ref[:, at], scaled_ref[...], 0, 0).astype(BF)
        inner_bias = jnp.zeros((1, step), F32)
        for image in range(images):
            rows = slice(image * padded, (image + 1) * padded)
            hidden_grad = dot(scaled_ref[rows, :], outer_ref[at, :], 1, 1) * slope_ref[
                rows, at
            ].astype(F32)
            inner_bias += row_sum(hidden_grad)
            slope_ref[rows, at] = hidden_grad.astype(BF)
        for piece in range(step // LANES):
            row = MIXER_IN_BIAS + part * (step // LANES) + piece
            vectors_ref[layer, row : row + 1, :] = inner_bias[:, piece * LANES : (piece + 1) * LANES]
        inner_grad_ref[:, at] = dot(low_ref[...], slope_ref[:, at], 0, 0).astype(BF)


def mixer_input_grad(
    layer, upper_ref, stream_ref, hidden_grad_ref, target_ref, inner_ref, vectors_ref,
    aff_scale_ref, images, padded,
):
    aff_scale = aff_scale_ref[layer : layer + 1, :]
    scale_grad = jnp.zeros((1, LANES), F32)
    shift_grad = jnp.zeros((1, LANES), F32)
    for image in range(images):
        rows = slice(image * padded, (image + 1) * padded)
        normed_grad = dot(hidden_grad_ref[rows, :], inner_ref[...], 1, 1)
        scale_grad += row_sum(normed_grad * stream_ref[rows, :].astype(F32))
        shift_grad += row_sum(normed_grad)
        target_ref[rows, :] = (
            upper_ref[rows, :].astype(F32) + normed_grad * aff_scale
        ).astype(BF)
    vectors_ref[layer, MIXER_AFF_SCALE : MIXER_AFF_SCALE + 1, :] = scale_grad
    vectors_ref[layer, MIXER_AFF_SHIFT : MIXER_AFF_SHIFT + 1, :] = shift_grad


def cross_backward(
    layer, stream_ref, upper_ref, target_ref, weight_grad_ref, vectors_ref, keep_ref, weight_ref,
    bias_ref, aff_scale_ref, aff_shift_ref, scale_ref, padded,
):
    aff_scale = aff_scale_ref[layer : layer + 1, :]
    aff_shift = aff_shift_ref[layer : layer + 1, :]
    scale = scale_ref[layer : layer + 1, :]
    aff_scale_grad = jnp.zeros((1, LANES), F32)
    aff_shift_grad = jnp.zeros((1, LANES), F32)
    scale_grad = jnp.zeros((1, LANES), F32)
    bias_grad = jnp.zeros((8, padded), F32)
    weight_grad = jnp.zeros((padded, padded), F32)
    ones = jnp.ones((8, LANES), BF)
    for image in range(keep_ref.shape[0]):
        rows = slice(image * padded, (image + 1) * padded)
        stream = stream_ref[rows, :].astype(F32)
        upper = upper_ref[rows, :].astype(F32)
        normed_low = (aff_scale * stream + aff_shift).astype(BF)
        kept = kept_weight(weight_ref, keep_ref, image, layer)
        shifted = dot(kept, normed_low) + bias_ref[:, layer : layer + 1]
        scale_grad += row_sum(upper * shifted)
        mixing_low = (upper * scale).astype(BF)
        bias_grad += dot(ones, mixing_low, 1, 1)
        weight_grad += dot(mixing_low, normed_low, 1, 1) * keep_ref[image, layer : layer + 1, :]
        normed_grad = dot(kept, mixing_low, 0, 0)
        aff_scale_grad += row_sum(normed_grad * stream)
        aff_shift_grad += row_sum(normed_grad)
        target_ref[rows, :] = (upper + normed_grad * aff_scale).astype(BF)
    weight_grad_ref[layer] = weight_grad
    vectors_ref[layer, CROSS_AFF_SCALE : CROSS_AFF_SCALE + 1, :] = aff_scale_grad
    vectors_ref[layer, CROSS_AFF_SHIFT : CROSS_AFF_SHIFT + 1, :] = aff_shift_grad
    vectors_ref[layer, CROSS_SCALE : CROSS_SCALE + 1, :] = scale_grad
    vectors_ref[layer, CROSS_BIAS : CROSS_BIAS + 1, 0:padded] = bias_grad[0:1]


def cross_setup(mask_ref, weight_ref, keep_ref, padded_weight_ref):
    layers, patches = weight_ref.shape[0], weight_ref.shape[1]
    pad_masks(mask_ref, keep_ref, layers)
    padded_weight_ref[...] = jnp.zeros_like(padded_weight_ref)
    for layer in range(layers):
        padded_weight_ref[layer, 0:patches, 0:patches] = weight_ref[layer]


def first_kernel(
    mesh_shape, patches, padded,
    x_hbm, mask_hbm, g_hbm, cross_weight, inner_hbm, outer_hbm,
    cross_aff_scale, cross_aff_shift, bias_columns, cross_scale,
    mixer_aff_scale, mixer_aff_shift, inner_bias, outer_bias, mixer_scale,
    output, kept, sent, vectors, s1, s2, fired0, slope0, result0, g1,
    x_in, mask_in, g_in, inner0, outer0, inner1, outer1, keep, weight, x_rows, g_rows,
    s3, low, fired1, slope1, scaled, inner_grad, outer_grad, sems,
):
    images = mask_in.shape[0]
    per = x_hbm.shape[0] // mesh_shape["pipe"]
    each = x_hbm.shape[1]
    own = lax.axis_index("pipe") * per
    copies = []
    for number, (source, target) in enumerate(
        ((x_hbm, x_in), (mask_hbm, mask_in), (g_hbm, g_in))
    ):
        for part in range(per):
            copies.append(
                pltpu.make_async_copy(
                    source.at[own + part],
                    target.at[part * each : (part + 1) * each],
                    sems.at[number * per + part],
                )
            )
    base = 3 * per
    for number, (source, target) in enumerate(
        (
            (inner_hbm.at[0], inner0),
            (outer_hbm.at[0], outer0),
            (inner_hbm.at[1], inner1),
            (outer_hbm.at[1], outer1),
        )
    ):
        copies.append(pltpu.make_async_copy(source, target, sems.at[base + number]))
    for copy in copies:
        copy.start()
    for copy in copies[: 2 * per]:
        copy.wait()
    vectors[...] = jnp.zeros_like(vectors)
    cross_setup(mask_in, cross_weight, keep, weight)
    pad_rows(x_in, x_rows, patches, padded)
    cross = (keep, weight, bias_columns, cross_aff_scale, cross_aff_shift, cross_scale)
    cross_forward(0, x_rows, s1, vectors, *cross, patches, padded)
    copies[base].wait()
    mixer = (mixer_aff_scale, mixer_aff_shift)
    mixer_hidden(
        0, s1, low, fired0, slope0, vectors, *mixer, inner0, inner_bias, images, patches, padded
    )
    copies[base + 1].wait()
    squares = jnp.zeros((1, LANES), F32)
    for image in range(images):
        rows = slice(image * padded, (image + 1) * padded)
        result = mixer_result(0, fired0, outer0, outer_bias, rows)
        result0[rows, :] = result.astype(BF)
        branch = mixer_scale[0:1, :] * result
        s2[rows, :] = (s1[rows, :].astype(F32) + branch).astype(BF)
        squares += row_sum(branch[0:patches] * branch[0:patches])
    vectors[0, SQUARES + 2 : SQUARES + 3, :] = squares
    cross_forward(1, s2, s3, vectors, *cross, patches, padded)
    copies[base + 2].wait()
    mixer_hidden(
        1, s3, low, fired1, slope1, vectors, *mixer, inner1, inner_bias, images, patches, padded
    )
    copies[base + 3].wait()
    for copy in copies[2 * per : 3 * per]:
        copy.wait()
    pad_rows(g_in, g_rows, patches, padded)
    mixer_backward(
        1, g_rows, low, fired1, slope1, scaled, inner1, outer1, inner_grad, outer_grad,
        vectors, mixer_scale, images, padded,
    )
    codes = own_codes(mesh_shape)
    pack_blocks(codes, inner_grad, outer_grad, kept, sent)
    squares = jnp.zeros((1, LANES), F32)
    scale_grad = jnp.zeros((1, LANES), F32)
    for image in range(images):
        rows = slice(image * padded, (image + 1) * padded)
        result = mixer_result(1, fired1, outer1, outer_bias, rows)
        scale_grad += row_sum(g_rows[rows, :].astype(F32) * result)
        branch = mixer_scale[1:2, :] * result
        leaving = (s3[rows, :].astype(F32) + branch).astype(BF)
        output[image // each, image % each] = leaving[0:patches]
        squares += row_sum(branch[0:patches] * branch[0:patches])
    vectors[1, SQUARES + 2 : SQUARES + 3, :] = squares
    vectors[1, MIXER_SCALE : MIXER_SCALE + 1, :] = scale_grad
    mixer_input_grad(
        1, g_rows, s3, slope1, g1, inner1, vectors, mixer_aff_scale, images, padded
    )


def second_kernel(
    mesh_shape, patches, padded,
    x_hbm, mask_hbm, cross_weight, inner_hbm, outer_hbm,
    s1, s2, fired0_hbm, slope0_hbm, result0, g1, vectors_in,
    cross_aff_scale, cross_aff_shift, bias_columns, cross_scale,
    mixer_aff_scale, mixer_aff_shift, mixer_scale,
    input_grad, kept, sent,
    x_in, mask_in, inner0, outer0, fired0, slope0, keep, weight, x_rows, g2, low, scaled, g0,
    inner_grad, outer_grad, weight_grad, vectors, small, sems,
):
    images = mask_in.shape[0]
    per = x_hbm.shape[0] // mesh_shape["pipe"]
    each = x_hbm.shape[1]
    own = lax.axis_index("pipe") * per
    copies = []
    for number, (source, target) in enumerate(((mask_hbm, mask_in), (x_hbm, x_in))):
        for part in range(per):
            copies.append(
                pltpu.make_async_copy(
                    source.at[own + part],
                    target.at[part * each : (part + 1) * each],
                    sems.at[number * per + part],
                )
            )
    base = 2 * per
    for number, (source, target) in enumerate(
        (
            (fired0_hbm, fired0),
            (outer_hbm.at[0], outer0),
            (slope0_hbm, slope0),
            (inner_hbm.at[0], inner0),
        )
    ):
        copies.append(pltpu.make_async_copy(source, target, sems.at[base + number]))
    for copy in copies:
        copy.start()
    for copy in copies[:per]:
        copy.wait()
    vectors[...] = vectors_in[...]
    cross_setup(mask_in, cross_weight, keep, weight)
    cross = (keep, weight, bias_columns, cross_aff_scale, cross_aff_shift, cross_scale)
    cross_backward(1, s2, g1, g2, weight_grad, vectors, *cross, padded)
    for image in range(images):
        rows = slice(image * padded, (image + 1) * padded)
        normed = mixer_aff_scale[0:1, :] * s1[rows, :].astype(F32) + mixer_aff_shift[0:1, :]
        low[rows, :] = normed.astype(BF)
    for copy in copies[base:]:
        copy.wait()
    mixer_backward(
        0, g2, low, fired0, slope0, scaled, inner0, outer0, inner_grad, outer_grad,
        vectors, mixer_scale, images, padded,
    )
    vectors[0, MIXER_SCALE : MIXER_SCALE + 1, :] = row_sum(
        g2[...].astype(F32) * result0[...].astype(F32)
    )
    mixer_input_grad(
        0, g2, s1, slope0, scaled, inner0, vectors, mixer_aff_scale, images, padded
    )
    for copy in copies[per:base]:
        copy.wait()
    pad_rows(x_in, x_rows, patches, padded)
    cross_backward(0, x_rows, scaled, g0, weight_grad, vectors, *cross, padded)
    for image in range(images):
        input_grad[image // each, image % each] = g0[image * padded : image * padded + patches, :]
    small[...] = jnp.zeros_like(small)
    groups = padded // VECTOR_ROWS
    layers = cross_weight.shape[0]
    for layer in range(layers):
        for group in range(groups):
            rows = slice(group * VECTOR_ROWS, (group + 1) * VECTOR_ROWS)
            small[layer * groups + group, :, 0:padded] = weight_grad[layer, rows, :].astype(BF)
        small[layers * groups + layer] = vectors[layer].astype(BF)
    pack_blocks(own_codes(mesh_shape), inner_grad, outer_grad, kept, sent, small)


def reduce_blocks(kept, sent, mesh_shape):
    terms = [kept]
    width = HALF
    terms.append(exchange(sent, mesh_shape, 0))
    for phase in range(1, SCATTERED):
        half = width // 2
        leaving = sum(t[half:width].astype(F32) for t in terms).astype(BF)
        terms.append(exchange(leaving, mesh_shape, phase))
        width = half
    total = sum(t[0:1].astype(F32) for t in terms)
    for phase in range(SCATTERED, len(phase_bits(mesh_shape)[0])):
        total = total.astype(BF)
        total = total.astype(F32) + exchange(total, mesh_shape, phase).astype(F32)
    return total.astype(BF)


def gather_blocks(own, mesh_shape):
    held = own
    for phase in reversed(range(1, SCATTERED)):
        held = jnp.concatenate([held, exchange(held, mesh_shape, phase)], axis=0)
    return held, exchange(held, mesh_shape, 0)


def last_kernel(
    mesh_shape, images_all, layers,
    kept1, other1, kept0, other0,
    inner_out, outer_out, weight_out, vectors_out,
):
    codes = own_codes(mesh_shape)
    depth = kept1.shape[1] // 2
    columns = inner_out.shape[2]
    groups = weight_out.shape[1] // VECTOR_ROWS

    def unpack(block, slot, values, layer):
        row_at, column_at = inner_spot(block, depth, columns)
        inner_out[layer, pl.ds(row_at, depth), pl.ds(column_at, LANES)] = (
            values[slot, 0:depth, :].astype(F32) / images_all
        )
        outer_at = pl.multiple_of(block * depth, depth)
        outer_out[layer, pl.ds(outer_at, depth), :] = (
            values[slot, depth : 2 * depth, :].astype(F32) / images_all
        )
        if layer == 0:
            small = values[slot, 2 * depth :, :].astype(F32) / images_all

            @pl.when(block < layers * groups)
            def _():
                at = pl.multiple_of((block % groups) * VECTOR_ROWS, VECTOR_ROWS)
                weight_out[block // groups, pl.ds(at, VECTOR_ROWS), :] = small

            @pl.when((block >= layers * groups) & (block < layers * (groups + 1)))
            def _():
                vectors_out[block - layers * groups] = small

    @pl.loop(0, HALF)
    def _(slot):
        unpack(kept_block(codes, slot), slot, kept1, 1)
        unpack(sent_block(codes, slot), slot, other1, 1)
        unpack(kept_block(codes, slot), slot, kept0, 0)
        unpack(sent_block(codes, slot), slot, other0, 0)


def on_device(
    mesh_shape,
    inputs,
    patch_masks,
    out_grad,
    cross_aff_scale,
    cross_aff_shift,
    cross_weight,
    cross_bias,
    cross_scale,
    mixer_aff_scale,
    mixer_aff_shift,
    mixer_in,
    mixer_in_bias,
    mixer_out,
    mixer_out_bias,
    mixer_scale,
):
    micros, each, patches, width = inputs.shape
    layers, _, columns = mixer_in.shape
    per = micros // mesh_shape["pipe"]
    images = per * each
    padded = -(-patches // 16) * 16
    rows = images * padded
    depth = width * columns // (BLOCKS * LANES)
    bias_columns = jnp.pad(cross_bias.T, ((0, padded - patches), (0, 0)))

    def struct(*shape, dtype=BF):
        return jax.ShapeDtypeStruct(shape, dtype)

    def scratch(*shape, dtype=BF):
        return pltpu.VMEM(shape, dtype)

    local = (per, each, patches, width)
    taken = [
        scratch(images, patches, width),
        scratch(images, layers, patches, dtype=jnp.int32),
    ]
    first_outs = (
        struct(*local),
        struct(HALF, 2 * depth, LANES),
        struct(HALF, 2 * depth, LANES),
        struct(layers, VECTOR_ROWS, LANES, dtype=F32),
        struct(rows, width),
        struct(rows, width),
        struct(rows, columns),
        struct(rows, columns),
        struct(rows, width),
        struct(rows, width),
    )
    output, kept1, sent1, vectors, s1, s2, fired0, slope0, result0, g1 = pl.pallas_call(
        functools.partial(first_kernel, mesh_shape, patches, padded),
        out_shape=first_outs,
        in_specs=[ANY] * 3 + [VMEM] + [ANY] * 2 + [VMEM] * 9,
        out_specs=[VMEM] * len(first_outs),
        scratch_shapes=[
            *taken,
            scratch(images, patches, width),
            scratch(width, columns),
            scratch(columns, width),
            scratch(width, columns),
            scratch(columns, width),
            scratch(images, 8, padded, dtype=F32),
            scratch(layers, padded, padded),
            scratch(rows, width),
            scratch(rows, width),
            scratch(rows, width),
            scratch(rows, width),
            scratch(rows, columns),
            scratch(rows, columns),
            scratch(rows, width),
            scratch(width, columns),
            scratch(columns, width),
            pltpu.SemaphoreType.DMA((3 * per + 4,)),
        ],
        compiler_params=PARAMS,
        name="forward_and_top",
    )(
        inputs, patch_masks, out_grad, cross_weight, mixer_in, mixer_out,
        cross_aff_scale, cross_aff_shift, bias_columns, cross_scale,
        mixer_aff_scale, mixer_aff_shift, mixer_in_bias, mixer_out_bias, mixer_scale,
    )
    second_outs = (
        struct(*local),
        struct(HALF, 2 * depth + VECTOR_ROWS, LANES),
        struct(HALF, 2 * depth + VECTOR_ROWS, LANES),
    )
    input_grad, kept0, sent0 = pl.pallas_call(
        functools.partial(second_kernel, mesh_shape, patches, padded),
        out_shape=second_outs,
        in_specs=[ANY] * 2 + [VMEM] + [ANY] * 2 + [VMEM] * 2 + [ANY] * 2 + [VMEM] * 10,
        out_specs=[VMEM] * len(second_outs),
        scratch_shapes=[
            *taken,
            scratch(width, columns),
            scratch(columns, width),
            scratch(rows, columns),
            scratch(rows, columns),
            scratch(images, 8, padded, dtype=F32),
            scratch(layers, padded, padded),
            scratch(rows, width),
            scratch(rows, width),
            scratch(rows, width),
            scratch(rows, width),
            scratch(rows, width),
            scratch(width, columns),
            scratch(columns, width),
            scratch(layers, padded, padded, dtype=F32),
            scratch(layers, VECTOR_ROWS, LANES, dtype=F32),
            scratch(BLOCKS, VECTOR_ROWS, LANES),
            pltpu.SemaphoreType.DMA((2 * per + 4,)),
        ],
        compiler_params=PARAMS,
        name="rest_of_backward",
    )(
        inputs, patch_masks, cross_weight, mixer_in, mixer_out,
        s1, s2, fired0, slope0, result0, g1, vectors,
        cross_aff_scale, cross_aff_shift, bias_columns, cross_scale,
        mixer_aff_scale, mixer_aff_shift, mixer_scale,
    )
    gathered1 = gather_blocks(reduce_blocks(kept1, sent1, mesh_shape), mesh_shape)
    gathered0 = gather_blocks(reduce_blocks(kept0, sent0, mesh_shape), mesh_shape)
    images_all = micros * each * mesh_shape["dp"]
    last_outs = (
        struct(layers, width, columns, dtype=F32),
        struct(layers, columns, width, dtype=F32),
        struct(layers, padded, LANES, dtype=F32),
        struct(layers, VECTOR_ROWS, LANES, dtype=F32),
    )
    inner_grad, outer_grad, weight_grad, sums = pl.pallas_call(
        functools.partial(last_kernel, mesh_shape, images_all, layers),
        out_shape=last_outs,
        in_specs=[VMEM] * 4,
        out_specs=[VMEM] * len(last_outs),
        compiler_params=PARAMS,
        name="unpack",
    )(*gathered1, *gathered0)
    squares = jnp.sum(sums[:, SQUARES:], axis=2).reshape(layers, 2, 2)
    return (
        output,
        input_grad,
        sums[:, CROSS_AFF_SCALE],
        sums[:, CROSS_AFF_SHIFT],
        weight_grad[:, :patches, :patches],
        sums[:, CROSS_BIAS, :patches],
        sums[:, CROSS_SCALE],
        sums[:, MIXER_AFF_SCALE],
        sums[:, MIXER_AFF_SHIFT],
        inner_grad,
        sums[:, MIXER_IN_BIAS:SQUARES].reshape(layers, columns),
        outer_grad,
        sums[:, MIXER_OUT_BIAS],
        sums[:, MIXER_SCALE],
        jnp.sqrt(squares / (patches * width)),
    )


def solution(mesh):
    split = P(None, "dp", None, None)
    owned = P("pipe", "dp", None, None)
    return jax.shard_map(
        functools.partial(on_device, dict(mesh.shape)),
        mesh=mesh,
        in_specs=(split,) * 3 + (P(),) * 12,
        out_specs=(owned,) * 2 + (P(),) * 13,
        check_vma=False,
    )
```

```python
import functools

import jax
import jax.numpy as jnp
from jax import lax
from jax.experimental import pallas as pl
from jax.experimental.pallas import tpu as pltpu
from jax.sharding import PartitionSpec as P

SQRT_HALF = 0.7071067811865476
INV_ROOT_TAU = 0.3989422804014327
AXES = ("dp", "pipe")
BLOCKS = 32
HALF = BLOCKS // 2
SCATTERED = 5
LANES = 384
VECTOR_ROWS = 16
BF = jnp.bfloat16
F32 = jnp.float32
VMEM = pl.BlockSpec(memory_space=pltpu.VMEM)
HBM = pl.BlockSpec(memory_space=pltpu.HBM)
VMEM_LIMIT = 28 * 2**20

CROSS_AFF_SCALE, CROSS_AFF_SHIFT, CROSS_SCALE, CROSS_BIAS = 0, 1, 2, 3
MIXER_AFF_SCALE, MIXER_AFF_SHIFT, MIXER_OUT_BIAS, MIXER_SCALE = 4, 5, 6, 7
MIXER_IN_BIAS = 8
SQUARES = 12


def dot(a, b, a_dim=1, b_dim=0):
    return lax.dot_general(
        a, b, (((a_dim,), (b_dim,)), ((), ())), preferred_element_type=F32
    )


def row_sum(values):
    return jnp.sum(values, axis=0, keepdims=True)


def phase_bits(mesh_shape):
    pipe_bits = [1 << b for b in range(mesh_shape["pipe"].bit_length() - 1)]
    dp_bits = [mesh_shape["pipe"] << b for b in range(mesh_shape["dp"].bit_length() - 1)]
    even = [pipe_bits[0], *pipe_bits[1:], *dp_bits]
    odd = list(even)
    odd[1], odd[2] = even[2], even[1]
    return even, odd


def block_code(mesh_shape, place):
    even, odd = phase_bits(mesh_shape)
    odd_place = place & 1
    code = jnp.int32(0)
    for even_bit, odd_bit in zip(even[:SCATTERED], odd[:SCATTERED]):
        bit = jnp.where(odd_place == 1, (place & odd_bit) != 0, (place & even_bit) != 0)
        code = 2 * code + bit.astype(jnp.int32)
    return code


def own_codes(mesh_shape):
    place = lax.axis_index("dp") * mesh_shape["pipe"] + lax.axis_index("pipe")
    return block_code(mesh_shape, place), block_code(mesh_shape, place ^ 1)


def kept_block(codes, slot):
    return codes[0] ^ slot


def sent_block(codes, slot):
    return codes[1] ^ slot


def inner_spot(block, rows, columns):
    across = columns // LANES
    row_at = pl.multiple_of((block // across) * rows, rows)
    return row_at, pl.multiple_of((block % across) * LANES, LANES)


def pack_halves(codes, block_at, kept_ref, sent_ref):
    @pl.loop(0, HALF)
    def _(slot):
        for block, out_ref in ((sent_block(codes, slot), sent_ref), (kept_block(codes, slot), kept_ref)):
            at = 0
            for piece in block_at(block):
                out_ref[slot, at : at + piece.shape[0], :] = piece
                at += piece.shape[0]


def pack_products(codes, inner_ref, outer_ref, kept_ref, sent_ref):
    depth = outer_ref.shape[0] // BLOCKS

    def block_at(block):
        row_at, column_at = inner_spot(block, depth, inner_ref.shape[1])
        outer_at = pl.multiple_of(block * depth, depth)
        return (
            inner_ref[pl.ds(row_at, depth), pl.ds(column_at, LANES)],
            outer_ref[pl.ds(outer_at, depth), :],
        )

    pack_halves(codes, block_at, kept_ref, sent_ref)


def read(ref, rows):
    return jnp.concatenate([ref[plane, rows, :] for plane in range(ref.shape[0])], axis=1)


def write(ref, rows, values):
    for plane in range(ref.shape[0]):
        ref[plane, rows, :] = values[:, plane * 128 : (plane + 1) * 128]


def rounded(values):
    return values.astype(BF).astype(F32)


def spread_rows(source_ref, target_ref):
    parts, patches, each, _ = source_ref.shape
    for part in range(parts):
        for patch in range(patches):
            base = (part * patches + patch) * each
            write(target_ref, slice(base, base + each), source_ref[part, patch].astype(F32))


def gather_rows(source_ref, target_ref):
    parts, patches, each, _ = target_ref.shape
    for part in range(parts):
        for patch in range(patches):
            base = (part * patches + patch) * each
            target_ref[part, patch] = read(source_ref, slice(base, base + each)).astype(BF)


def image_rows(image, patches, each):
    return pl.ds((image // each) * patches * each + image % each, patches, stride=each)


def row_tiles(rows):
    tile = max(t for t in range(16, 209, 16) if rows % t == 0)
    return [slice(at, at + tile) for at in range(0, rows, tile)]


def cross_setup(mask_ref, weight_ref, bias_ref, kept_ref, keep_ref, bias_columns_ref, rows_ref):
    patches, layers, _ = weight_ref.shape
    padded = kept_ref.shape[2]
    for patch in range(patches):
        base = patch * layers
        weight = weight_ref[patch].astype(F32)
        rows_ref[0, base : base + layers, :] = weight[:, 0:128]
        rows_ref[1, base : base + layers, 0 : patches - 128] = weight[:, 128:]
    keep_ref[...] = jnp.zeros_like(keep_ref)
    kept_ref[...] = jnp.zeros_like(kept_ref)
    for layer in range(layers):
        weight = read(rows_ref, pl.ds(layer, patches, stride=layers))[:, 0:patches]
        for image in range(mask_ref.shape[0]):
            keep_row = mask_ref[image, layer : layer + 1, :].astype(F32)
            keep_ref[image, layer : layer + 1, 0:patches] = keep_row
            kept_ref[layer, image, 0:patches, 0:patches] = (weight * keep_row).astype(BF)
    bias_rows = jnp.concatenate([bias_ref[...], jnp.zeros((8 - layers, patches), F32)], axis=0)
    bias_rows = jnp.concatenate([bias_rows, jnp.zeros((8, 256 - patches), F32)], axis=1)
    bias_columns_ref[...] = jnp.transpose(bias_rows)[0:padded]


def cross_forward(
    layer, source_ref, target_ref, vectors_ref, kept_ref, bias_ref,
    aff_scale_ref, aff_shift_ref, scale_ref, low_ref, patches, each,
):
    aff_scale = aff_scale_ref[layer : layer + 1, :]
    aff_shift = aff_shift_ref[layer : layer + 1, :]
    scale = scale_ref[layer : layer + 1, :]
    branch_squares = jnp.zeros((1, LANES), F32)
    normed_squares = jnp.zeros((1, LANES), F32)
    for image in range(kept_ref.shape[1]):
        rows = image_rows(image, patches, each)
        stream = read(source_ref, rows)
        normed = aff_scale * stream + aff_shift
        low_ref[image, 0:patches, :] = normed.astype(BF)
        mixing = dot(kept_ref[layer, image], low_ref[image])
        branch = scale * (mixing + bias_ref[:, layer : layer + 1])[0:patches]
        write(target_ref, rows, rounded(stream + branch))
        branch_squares += row_sum(branch * branch)
        normed_squares += row_sum(normed * normed)
    vectors_ref[layer, SQUARES : SQUARES + 1, :] = branch_squares
    vectors_ref[layer, SQUARES + 1 : SQUARES + 2, :] = normed_squares


def mixer_hidden(
    layer, stream_ref, low_ref, fired_ref, slope_ref, vectors_ref,
    aff_scale_ref, aff_shift_ref, inner_ref, inner_bias_ref,
):
    aff_scale = aff_scale_ref[layer : layer + 1, :]
    aff_shift = aff_shift_ref[layer : layer + 1, :]
    tiles = row_tiles(stream_ref.shape[1])
    squares = jnp.zeros((1, LANES), F32)
    for rows in tiles:
        normed = aff_scale * read(stream_ref, rows) + aff_shift
        low_ref[rows, :] = normed.astype(BF)
        squares += row_sum(normed * normed)
    vectors_ref[layer, SQUARES + 3 : SQUARES + 4, :] = squares
    step = inner_ref.shape[1] // 2

    @pl.loop(0, 2)
    def _(part):
        at = pl.ds(pl.multiple_of(part * step, step), step)
        for rows in tiles:
            hidden = dot(low_ref[rows, :], inner_ref[:, at]) + inner_bias_ref[layer : layer + 1, at]
            normal_cdf = 0.5 * (1.0 + lax.erf(hidden * SQRT_HALF))
            density = INV_ROOT_TAU * jnp.exp(-0.5 * hidden * hidden)
            fired_ref[rows, at] = (hidden * normal_cdf).astype(BF)
            slope_ref[rows, at] = (normal_cdf + hidden * density).astype(BF)


def mixer_backward(
    layer, upper_ref, low_ref, fired_ref, slope_ref, scaled_ref, inner_ref, outer_ref,
    inner_grad_ref, outer_grad_ref, vectors_ref, scale_ref,
):
    scale = scale_ref[layer : layer + 1, :]
    tiles = row_tiles(upper_ref.shape[1])
    bias = jnp.zeros((1, LANES), F32)
    for rows in tiles:
        result_grad = read(upper_ref, rows) * scale
        bias += row_sum(result_grad)
        scaled_ref[rows, :] = result_grad.astype(BF)
    vectors_ref[layer, MIXER_OUT_BIAS : MIXER_OUT_BIAS + 1, :] = bias
    columns = inner_ref.shape[1]
    step = 2 * LANES
    for part in range(columns // step):
        at = slice(part * step, (part + 1) * step)
        outer_grad_ref[at, :] = dot(fired_ref[:, at], scaled_ref[...], 0, 0).astype(BF)
        inner_bias = jnp.zeros((1, step), F32)
        for rows in tiles:
            hidden_grad = dot(scaled_ref[rows, :], outer_ref[at, :], 1, 1) * slope_ref[
                rows, at
            ].astype(F32)
            inner_bias += row_sum(hidden_grad)
            slope_ref[rows, at] = hidden_grad.astype(BF)
        for piece in range(step // LANES):
            row = MIXER_IN_BIAS + part * (step // LANES) + piece
            vectors_ref[layer, row : row + 1, :] = inner_bias[:, piece * LANES : (piece + 1) * LANES]
        inner_grad_ref[:, at] = dot(low_ref[...], slope_ref[:, at], 0, 0).astype(BF)


def mixer_input_grad(
    layer, upper_ref, stream_ref, hidden_grad_ref, target_ref, inner_ref, vectors_ref,
    aff_scale_ref,
):
    aff_scale = aff_scale_ref[layer : layer + 1, :]
    scale_grad = jnp.zeros((1, LANES), F32)
    shift_grad = jnp.zeros((1, LANES), F32)
    for rows in row_tiles(upper_ref.shape[1]):
        normed_grad = dot(hidden_grad_ref[rows, :], inner_ref[...], 1, 1)
        scale_grad += row_sum(normed_grad * read(stream_ref, rows))
        shift_grad += row_sum(normed_grad)
        write(target_ref, rows, rounded(read(upper_ref, rows) + normed_grad * aff_scale))
    vectors_ref[layer, MIXER_AFF_SCALE : MIXER_AFF_SCALE + 1, :] = scale_grad
    vectors_ref[layer, MIXER_AFF_SHIFT : MIXER_AFF_SHIFT + 1, :] = shift_grad


def cross_backward(
    layer, stream_ref, upper_ref, target_ref, weight_grad_ref, vectors_ref, kept_ref, keep_ref,
    bias_ref, aff_scale_ref, aff_shift_ref, scale_ref, low_ref, mixing_low_ref, patches, each,
):
    padded = kept_ref.shape[2]
    aff_scale = aff_scale_ref[layer : layer + 1, :]
    aff_shift = aff_shift_ref[layer : layer + 1, :]
    scale = scale_ref[layer : layer + 1, :]
    aff_scale_grad = jnp.zeros((1, LANES), F32)
    aff_shift_grad = jnp.zeros((1, LANES), F32)
    scale_grad = jnp.zeros((1, LANES), F32)
    bias_grad = jnp.zeros((8, padded), F32)
    weight_grad = jnp.zeros((padded, padded), F32)
    ones = jnp.ones((8, LANES), BF)
    for image in range(kept_ref.shape[1]):
        rows = image_rows(image, patches, each)
        stream = read(stream_ref, rows)
        upper = read(upper_ref, rows)
        low_ref[image, 0:patches, :] = (aff_scale * stream + aff_shift).astype(BF)
        mixing_low_ref[image, 0:patches, :] = (upper * scale).astype(BF)
        kept = kept_ref[layer, image]
        shifted = dot(kept, low_ref[image]) + bias_ref[:, layer : layer + 1]
        scale_grad += row_sum(upper * shifted[0:patches])
        mixing_low = mixing_low_ref[image]
        bias_grad += dot(ones, mixing_low, 1, 1)
        weight_grad += (
            dot(mixing_low, low_ref[image], 1, 1) * keep_ref[image, layer : layer + 1, :]
        )
        normed_grad = dot(kept, mixing_low, 0, 0)[0:patches]
        aff_scale_grad += row_sum(normed_grad * stream)
        aff_shift_grad += row_sum(normed_grad)
        write(target_ref, rows, rounded(upper + normed_grad * aff_scale))
    weight_grad_ref[...] = weight_grad
    vectors_ref[layer, CROSS_AFF_SCALE : CROSS_AFF_SCALE + 1, :] = aff_scale_grad
    vectors_ref[layer, CROSS_AFF_SHIFT : CROSS_AFF_SHIFT + 1, :] = aff_shift_grad
    vectors_ref[layer, CROSS_SCALE : CROSS_SCALE + 1, :] = scale_grad
    vectors_ref[layer, CROSS_BIAS : CROSS_BIAS + 1, 0:padded] = bias_grad[0:1]


def clear_padding(*padded_refs, patches):
    for ref in padded_refs:
        images, padded, width = ref.shape
        for image in range(images):
            ref[image, padded - 16 :, :] = jnp.zeros((16, width), BF)


def first_kernel(
    mesh_shape,
    x_hbm, mask_hbm, g_hbm, inner_hbm, outer_hbm, cross_weight_hbm, cross_bias_hbm,
    inner_bias_hbm, mixer_aff_shift_hbm, *parameters_hbm_and_rest,
):
    parameters_hbm, rest = parameters_hbm_and_rest[:6], parameters_hbm_and_rest[6:]
    parameters, rest = rest[:6], rest[6:]
    cross_aff_scale, cross_aff_shift, cross_scale, mixer_aff_scale, outer_bias, mixer_scale = parameters
    (
    kept, sent, vectors, s0, s1, s2, s3, g_rows, low0, fired0, slope0, result0, fired1, slope1,
    inner0, outer0, inner1, outer1, kept_weight, keep, bias_columns,
    x_in, mask_in, g_in, cross_weight, cross_bias, inner_bias, mixer_aff_shift, weight_rows, padded_low,
    low1, scaled, inner_grad, outer_grad, sems,
    ) = rest
    _, patches, each, _ = x_in.shape
    per = x_in.shape[0]
    own = lax.axis_index("pipe") * per
    sources = (
        (cross_weight_hbm, cross_weight),
        (cross_bias_hbm, cross_bias),
        (inner_bias_hbm, inner_bias),
        (mixer_aff_shift_hbm, mixer_aff_shift),
        *zip(parameters_hbm, parameters),
        (mask_hbm.at[pl.ds(own, per)], mask_in),
        (x_hbm.at[pl.ds(own, per)], x_in),
        (inner_hbm.at[0], inner0),
        (outer_hbm.at[0], outer0),
        (inner_hbm.at[1], inner1),
        (g_hbm.at[pl.ds(own, per)], g_in),
        (outer_hbm.at[1], outer1),
    )
    copies = [
        pltpu.make_async_copy(source, target, sems.at[number])
        for number, (source, target) in enumerate(sources)
    ]
    for copy in copies:
        copy.start()
    vectors[...] = jnp.zeros_like(vectors)
    clear_padding(padded_low, patches=patches)
    for copy in copies[:-6]:
        copy.wait()
    copies = copies[-7:]
    masks = mask_in[...].reshape((per * each,) + mask_in.shape[2:])
    cross_setup(masks, cross_weight, cross_bias, kept_weight, keep, bias_columns, weight_rows)
    copies[1].wait()
    spread_rows(x_in, s0)
    cross = (kept_weight, bias_columns, cross_aff_scale, cross_aff_shift, cross_scale, padded_low)
    cross_forward(0, s0, s1, vectors, *cross, patches, each)
    copies[2].wait()
    mixer = (mixer_aff_scale, mixer_aff_shift)
    mixer_hidden(0, s1, low0, fired0, slope0, vectors, *mixer, inner0, inner_bias)
    copies[3].wait()
    squares = jnp.zeros((1, LANES), F32)
    for rows in row_tiles(s1.shape[1]):
        result = dot(fired0[rows, :], outer0[...]) + outer_bias[0:1, :]
        result0[rows, :] = result.astype(BF)
        branch = mixer_scale[0:1, :] * result
        write(s2, rows, rounded(read(s1, rows) + branch))
        squares += row_sum(branch * branch)
    vectors[0, SQUARES + 2 : SQUARES + 3, :] = squares
    cross_forward(1, s2, s3, vectors, *cross, patches, each)
    copies[4].wait()
    mixer_hidden(1, s3, low1, fired1, slope1, vectors, *mixer, inner1, inner_bias)
    copies[5].wait()
    spread_rows(g_in, g_rows)
    copies[6].wait()
    mixer_backward(
        1, g_rows, low1, fired1, slope1, scaled, inner1, outer1, inner_grad, outer_grad,
        vectors, mixer_scale,
    )
    pack_products(own_codes(mesh_shape), inner_grad, outer_grad, kept, sent)


def second_kernel(
    s2, s3, g_rows, fired1, hidden_grad, inner1, outer1, kept_weight, keep, bias_columns,
    vectors_in, cross_aff_scale, cross_aff_shift, cross_scale, mixer_aff_scale, outer_bias,
    mixer_scale,
    output, g2, weight_grad, vectors,
    leaving, g1, padded_low, padded_mixing,
):
    _, patches, each, _ = output.shape
    vectors[...] = vectors_in[...]
    clear_padding(padded_low, padded_mixing, patches=patches)
    squares = jnp.zeros((1, LANES), F32)
    scale_grad = jnp.zeros((1, LANES), F32)
    for rows in row_tiles(s3.shape[1]):
        result = dot(fired1[rows, :], outer1[...]) + outer_bias[1:2, :]
        scale_grad += row_sum(read(g_rows, rows) * result)
        branch = mixer_scale[1:2, :] * result
        write(leaving, rows, read(s3, rows) + branch)
        squares += row_sum(branch * branch)
    vectors[1, SQUARES + 2 : SQUARES + 3, :] = squares
    vectors[1, MIXER_SCALE : MIXER_SCALE + 1, :] = scale_grad
    mixer_input_grad(1, g_rows, s3, hidden_grad, g1, inner1, vectors, mixer_aff_scale)
    gather_rows(leaving, output)
    cross_backward(
        1, s2, g1, g2, weight_grad, vectors, kept_weight, keep, bias_columns,
        cross_aff_scale, cross_aff_shift, cross_scale, padded_low, padded_mixing, patches, each,
    )


def third_kernel(
    mesh_shape,
    g2, low0, fired0, slope0, result0, inner0, outer0, vectors_in, mixer_scale,
    kept, sent, hidden_grad, vectors,
    scaled, inner_grad, outer_grad,
):
    vectors[...] = vectors_in[...]
    hidden_grad[...] = slope0[...]
    mixer_backward(
        0, g2, low0, fired0, hidden_grad, scaled, inner0, outer0, inner_grad, outer_grad,
        vectors, mixer_scale,
    )
    pack_products(own_codes(mesh_shape), inner_grad, outer_grad, kept, sent)
    scale_grad = jnp.zeros((1, LANES), F32)
    for rows in row_tiles(g2.shape[1]):
        scale_grad += row_sum(read(g2, rows) * result0[rows, :].astype(F32))
    vectors[0, MIXER_SCALE : MIXER_SCALE + 1, :] = scale_grad


def fourth_kernel(
    mesh_shape,
    s0, s1, g2, hidden_grad, inner0, kept_weight, keep, bias_columns, weight_grad1, vectors_in,
    cross_aff_scale, cross_aff_shift, cross_scale, mixer_aff_scale,
    input_grad, kept, sent,
    g1, g0, weight_grad0, vectors, small, padded_low, padded_mixing,
):
    _, patches, each, _ = input_grad.shape
    vectors[...] = vectors_in[...]
    clear_padding(padded_low, padded_mixing, patches=patches)
    mixer_input_grad(0, g2, s1, hidden_grad, g1, inner0, vectors, mixer_aff_scale)
    cross_backward(
        0, s0, g1, g0, weight_grad0, vectors, kept_weight, keep, bias_columns,
        cross_aff_scale, cross_aff_shift, cross_scale, padded_low, padded_mixing, patches, each,
    )
    layers, padded = kept_weight.shape[0], kept_weight.shape[2]
    groups = padded // VECTOR_ROWS
    small[...] = jnp.zeros_like(small)
    for layer, weight_grad in enumerate((weight_grad0, weight_grad1)):
        for group in range(groups):
            rows = slice(group * VECTOR_ROWS, (group + 1) * VECTOR_ROWS)
            small[layer * groups + group, :, 0:padded] = weight_grad[rows, :].astype(BF)
        small[layers * groups + layer] = vectors[layer].astype(BF)
    pack_halves(own_codes(mesh_shape), lambda block: (small[block],), kept, sent)
    gather_rows(g0, input_grad)


def exchange_bits(values, mesh_shape, phases):
    even, odd = phase_bits(mesh_shape)
    places = range(mesh_shape["dp"] * mesh_shape["pipe"])

    def partner(place):
        for phase in phases:
            place ^= (odd if place & 1 else even)[phase]
        return place

    return lax.ppermute(values, AXES, [(i, partner(i)) for i in places])


def across(slot):
    return [phase for phase, bit in ((SCATTERED - 2, 2), (SCATTERED - 1, 1)) if slot & bit]


def part_sum(terms, start, stop):
    return sum(t[start:stop].astype(F32) for t in terms)


def halve(terms, width, mesh_shape, phase):
    half = width // 2
    leaving = part_sum(terms, half, width).astype(BF)
    return leaving, terms + [exchange_bits(leaving, mesh_shape, [phase])]


def scatter_last(terms, mesh_shape):
    arrived = [
        exchange_bits(part_sum(terms, slot, slot + 1).astype(BF), mesh_shape, across(slot))
        for slot in (1, 3, 2)
    ]
    total = part_sum(terms, 0, 1) + sum(a.astype(F32) for a in arrived)
    for phase in range(SCATTERED, len(phase_bits(mesh_shape)[0])):
        total = total.astype(BF)
        total = total.astype(F32) + exchange_bits(total, mesh_shape, [phase]).astype(F32)
    return total.astype(BF)


def gather_last(own, mesh_shape):
    arrived = {slot: exchange_bits(own, mesh_shape, across(slot)) for slot in (1, 3, 2)}
    return jnp.concatenate([own, arrived[1], arrived[2], arrived[3]], axis=0)


def double(held, mesh_shape, phase):
    return jnp.concatenate([held, exchange_bits(held, mesh_shape, [phase])], axis=0)


def after(values, *others):
    return lax.optimization_barrier((values, *others))[0]


def unpack_block(block, values, images_all, layer, inner_rows, outer_rows, inner_out, outer_out, sems):
    depth = outer_rows.shape[0] // BLOCKS
    row_at, column_at = inner_spot(block, depth, inner_rows.shape[1])
    inner_at = (pl.ds(row_at, depth), pl.ds(column_at, LANES))
    outer_at = pl.ds(pl.multiple_of(block * depth, depth), depth)
    copies = (
        pltpu.make_async_copy(inner_rows.at[inner_at], inner_out.at[(layer,) + inner_at], sems.at[0, block]),
        pltpu.make_async_copy(outer_rows.at[outer_at], outer_out.at[layer, outer_at], sems.at[1, block]),
    )
    if values is not None:
        inner_rows[inner_at] = values[0:depth, :].astype(F32) / images_all
        outer_rows[outer_at, :] = values[depth : 2 * depth, :].astype(F32) / images_all
    return copies


def unpack_layer(mesh_shape, images_all, layer, quarters, rows, outs, sems, extra=None):
    codes = own_codes(mesh_shape)
    quarter = HALF // 2
    places = []
    for number, values in enumerate(quarters):
        block_of = kept_block if number < 2 else sent_block
        places.append((values, block_of, (number % 2) * quarter))

    @pl.loop(0, quarter)
    def _(slot):
        for values, block_of, base in places:
            block = block_of(codes, slot + base)
            for copy in unpack_block(block, values.at[slot], images_all, layer, *rows, *outs, sems):
                copy.start()
            if extra is not None:
                extra(block, values.at[slot])

    @pl.loop(0, BLOCKS)
    def _(block):
        for copy in unpack_block(block, None, images_all, layer, *rows, *outs, sems):
            copy.wait()


def unpack_last_layer(
    mesh_shape, images_all, held, late, other_held, other_late,
    inner_out, outer_out, inner_rows, outer_rows, sems,
):
    unpack_layer(
        mesh_shape, images_all, 1, (held, late, other_held, other_late),
        (inner_rows, outer_rows), (inner_out, outer_out), sems,
    )


def unpack_first_layer(
    mesh_shape, images_all, held, late, other_held, other_late, inner_in, outer_in,
    inner_out, outer_out, weight_out, aff_scale_out, aff_shift_out, cross_bias_out,
    cross_scale_out, mixer_aff_scale_out, mixer_aff_shift_out, inner_bias_out, outer_bias_out,
    mixer_scale_out, magnitudes_out,
    inner_rows, outer_rows, weight_rows, vectors, sems,
):
    patches, layers, _ = weight_out.shape
    depth = outer_rows.shape[0] // BLOCKS
    groups = weight_rows.shape[1] // VECTOR_ROWS

    def extra(block, values):
        small = values[2 * depth :, :].astype(F32) / images_all

        @pl.when(block < layers * groups)
        def _():
            at = pl.multiple_of((block % groups) * VECTOR_ROWS, VECTOR_ROWS)
            weight_rows[block // groups, pl.ds(at, VECTOR_ROWS), :] = small

        @pl.when((block >= layers * groups) & (block < layers * (groups + 1)))
        def _():
            vectors[block - layers * groups] = small

    unpack_layer(
        mesh_shape, images_all, 0, (held, late, other_held, other_late),
        (inner_rows, outer_rows), (inner_out, outer_out), sems, extra,
    )
    for layer in range(layers):
        row = slice(layer, layer + 1)
        weight_out[:, layer, :] = weight_rows[layer, 0:patches, 0:patches]
        aff_scale_out[row, :] = vectors[layer, CROSS_AFF_SCALE : CROSS_AFF_SCALE + 1, :]
        aff_shift_out[row, :] = vectors[layer, CROSS_AFF_SHIFT : CROSS_AFF_SHIFT + 1, :]
        cross_bias_out[row, :] = vectors[layer, CROSS_BIAS : CROSS_BIAS + 1, 0:patches]
        cross_scale_out[row, :] = vectors[layer, CROSS_SCALE : CROSS_SCALE + 1, :]
        mixer_aff_scale_out[row, :] = vectors[layer, MIXER_AFF_SCALE : MIXER_AFF_SCALE + 1, :]
        mixer_aff_shift_out[row, :] = vectors[layer, MIXER_AFF_SHIFT : MIXER_AFF_SHIFT + 1, :]
        outer_bias_out[row, :] = vectors[layer, MIXER_OUT_BIAS : MIXER_OUT_BIAS + 1, :]
        mixer_scale_out[row, :] = vectors[layer, MIXER_SCALE : MIXER_SCALE + 1, :]
        for piece in range(SQUARES - MIXER_IN_BIAS):
            at = slice(piece * LANES, (piece + 1) * LANES)
            inner_bias_out[row, at] = vectors[layer, MIXER_IN_BIAS + piece : MIXER_IN_BIAS + piece + 1, :]
        squares = vectors[layer, SQUARES : SQUARES + 4, :] / (patches * LANES)
        means = jnp.sqrt(jnp.sum(squares, axis=1, keepdims=True))
        for kind in range(2):
            for which in range(2):
                at = 2 * kind + which
                magnitudes_out[layer, kind : kind + 1, which : which + 1] = means[at : at + 1]


def call(kernel, name, args, outs, scratch, in_specs=None, out_specs=None, aliases=None, us=1):
    return pl.pallas_call(
        kernel,
        out_shape=outs,
        in_specs=[VMEM] * len(args) if in_specs is None else in_specs,
        out_specs=[VMEM] * len(outs) if out_specs is None else out_specs,
        scratch_shapes=scratch,
        input_output_aliases=aliases or {},
        compiler_params=pltpu.CompilerParams(vmem_limit_bytes=VMEM_LIMIT),
        cost_estimate=pl.CostEstimate(
            flops=int(us * 1e9), bytes_accessed=int(us * 3e6), transcendentals=0
        ),
        name=name,
    )(*args)


def in_vmem(arrays):
    return [pltpu.with_memory_space_constraint(a, pltpu.VMEM) for a in arrays]


def in_hbm(arrays):
    return [pltpu.with_memory_space_constraint(a, pltpu.HBM) for a in arrays]


def on_device(
    mesh_shape,
    inputs,
    patch_masks,
    out_grad,
    cross_aff_scale,
    cross_aff_shift,
    cross_weight,
    cross_bias,
    cross_scale,
    mixer_aff_scale,
    mixer_aff_shift,
    mixer_in,
    mixer_in_bias,
    mixer_out,
    mixer_out_bias,
    mixer_scale,
):
    micros, each, patches, width = inputs.shape
    layers, _, columns = mixer_in.shape
    per = micros // mesh_shape["pipe"]
    images = per * each
    padded = -(-patches // 16) * 16
    rows = images * patches
    depth = width * columns // (BLOCKS * LANES)
    images_all = micros * each * mesh_shape["dp"]
    x_rows = jnp.transpose(inputs, (0, 2, 1, 3))
    g_rows = jnp.transpose(out_grad, (0, 2, 1, 3))
    weight_rows = jnp.transpose(cross_weight, (1, 0, 2))

    def vmem(*shape, dtype=BF):
        return pltpu.VMEM(shape, dtype)

    def hbm(*shape, dtype=F32):
        return jax.ShapeDtypeStruct(shape, dtype)

    stream = vmem(width // 128, rows, 128, dtype=F32)
    hidden = vmem(rows, columns)
    inner, outer = vmem(width, columns), vmem(columns, width)
    vectors = vmem(layers, VECTOR_ROWS, LANES, dtype=F32)
    padded_images = vmem(images, padded, width)
    local = (per, patches, each, width)
    first = call(
        functools.partial(first_kernel, mesh_shape),
        "forward",
        in_hbm((
            x_rows, patch_masks, g_rows, mixer_in, mixer_out, weight_rows, cross_bias,
            mixer_in_bias, mixer_aff_shift, cross_aff_scale, cross_aff_shift, cross_scale,
            mixer_aff_scale, mixer_out_bias, mixer_scale,
        )),
        (
            *[vmem(layers, width, dtype=F32)] * 6,
            vmem(HALF, 2 * depth, LANES),
            vmem(HALF, 2 * depth, LANES),
            vectors,
            *[stream] * 5,
            vmem(rows, width),
            hidden,
            hidden,
            vmem(rows, width),
            hidden,
            hidden,
            inner,
            outer,
            inner,
            outer,
            vmem(layers, images, padded, padded),
            vmem(images, 8, padded, dtype=F32),
            vmem(padded, 8, dtype=F32),
        ),
        [
            vmem(*local),
            vmem(per, each, layers, patches, dtype=jnp.int32),
            vmem(*local),
            vmem(patches, layers, patches),
            vmem(layers, patches, dtype=F32),
            vmem(layers, columns, dtype=F32),
            vmem(layers, width, dtype=F32),
            vmem(2, layers * patches, 128, dtype=F32),
            padded_images,
            vmem(rows, width),
            vmem(rows, width),
            inner,
            outer,
            pltpu.SemaphoreType.DMA((17,)),
        ],
        in_specs=[HBM] * 15,
        us=18,
    )
    aff_scale, aff_shift, scale, mixer_aff, result_bias, result_scale = in_vmem(first[:6])
    (
        kept1, sent1, sums, s0, s1, s2, s3, upper, low0, fired0, slope0, result0, fired1,
        hidden_grad1, inner0, outer0, inner1, outer1, kept_weight, keep, bias_columns,
    ) = first[6:]
    output, g2, weight_grad1, sums = call(
        second_kernel,
        "middle",
        (
            *in_vmem((
                s2, s3, upper, fired1, hidden_grad1, inner1, outer1, kept_weight, keep,
                bias_columns, sums,
            )),
            aff_scale, aff_shift, scale, mixer_aff, result_bias, result_scale,
        ),
        (hbm(*local, dtype=BF), stream, vmem(padded, padded, dtype=F32), vectors),
        [stream, stream, padded_images, padded_images],
        us=5,
    )
    terms1 = [kept1, exchange_bits(sent1, mesh_shape, [0])]
    leaving1, terms1 = halve(terms1, HALF, mesh_shape, 1)
    g2, _ = lax.optimization_barrier((g2, leaving1))
    halves = vmem(HALF, 2 * depth, LANES)
    kept0, sent0, hidden_grad0, sums = call(
        functools.partial(third_kernel, mesh_shape),
        "first_layer_weights",
        (*in_vmem((g2, low0, fired0, slope0, result0, inner0, outer0, sums)), result_scale),
        (halves, halves, hidden, vectors),
        [vmem(rows, width), inner, outer],
        us=7,
    )
    sent0, sums, _ = lax.optimization_barrier((sent0, sums, terms1[-1]))
    arrived0 = exchange_bits(sent0, mesh_shape, [0])
    halves = vmem(HALF, VECTOR_ROWS, LANES)
    input_grad, kept_small, sent_small = call(
        functools.partial(fourth_kernel, mesh_shape),
        "first_layer_input",
        (
            *in_vmem((
                s0, s1, g2, hidden_grad0, inner0, kept_weight, keep, bias_columns, weight_grad1,
                sums,
            )),
            aff_scale, aff_shift, scale, mixer_aff,
        ),
        (hbm(*local, dtype=BF), halves, halves),
        [
            stream,
            stream,
            vmem(padded, padded, dtype=F32),
            vectors,
            vmem(BLOCKS, VECTOR_ROWS, LANES),
            padded_images,
            padded_images,
        ],
        us=5,
    )
    _, terms1 = halve(terms1, HALF // 2, mesh_shape, 2)
    sent_small = after(sent_small, terms1[-1])
    arrived_small = exchange_bits(sent_small, mesh_shape, [0])
    terms0 = [
        jnp.concatenate([kept0, kept_small], axis=1),
        jnp.concatenate([arrived0, arrived_small], axis=1),
    ]
    _, terms0 = halve(terms0, HALF, mesh_shape, 1)
    own1 = scatter_last(terms1, mesh_shape)
    terms0[-1], own1 = lax.optimization_barrier((terms0[-1], own1))
    _, terms0 = halve(terms0, HALF // 2, mesh_shape, 2)
    four1 = gather_last(own1, mesh_shape)
    terms0[-1], four1 = lax.optimization_barrier((terms0[-1], four1))
    own0 = scatter_last(terms0, mesh_shape)
    held1 = double(four1, mesh_shape, 2)
    own0, held1 = lax.optimization_barrier((own0, held1))
    four0 = gather_last(own0, mesh_shape)
    late1 = exchange_bits(held1, mesh_shape, [1])
    other_held1 = exchange_bits(held1, mesh_shape, [0])
    four0, late1 = lax.optimization_barrier((four0, late1))
    held0 = double(four0, mesh_shape, 2)
    other_late1 = exchange_bits(late1, mesh_shape, [0])
    held0, other_late1 = lax.optimization_barrier((held0, other_late1))
    late0 = exchange_bits(held0, mesh_shape, [1])
    other_held0 = exchange_bits(held0, mesh_shape, [0])
    quarters1 = (held1, late1, other_held1, other_late1)
    inner_out, outer_out = hbm(layers, width, columns), hbm(layers, columns, width)
    unpacked = [
        vmem(width, columns, dtype=F32),
        vmem(columns, width, dtype=F32),
    ]
    sems = pltpu.SemaphoreType.DMA((2, BLOCKS))
    grads = call(
        functools.partial(unpack_last_layer, mesh_shape, images_all),
        "unpack_last_layer",
        in_vmem(quarters1),
        (inner_out, outer_out),
        unpacked + [sems],
        out_specs=[HBM] * 2,
        us=3,
    )
    late0, grads = lax.optimization_barrier((late0, grads))
    quarters0 = (held0, late0, other_held0, exchange_bits(late0, mesh_shape, [0]))
    row = hbm(layers, width)
    (
        inner_grad, outer_grad, weight_grad, aff_scale_grad, aff_shift_grad, bias_grad,
        scale_grad, mixer_aff_scale_grad, mixer_aff_shift_grad, inner_bias_grad,
        outer_bias_grad, mixer_scale_grad, magnitudes,
    ) = call(
        functools.partial(unpack_first_layer, mesh_shape, images_all),
        "unpack_first_layer",
        (*in_vmem(quarters0), *grads),
        (
            inner_out, outer_out, hbm(patches, layers, patches), row, row,
            hbm(layers, patches), row, row, row, hbm(layers, columns), row, row,
            hbm(layers, 2, 2),
        ),
        unpacked + [vmem(layers, padded, LANES, dtype=F32), vectors, sems],
        in_specs=[VMEM] * 4 + [HBM] * 2,
        out_specs=[HBM] * 2 + [VMEM] * 11,
        aliases={4: 0, 5: 1},
        us=3,
    )
    return (
        jnp.transpose(output, (0, 2, 1, 3)),
        jnp.transpose(input_grad, (0, 2, 1, 3)),
        aff_scale_grad,
        aff_shift_grad,
        jnp.transpose(weight_grad, (1, 0, 2)),
        bias_grad,
        scale_grad,
        mixer_aff_scale_grad,
        mixer_aff_shift_grad,
        inner_grad,
        inner_bias_grad,
        outer_grad,
        outer_bias_grad,
        mixer_scale_grad,
        magnitudes,
    )


def solution(mesh):
    split = P(None, "dp", None, None)
    owned = P("pipe", "dp", None, None)
    return jax.shard_map(
        functools.partial(on_device, dict(mesh.shape)),
        mesh=mesh,
        in_specs=(split,) * 3 + (P(),) * 12,
        out_specs=(owned,) * 2 + (P(),) * 13,
        check_vma=False,
    )
```

```python
import functools

import jax
import jax.numpy as jnp
from jax import lax
from jax.experimental import pallas as pl
from jax.experimental.pallas import tpu as pltpu
from jax.sharding import PartitionSpec as P

SQRT_HALF = 0.7071067811865476
INV_ROOT_TAU = 0.3989422804014327
AXES = ("dp", "pipe")
BLOCKS = 32
HALF = BLOCKS // 2
SCATTERED = 5
LANES = 384
VECTOR_ROWS = 16
BF = jnp.bfloat16
F32 = jnp.float32
VMEM = pl.BlockSpec(memory_space=pltpu.VMEM)
HBM = pl.BlockSpec(memory_space=pltpu.HBM)
VMEM_LIMIT = 28 * 2**20

CROSS_AFF_SCALE, CROSS_AFF_SHIFT, CROSS_SCALE, CROSS_BIAS = 0, 1, 2, 3
MIXER_AFF_SCALE, MIXER_AFF_SHIFT, MIXER_OUT_BIAS, MIXER_SCALE = 4, 5, 6, 7
MIXER_IN_BIAS = 8
SQUARES = 12


def dot(a, b, a_dim=1, b_dim=0):
    return lax.dot_general(
        a, b, (((a_dim,), (b_dim,)), ((), ())), preferred_element_type=F32
    )


def row_sum(values):
    return jnp.sum(values, axis=0, keepdims=True)


def phase_bits(mesh_shape):
    pipe_bits = [1 << b for b in range(mesh_shape["pipe"].bit_length() - 1)]
    dp_bits = [mesh_shape["pipe"] << b for b in range(mesh_shape["dp"].bit_length() - 1)]
    even = [pipe_bits[0], *pipe_bits[1:], *dp_bits]
    odd = list(even)
    odd[1], odd[2] = even[2], even[1]
    return even, odd


def block_code(mesh_shape, place):
    even, odd = phase_bits(mesh_shape)
    odd_place = place & 1
    code = jnp.int32(0)
    for even_bit, odd_bit in zip(even[:SCATTERED], odd[:SCATTERED]):
        bit = jnp.where(odd_place == 1, (place & odd_bit) != 0, (place & even_bit) != 0)
        code = 2 * code + bit.astype(jnp.int32)
    return code


def own_codes(mesh_shape):
    place = lax.axis_index("dp") * mesh_shape["pipe"] + lax.axis_index("pipe")
    return block_code(mesh_shape, place), block_code(mesh_shape, place ^ 1)


def kept_block(codes, slot):
    return codes[0] ^ slot


def sent_block(codes, slot):
    return codes[1] ^ slot


def inner_spot(block, rows, columns):
    across = columns // LANES
    row_at = pl.multiple_of((block // across) * rows, rows)
    return row_at, pl.multiple_of((block % across) * LANES, LANES)


def pack_halves(codes, block_at, kept_ref, sent_ref):
    @pl.loop(0, HALF)
    def _(slot):
        for block, out_ref in ((sent_block(codes, slot), sent_ref), (kept_block(codes, slot), kept_ref)):
            at = 0
            for piece in block_at(block):
                out_ref[slot, at : at + piece.shape[0], :] = piece
                at += piece.shape[0]


def pack_products(codes, inner_ref, outer_ref, kept_ref, sent_ref):
    depth = outer_ref.shape[0] // BLOCKS

    def block_at(block):
        row_at, column_at = inner_spot(block, depth, inner_ref.shape[1])
        outer_at = pl.multiple_of(block * depth, depth)
        return (
            inner_ref[pl.ds(row_at, depth), pl.ds(column_at, LANES)],
            outer_ref[pl.ds(outer_at, depth), :],
        )

    pack_halves(codes, block_at, kept_ref, sent_ref)


def read(ref, rows):
    return jnp.concatenate([ref[plane, rows, :] for plane in range(ref.shape[0])], axis=1)


def write(ref, rows, values):
    for plane in range(ref.shape[0]):
        ref[plane, rows, :] = values[:, plane * 128 : (plane + 1) * 128]


def rounded(values):
    return values.astype(BF).astype(F32)


def spread_rows(source_ref, target_ref):
    parts, patches, each, _ = source_ref.shape
    for part in range(parts):
        for patch in range(patches):
            base = (part * patches + patch) * each
            write(target_ref, slice(base, base + each), source_ref[part, patch].astype(F32))


def gather_rows(source_ref, target_ref):
    parts, patches, each, _ = target_ref.shape
    for part in range(parts):
        for patch in range(patches):
            base = (part * patches + patch) * each
            target_ref[part, patch] = read(source_ref, slice(base, base + each)).astype(BF)


def image_rows(image, patches, each):
    return pl.ds((image // each) * patches * each + image % each, patches, stride=each)


def row_tiles(rows):
    tile = max(t for t in range(16, 209, 16) if rows % t == 0)
    return [slice(at, at + tile) for at in range(0, rows, tile)]


def row_halves(rows):
    middle = -(-rows // 32) * 16
    return [slice(0, middle), slice(middle, rows)]


def cross_setup(mask_ref, weight_ref, bias_ref, kept_ref, keep_ref, bias_columns_ref, rows_ref):
    patches, layers, _ = weight_ref.shape
    padded = kept_ref.shape[2]
    for patch in range(patches):
        base = patch * layers
        weight = weight_ref[patch].astype(F32)
        rows_ref[0, base : base + layers, :] = weight[:, 0:128]
        rows_ref[1, base : base + layers, 0 : patches - 128] = weight[:, 128:]
    keep_ref[...] = jnp.zeros_like(keep_ref)
    kept_ref[...] = jnp.zeros_like(kept_ref)
    for layer in range(layers):
        weight = read(rows_ref, pl.ds(layer, patches, stride=layers))[:, 0:patches]
        for image in range(mask_ref.shape[0]):
            keep_row = mask_ref[image, layer : layer + 1, :].astype(F32)
            keep_ref[image, layer : layer + 1, 0:patches] = keep_row
            kept_ref[layer, image, 0:patches, 0:patches] = (weight * keep_row).astype(BF)
    bias_rows = jnp.concatenate([bias_ref[...], jnp.zeros((8 - layers, patches), F32)], axis=0)
    bias_rows = jnp.concatenate([bias_rows, jnp.zeros((8, 256 - patches), F32)], axis=1)
    bias_columns_ref[...] = jnp.transpose(bias_rows)[0:padded]


def cross_forward(
    layer, source_ref, target_ref, vectors_ref, kept_ref, bias_ref,
    aff_scale_ref, aff_shift_ref, scale_ref, low_ref, patches, each,
):
    aff_scale = aff_scale_ref[layer : layer + 1, :]
    aff_shift = aff_shift_ref[layer : layer + 1, :]
    scale = scale_ref[layer : layer + 1, :]
    branch_squares = jnp.zeros((1, LANES), F32)
    normed_squares = jnp.zeros((1, LANES), F32)
    for image in range(kept_ref.shape[1]):
        rows = image_rows(image, patches, each)
        stream = read(source_ref, rows)
        normed = aff_scale * stream + aff_shift
        low_ref[image, 0:patches, :] = normed.astype(BF)
        mixing = dot(kept_ref[layer, image], low_ref[image])
        branch = scale * (mixing + bias_ref[:, layer : layer + 1])[0:patches]
        write(target_ref, rows, rounded(stream + branch))
        branch_squares += row_sum(branch * branch)
        normed_squares += row_sum(normed * normed)
    vectors_ref[layer, SQUARES : SQUARES + 1, :] = branch_squares
    vectors_ref[layer, SQUARES + 1 : SQUARES + 2, :] = normed_squares


def mixer_hidden(
    layer, stream_ref, low_ref, fired_ref, slope_ref, vectors_ref,
    aff_scale_ref, aff_shift_ref, inner_ref, inner_bias_ref,
):
    aff_scale = aff_scale_ref[layer : layer + 1, :]
    aff_shift = aff_shift_ref[layer : layer + 1, :]
    tiles = row_tiles(stream_ref.shape[1])
    squares = jnp.zeros((1, LANES), F32)
    for rows in tiles:
        normed = aff_scale * read(stream_ref, rows) + aff_shift
        low_ref[rows, :] = normed.astype(BF)
        squares += row_sum(normed * normed)
    vectors_ref[layer, SQUARES + 3 : SQUARES + 4, :] = squares
    step = inner_ref.shape[1] // 3
    for part in range(3):
        at = slice(part * step, (part + 1) * step)
        for rows in tiles:
            hidden = dot(low_ref[rows, :], inner_ref[:, at]) + inner_bias_ref[layer : layer + 1, at]
            normal_cdf = 0.5 * (1.0 + lax.erf(hidden * SQRT_HALF))
            density = INV_ROOT_TAU * jnp.exp(-0.5 * hidden * hidden)
            fired_ref[rows, at] = (hidden * normal_cdf).astype(BF)
            slope_ref[rows, at] = (normal_cdf + hidden * density).astype(BF)


def mixer_backward(
    layer, upper_ref, low_ref, fired_ref, slope_ref, scaled_ref, inner_ref, outer_ref,
    inner_grad_ref, outer_grad_ref, vectors_ref, scale_ref,
):
    scale = scale_ref[layer : layer + 1, :]
    tiles = row_tiles(upper_ref.shape[1])
    bias = jnp.zeros((1, LANES), F32)
    for rows in tiles:
        result_grad = read(upper_ref, rows) * scale
        bias += row_sum(result_grad)
        scaled_ref[rows, :] = result_grad.astype(BF)
    vectors_ref[layer, MIXER_OUT_BIAS : MIXER_OUT_BIAS + 1, :] = bias
    columns = inner_ref.shape[1]
    step = 2 * LANES
    tiles = row_halves(upper_ref.shape[1])
    for part in range(columns // step):
        at = slice(part * step, (part + 1) * step)
        outer_grad_ref[at, :] = dot(fired_ref[:, at], scaled_ref[...], 0, 0).astype(BF)
        inner_bias = jnp.zeros((1, step), F32)
        for rows in tiles:
            hidden_grad = dot(scaled_ref[rows, :], outer_ref[at, :], 1, 1) * slope_ref[
                rows, at
            ].astype(F32)
            inner_bias += row_sum(hidden_grad)
            slope_ref[rows, at] = hidden_grad.astype(BF)
        for piece in range(step // LANES):
            row = MIXER_IN_BIAS + part * (step // LANES) + piece
            vectors_ref[layer, row : row + 1, :] = inner_bias[:, piece * LANES : (piece + 1) * LANES]
        inner_grad_ref[:, at] = dot(low_ref[...], slope_ref[:, at], 0, 0).astype(BF)


def mixer_input_grad(
    layer, upper_ref, stream_ref, hidden_grad_ref, target_ref, inner_ref, vectors_ref,
    aff_scale_ref,
):
    aff_scale = aff_scale_ref[layer : layer + 1, :]
    scale_grad = jnp.zeros((1, LANES), F32)
    shift_grad = jnp.zeros((1, LANES), F32)
    for rows in row_halves(upper_ref.shape[1]):
        normed_grad = dot(hidden_grad_ref[rows, :], inner_ref[...], 1, 1)
        scale_grad += row_sum(normed_grad * read(stream_ref, rows))
        shift_grad += row_sum(normed_grad)
        write(target_ref, rows, rounded(read(upper_ref, rows) + normed_grad * aff_scale))
    vectors_ref[layer, MIXER_AFF_SCALE : MIXER_AFF_SCALE + 1, :] = scale_grad
    vectors_ref[layer, MIXER_AFF_SHIFT : MIXER_AFF_SHIFT + 1, :] = shift_grad


def cross_backward(
    layer, stream_ref, upper_ref, target_ref, weight_grad_ref, vectors_ref, kept_ref, keep_ref,
    bias_ref, aff_scale_ref, aff_shift_ref, scale_ref, low_ref, mixing_low_ref, patches, each,
):
    padded = kept_ref.shape[2]
    aff_scale = aff_scale_ref[layer : layer + 1, :]
    aff_shift = aff_shift_ref[layer : layer + 1, :]
    scale = scale_ref[layer : layer + 1, :]
    aff_scale_grad = jnp.zeros((1, LANES), F32)
    aff_shift_grad = jnp.zeros((1, LANES), F32)
    scale_grad = jnp.zeros((1, LANES), F32)
    bias_grad = jnp.zeros((8, padded), F32)
    weight_grad = jnp.zeros((padded, padded), F32)
    ones = jnp.ones((8, LANES), BF)
    for image in range(kept_ref.shape[1]):
        rows = image_rows(image, patches, each)
        stream = read(stream_ref, rows)
        upper = read(upper_ref, rows)
        low_ref[image, 0:patches, :] = (aff_scale * stream + aff_shift).astype(BF)
        mixing_low_ref[image, 0:patches, :] = (upper * scale).astype(BF)
        kept = kept_ref[layer, image]
        shifted = dot(kept, low_ref[image]) + bias_ref[:, layer : layer + 1]
        scale_grad += row_sum(upper * shifted[0:patches])
        mixing_low = mixing_low_ref[image]
        bias_grad += dot(ones, mixing_low, 1, 1)
        weight_grad += (
            dot(mixing_low, low_ref[image], 1, 1) * keep_ref[image, layer : layer + 1, :]
        )
        normed_grad = dot(kept, mixing_low, 0, 0)[0:patches]
        aff_scale_grad += row_sum(normed_grad * stream)
        aff_shift_grad += row_sum(normed_grad)
        write(target_ref, rows, rounded(upper + normed_grad * aff_scale))
    weight_grad_ref[...] = weight_grad
    vectors_ref[layer, CROSS_AFF_SCALE : CROSS_AFF_SCALE + 1, :] = aff_scale_grad
    vectors_ref[layer, CROSS_AFF_SHIFT : CROSS_AFF_SHIFT + 1, :] = aff_shift_grad
    vectors_ref[layer, CROSS_SCALE : CROSS_SCALE + 1, :] = scale_grad
    vectors_ref[layer, CROSS_BIAS : CROSS_BIAS + 1, 0:padded] = bias_grad[0:1]


def clear_padding(*padded_refs, patches):
    for ref in padded_refs:
        images, padded, width = ref.shape
        for image in range(images):
            ref[image, padded - 16 :, :] = jnp.zeros((16, width), BF)


def first_kernel(
    mesh_shape,
    x_hbm, mask_hbm, g_hbm, inner_hbm, outer_hbm, cross_weight_hbm, cross_bias_hbm,
    inner_bias_hbm, mixer_aff_shift_hbm, *parameters_hbm_and_rest,
):
    parameters_hbm, rest = parameters_hbm_and_rest[:6], parameters_hbm_and_rest[6:]
    parameters, rest = rest[:6], rest[6:]
    cross_aff_scale, cross_aff_shift, cross_scale, mixer_aff_scale, outer_bias, mixer_scale = parameters
    (
    kept, sent, vectors, s0, s1, s2, s3, g_rows, low0, fired0, slope0, result0, fired1, slope1,
    inner0, outer0, inner1, outer1, kept_weight, keep, bias_columns,
    x_in, mask_in, g_in, cross_weight, cross_bias, inner_bias, mixer_aff_shift, weight_rows, padded_low,
    low1, scaled, inner_grad, outer_grad, sems,
    ) = rest
    _, patches, each, _ = x_in.shape
    per = x_in.shape[0]
    own = lax.axis_index("pipe") * per
    sources = (
        (cross_weight_hbm, cross_weight),
        (cross_bias_hbm, cross_bias),
        (inner_bias_hbm, inner_bias),
        (mixer_aff_shift_hbm, mixer_aff_shift),
        *zip(parameters_hbm, parameters),
        (mask_hbm.at[pl.ds(own, per)], mask_in),
        (x_hbm.at[pl.ds(own, per)], x_in),
        (inner_hbm.at[0], inner0),
        (outer_hbm.at[0], outer0),
        (inner_hbm.at[1], inner1),
        (g_hbm.at[pl.ds(own, per)], g_in),
        (outer_hbm.at[1], outer1),
    )
    copies = [
        pltpu.make_async_copy(source, target, sems.at[number])
        for number, (source, target) in enumerate(sources)
    ]
    for copy in copies:
        copy.start()
    vectors[...] = jnp.zeros_like(vectors)
    clear_padding(padded_low, patches=patches)
    for copy in copies[:-6]:
        copy.wait()
    copies = copies[-7:]
    masks = mask_in[...].reshape((per * each,) + mask_in.shape[2:])
    cross_setup(masks, cross_weight, cross_bias, kept_weight, keep, bias_columns, weight_rows)
    copies[1].wait()
    spread_rows(x_in, s0)
    cross = (kept_weight, bias_columns, cross_aff_scale, cross_aff_shift, cross_scale, padded_low)
    cross_forward(0, s0, s1, vectors, *cross, patches, each)
    copies[2].wait()
    mixer = (mixer_aff_scale, mixer_aff_shift)
    mixer_hidden(0, s1, low0, fired0, slope0, vectors, *mixer, inner0, inner_bias)
    copies[3].wait()
    squares = jnp.zeros((1, LANES), F32)
    for rows in row_halves(s1.shape[1]):
        result = dot(fired0[rows, :], outer0[...]) + outer_bias[0:1, :]
        result0[rows, :] = result.astype(BF)
        branch = mixer_scale[0:1, :] * result
        write(s2, rows, rounded(read(s1, rows) + branch))
        squares += row_sum(branch * branch)
    vectors[0, SQUARES + 2 : SQUARES + 3, :] = squares
    cross_forward(1, s2, s3, vectors, *cross, patches, each)
    copies[4].wait()
    mixer_hidden(1, s3, low1, fired1, slope1, vectors, *mixer, inner1, inner_bias)
    copies[5].wait()
    spread_rows(g_in, g_rows)
    copies[6].wait()
    mixer_backward(
        1, g_rows, low1, fired1, slope1, scaled, inner1, outer1, inner_grad, outer_grad,
        vectors, mixer_scale,
    )
    pack_products(own_codes(mesh_shape), inner_grad, outer_grad, kept, sent)


def second_kernel(
    s2, s3, g_rows, hidden_grad, inner1, kept_weight, keep, bias_columns, vectors_in,
    cross_aff_scale, cross_aff_shift, cross_scale, mixer_aff_scale,
    g2, weight_grad, vectors,
    g1, padded_low, padded_mixing, *, each,
):
    patches = s2.shape[1] // padded_low.shape[0]
    vectors[...] = vectors_in[...]
    clear_padding(padded_low, padded_mixing, patches=patches)
    mixer_input_grad(1, g_rows, s3, hidden_grad, g1, inner1, vectors, mixer_aff_scale)
    cross_backward(
        1, s2, g1, g2, weight_grad, vectors, kept_weight, keep, bias_columns,
        cross_aff_scale, cross_aff_shift, cross_scale, padded_low, padded_mixing, patches, each,
    )


def third_kernel(
    mesh_shape,
    s1, g2, low0, fired0, slope0, result0, inner0, outer0, vectors_in, mixer_aff_scale, mixer_scale,
    kept, sent, g1, vectors,
    hidden_grad, scaled, inner_grad, outer_grad,
):
    vectors[...] = vectors_in[...]
    hidden_grad[...] = slope0[...]
    mixer_backward(
        0, g2, low0, fired0, hidden_grad, scaled, inner0, outer0, inner_grad, outer_grad,
        vectors, mixer_scale,
    )
    pack_products(own_codes(mesh_shape), inner_grad, outer_grad, kept, sent)
    scale_grad = jnp.zeros((1, LANES), F32)
    for rows in row_tiles(g2.shape[1]):
        scale_grad += row_sum(read(g2, rows) * result0[rows, :].astype(F32))
    vectors[0, MIXER_SCALE : MIXER_SCALE + 1, :] = scale_grad
    mixer_input_grad(0, g2, s1, hidden_grad, g1, inner0, vectors, mixer_aff_scale)


def fourth_kernel(
    mesh_shape,
    s0, g1, kept_weight, keep, bias_columns, weight_grad1, vectors_in,
    s3, g_rows, fired1, outer1,
    cross_aff_scale, cross_aff_shift, cross_scale, outer_bias, mixer_scale,
    input_grad, output, kept, sent,
    g0, leaving, weight_grad0, vectors, small, padded_low, padded_mixing,
):
    _, patches, each, _ = input_grad.shape
    vectors[...] = vectors_in[...]
    clear_padding(padded_low, padded_mixing, patches=patches)
    cross_backward(
        0, s0, g1, g0, weight_grad0, vectors, kept_weight, keep, bias_columns,
        cross_aff_scale, cross_aff_shift, cross_scale, padded_low, padded_mixing, patches, each,
    )
    squares = jnp.zeros((1, LANES), F32)
    scale_grad = jnp.zeros((1, LANES), F32)
    for rows in row_halves(s3.shape[1]):
        result = dot(fired1[rows, :], outer1[...]) + outer_bias[1:2, :]
        scale_grad += row_sum(read(g_rows, rows) * result)
        branch = mixer_scale[1:2, :] * result
        write(leaving, rows, read(s3, rows) + branch)
        squares += row_sum(branch * branch)
    vectors[1, SQUARES + 2 : SQUARES + 3, :] = squares
    vectors[1, MIXER_SCALE : MIXER_SCALE + 1, :] = scale_grad
    layers, padded = kept_weight.shape[0], kept_weight.shape[2]
    groups = padded // VECTOR_ROWS
    small[...] = jnp.zeros_like(small)
    for layer, weight_grad in enumerate((weight_grad0, weight_grad1)):
        for group in range(groups):
            rows = slice(group * VECTOR_ROWS, (group + 1) * VECTOR_ROWS)
            small[layer * groups + group, :, 0:padded] = weight_grad[rows, :].astype(BF)
        small[layers * groups + layer] = vectors[layer].astype(BF)
    pack_halves(own_codes(mesh_shape), lambda block: (small[block],), kept, sent)
    gather_rows(g0, input_grad)
    gather_rows(leaving, output)


def exchange_bits(values, mesh_shape, phases):
    even, odd = phase_bits(mesh_shape)
    places = range(mesh_shape["dp"] * mesh_shape["pipe"])

    def partner(place):
        for phase in phases:
            place ^= (odd if place & 1 else even)[phase]
        return place

    return lax.ppermute(values, AXES, [(i, partner(i)) for i in places])


def across(slot):
    return [phase for phase, bit in ((SCATTERED - 2, 2), (SCATTERED - 1, 1)) if slot & bit]


def part_sum(terms, start, stop):
    return sum(t[start:stop].astype(F32) for t in terms)


def joint_sum(families, start, stop):
    sums = [part_sum(terms, start, stop).astype(BF) for terms in families]
    return sums[0] if len(sums) == 1 else jnp.concatenate(sums, axis=1)


def halve(terms, width, mesh_shape, phase):
    half = width // 2
    leaving = part_sum(terms, half, width).astype(BF)
    return leaving, terms + [exchange_bits(leaving, mesh_shape, [phase])]


def halve_all(families, width, mesh_shape, phase):
    half = width // 2
    arrived = exchange_bits(joint_sum(families, half, width), mesh_shape, [phase])
    grown, at = [], 0
    for terms in families:
        rows = terms[0].shape[1]
        grown.append(terms + [arrived[:, at : at + rows]])
        at += rows
    return arrived, grown


def scatter_last(families, mesh_shape):
    arrived = [
        exchange_bits(joint_sum(families, slot, slot + 1), mesh_shape, across(slot))
        for slot in (2, 3, 1)
    ]
    sums = [part_sum(terms, 0, 1) for terms in families]
    total = sums[0] if len(sums) == 1 else jnp.concatenate(sums, axis=1)
    total = total + sum(a.astype(F32) for a in arrived)
    for phase in range(SCATTERED, len(phase_bits(mesh_shape)[0])):
        total = total.astype(BF)
        total = total.astype(F32) + exchange_bits(total, mesh_shape, [phase]).astype(F32)
    return total.astype(BF)


def gather_last(own, mesh_shape):
    arrived = {slot: exchange_bits(own, mesh_shape, across(slot)) for slot in (2, 3, 1)}
    return jnp.concatenate([own, arrived[1], arrived[2], arrived[3]], axis=0)


def double(held, mesh_shape, phase):
    return jnp.concatenate([held, exchange_bits(held, mesh_shape, [phase])], axis=0)


def after(values, *others):
    return lax.optimization_barrier((values, *others))[0]


def unpack_quarters(mesh_shape, images_all, layer, plan, quarters, inner_out, outer_out, stage, sems):
    codes = own_codes(mesh_shape)
    quarter, depth = HALF // 2, stage.shape[2]
    columns = inner_out.shape[2]

    def copies(number, slot):
        block_of, base = plan[number]
        block = block_of(codes, slot + base)
        row_at, column_at = inner_spot(block, depth, columns)
        outer_at = pl.multiple_of(block * depth, depth)
        index = number * quarter + slot
        return (
            pltpu.make_async_copy(
                stage.at[0, index],
                inner_out.at[layer, pl.ds(row_at, depth), pl.ds(column_at, LANES)],
                sems.at[0, index],
            ),
            pltpu.make_async_copy(
                stage.at[1, index], outer_out.at[layer, pl.ds(outer_at, depth), :], sems.at[1, index]
            ),
        )

    for number, values in enumerate(quarters):

        @pl.loop(0, quarter)
        def _(slot):
            for kind, copy in enumerate(copies(number, slot)):
                block = values[slot, kind * depth : (kind + 1) * depth, :]
                stage[kind, number * quarter + slot] = block.astype(F32) / images_all
                copy.start()

    for number in range(len(quarters)):

        @pl.loop(0, quarter)
        def _(slot):
            for copy in copies(number, slot):
                copy.wait()


QUARTERS = ((kept_block, 0), (kept_block, HALF // 2), (sent_block, 0), (sent_block, HALF // 2))


def unpack_first(mesh_shape, images_all, layer, numbers, *refs):
    quarters, outs = refs[: len(numbers)], refs[len(numbers) :]
    unpack_quarters(mesh_shape, images_all, layer, [QUARTERS[n] for n in numbers], quarters, *outs)


def unpack_more(mesh_shape, images_all, layer, numbers, *refs):
    quarters, outs = refs[: len(numbers)], refs[len(numbers) + 2 :]
    unpack_quarters(mesh_shape, images_all, layer, [QUARTERS[n] for n in numbers], quarters, *outs)


def unpack_rest(
    mesh_shape, images_all, held, late, other_held, other_late, inner_in, outer_in,
    inner_out, outer_out, weight_out, aff_scale_out, aff_shift_out, cross_bias_out,
    cross_scale_out, mixer_aff_scale_out, mixer_aff_shift_out, inner_bias_out, outer_bias_out,
    mixer_scale_out, magnitudes_out,
    stage, weight_rows, vectors, sems,
):
    patches, layers, _ = weight_out.shape
    groups = weight_rows.shape[1] // VECTOR_ROWS
    codes = own_codes(mesh_shape)
    for values, (block_of, base) in zip((held, late, other_held, other_late), QUARTERS):

        @pl.loop(0, HALF // 2)
        def _(slot):
            block = block_of(codes, slot + base)
            small = values[slot, 2 * stage.shape[2] :, :].astype(F32) / images_all

            @pl.when(block < layers * groups)
            def _():
                at = pl.multiple_of((block % groups) * VECTOR_ROWS, VECTOR_ROWS)
                weight_rows[block // groups, pl.ds(at, VECTOR_ROWS), :] = small

            @pl.when((block >= layers * groups) & (block < layers * (groups + 1)))
            def _():
                vectors[block - layers * groups] = small

    for layer in range(layers):
        row = slice(layer, layer + 1)
        weight_out[:, layer, :] = weight_rows[layer, 0:patches, 0:patches]
        aff_scale_out[row, :] = vectors[layer, CROSS_AFF_SCALE : CROSS_AFF_SCALE + 1, :]
        aff_shift_out[row, :] = vectors[layer, CROSS_AFF_SHIFT : CROSS_AFF_SHIFT + 1, :]
        cross_bias_out[row, :] = vectors[layer, CROSS_BIAS : CROSS_BIAS + 1, 0:patches]
        cross_scale_out[row, :] = vectors[layer, CROSS_SCALE : CROSS_SCALE + 1, :]
        mixer_aff_scale_out[row, :] = vectors[layer, MIXER_AFF_SCALE : MIXER_AFF_SCALE + 1, :]
        mixer_aff_shift_out[row, :] = vectors[layer, MIXER_AFF_SHIFT : MIXER_AFF_SHIFT + 1, :]
        outer_bias_out[row, :] = vectors[layer, MIXER_OUT_BIAS : MIXER_OUT_BIAS + 1, :]
        mixer_scale_out[row, :] = vectors[layer, MIXER_SCALE : MIXER_SCALE + 1, :]
        for piece in range(SQUARES - MIXER_IN_BIAS):
            at = slice(piece * LANES, (piece + 1) * LANES)
            inner_bias_out[row, at] = vectors[layer, MIXER_IN_BIAS + piece : MIXER_IN_BIAS + piece + 1, :]
        squares = vectors[layer, SQUARES : SQUARES + 4, :] / (patches * LANES)
        means = jnp.sqrt(jnp.sum(squares, axis=1, keepdims=True))
        for kind in range(2):
            for which in range(2):
                at = 2 * kind + which
                magnitudes_out[layer, kind : kind + 1, which : which + 1] = means[at : at + 1]
    unpack_quarters(
        mesh_shape, images_all, 0, [QUARTERS[3]], (other_late,), inner_out, outer_out, stage, sems
    )


def call(kernel, name, args, outs, scratch, in_specs=None, out_specs=None, aliases=None, us=1):
    return pl.pallas_call(
        kernel,
        out_shape=outs,
        in_specs=[VMEM] * len(args) if in_specs is None else in_specs,
        out_specs=[VMEM] * len(outs) if out_specs is None else out_specs,
        scratch_shapes=scratch,
        input_output_aliases=aliases or {},
        compiler_params=pltpu.CompilerParams(vmem_limit_bytes=VMEM_LIMIT),
        cost_estimate=pl.CostEstimate(
            flops=int(us * 1e9), bytes_accessed=int(us * 3e6), transcendentals=0
        ),
        name=name,
    )(*args)


def in_vmem(arrays):
    return [pltpu.with_memory_space_constraint(a, pltpu.VMEM) for a in arrays]


def in_hbm(arrays):
    return [pltpu.with_memory_space_constraint(a, pltpu.HBM) for a in arrays]


def on_device(
    mesh_shape,
    inputs,
    patch_masks,
    out_grad,
    cross_aff_scale,
    cross_aff_shift,
    cross_weight,
    cross_bias,
    cross_scale,
    mixer_aff_scale,
    mixer_aff_shift,
    mixer_in,
    mixer_in_bias,
    mixer_out,
    mixer_out_bias,
    mixer_scale,
):
    micros, each, patches, width = inputs.shape
    layers, _, columns = mixer_in.shape
    per = micros // mesh_shape["pipe"]
    images = per * each
    padded = -(-patches // 16) * 16
    rows = images * patches
    depth = width * columns // (BLOCKS * LANES)
    images_all = micros * each * mesh_shape["dp"]
    x_rows = jnp.transpose(inputs, (0, 2, 1, 3))
    g_rows = jnp.transpose(out_grad, (0, 2, 1, 3))
    weight_rows = jnp.transpose(cross_weight, (1, 0, 2))

    def vmem(*shape, dtype=BF):
        return pltpu.VMEM(shape, dtype)

    def hbm(*shape, dtype=F32):
        return jax.ShapeDtypeStruct(shape, dtype)

    stream = vmem(width // 128, rows, 128, dtype=F32)
    hidden = vmem(rows, columns)
    inner, outer = vmem(width, columns), vmem(columns, width)
    vectors = vmem(layers, VECTOR_ROWS, LANES, dtype=F32)
    padded_images = vmem(images, padded, width)
    local = (per, patches, each, width)
    first = call(
        functools.partial(first_kernel, mesh_shape),
        "forward",
        in_hbm((
            x_rows, patch_masks, g_rows, mixer_in, mixer_out, weight_rows, cross_bias,
            mixer_in_bias, mixer_aff_shift, cross_aff_scale, cross_aff_shift, cross_scale,
            mixer_aff_scale, mixer_out_bias, mixer_scale,
        )),
        (
            *[vmem(layers, width, dtype=F32)] * 6,
            vmem(HALF, 2 * depth, LANES),
            vmem(HALF, 2 * depth, LANES),
            vectors,
            *[stream] * 5,
            vmem(rows, width),
            hidden,
            hidden,
            vmem(rows, width),
            hidden,
            hidden,
            inner,
            outer,
            inner,
            outer,
            vmem(layers, images, padded, padded),
            vmem(images, 8, padded, dtype=F32),
            vmem(padded, 8, dtype=F32),
        ),
        [
            vmem(*local),
            vmem(per, each, layers, patches, dtype=jnp.int32),
            vmem(*local),
            vmem(patches, layers, patches),
            vmem(layers, patches, dtype=F32),
            vmem(layers, columns, dtype=F32),
            vmem(layers, width, dtype=F32),
            vmem(2, layers * patches, 128, dtype=F32),
            padded_images,
            vmem(rows, width),
            vmem(rows, width),
            inner,
            outer,
            pltpu.SemaphoreType.DMA((17,)),
        ],
        in_specs=[HBM] * 15,
        us=18,
    )
    aff_scale, aff_shift, scale, mixer_aff, result_bias, result_scale = in_vmem(first[:6])
    (
        kept1, sent1, sums, s0, s1, s2, s3, upper, low0, fired0, slope0, result0, fired1,
        hidden_grad1, inner0, outer0, inner1, outer1, kept_weight, keep, bias_columns,
    ) = first[6:]
    g2, weight_grad1, sums = call(
        functools.partial(second_kernel, each=each),
        "last_layer",
        (
            *in_vmem((
                s2, s3, upper, hidden_grad1, inner1, kept_weight, keep, bias_columns, sums,
            )),
            aff_scale, aff_shift, scale, mixer_aff,
        ),
        (stream, vmem(padded, padded, dtype=F32), vectors),
        [stream, padded_images, padded_images],
        us=4,
    )
    main1 = [kept1, exchange_bits(sent1, mesh_shape, [0])]
    leaving1, main1 = halve(main1, HALF, mesh_shape, 1)
    g2 = after(g2, leaving1)
    halves = vmem(HALF, 2 * depth, LANES)
    kept0, sent0, g1, sums = call(
        functools.partial(third_kernel, mesh_shape),
        "first_feed_forward",
        (
            *in_vmem((s1, g2, low0, fired0, slope0, result0, inner0, outer0, sums)),
            mixer_aff, result_scale,
        ),
        (halves, halves, stream, vectors),
        [hidden, vmem(rows, width), inner, outer],
        us=9,
    )
    sent0, sums = lax.optimization_barrier((sent0, sums, main1[-1]))[:2]
    main0 = [kept0, exchange_bits(sent0, mesh_shape, [0])]
    leaving1, main1 = halve(main1, HALF // 2, mesh_shape, 2)
    sums = after(sums, leaving1)
    halves = vmem(HALF, VECTOR_ROWS, LANES)
    input_grad, output, kept_small, sent_small = call(
        functools.partial(fourth_kernel, mesh_shape),
        "first_cross",
        (
            *in_vmem((
                s0, g1, kept_weight, keep, bias_columns, weight_grad1, sums, s3, upper, fired1,
                outer1,
            )),
            aff_scale, aff_shift, scale, result_bias, result_scale,
        ),
        (hbm(*local, dtype=BF), hbm(*local, dtype=BF), halves, halves),
        [
            stream,
            stream,
            vmem(padded, padded, dtype=F32),
            vectors,
            vmem(BLOCKS, VECTOR_ROWS, LANES),
            padded_images,
            padded_images,
        ],
        us=5,
    )
    sent_small = after(sent_small, main1[-1])
    small = [kept_small, exchange_bits(sent_small, mesh_shape, [0])]
    _, main0 = halve(main0, HALF, mesh_shape, 1)
    _, small = halve(small, HALF, mesh_shape, 1)
    own1 = scatter_last([main1], mesh_shape)
    main0[-1], small[-1], own1 = lax.optimization_barrier((main0[-1], small[-1], own1))
    width0 = HALF // 2
    terms0 = [[t[:width0] for t in main0], [t[:width0] for t in small]]
    _, terms0 = halve_all(terms0, width0, mesh_shape, 2)
    four1 = gather_last(own1, mesh_shape)
    terms0, four1 = lax.optimization_barrier((terms0, four1))
    own0 = scatter_last(terms0, mesh_shape)
    held1 = double(four1, mesh_shape, 2)
    own0, held1 = lax.optimization_barrier((own0, held1))
    four0 = gather_last(own0, mesh_shape)
    late1 = exchange_bits(held1, mesh_shape, [1])
    other_held1 = exchange_bits(held1, mesh_shape, [0])
    four0, late1 = lax.optimization_barrier((four0, late1))
    held0 = double(four0, mesh_shape, 2)
    other_late1 = exchange_bits(late1, mesh_shape, [0])
    held0, other_late1 = lax.optimization_barrier((held0, other_late1))
    late0 = exchange_bits(held0, mesh_shape, [1])
    other_held0 = exchange_bits(held0, mesh_shape, [0])
    quarters1 = (held1, late1, other_held1, other_late1)
    inner_out, outer_out = hbm(layers, width, columns), hbm(layers, columns, width)
    quarter = HALF // 2

    def staging(quarters):
        return [
            vmem(2, quarters * quarter, depth, LANES, dtype=F32),
            pltpu.SemaphoreType.DMA((2, quarters * quarter)),
        ]

    grads = call(
        functools.partial(unpack_first, mesh_shape, images_all, 1, (0, 1, 2, 3)),
        "unpack_last_layer",
        in_vmem(quarters1),
        (inner_out, outer_out),
        staging(4),
        out_specs=[HBM] * 2,
        us=3,
    )
    grads = call(
        functools.partial(unpack_more, mesh_shape, images_all, 0, (0, 2)),
        "unpack_held",
        (*in_vmem((held0, other_held0)), *grads),
        (inner_out, outer_out),
        staging(2),
        in_specs=[VMEM] * 2 + [HBM] * 2,
        out_specs=[HBM] * 2,
        aliases={2: 0, 3: 1},
        us=2,
    )
    late0, grads = lax.optimization_barrier((late0, grads))
    other_late0 = exchange_bits(late0, mesh_shape, [0])
    grads = call(
        functools.partial(unpack_more, mesh_shape, images_all, 0, (1,)),
        "unpack_late",
        (*in_vmem((late0,)), *grads),
        (inner_out, outer_out),
        staging(1),
        in_specs=[VMEM] + [HBM] * 2,
        out_specs=[HBM] * 2,
        aliases={1: 0, 2: 1},
        us=1,
    )
    row = hbm(layers, width)
    stage, sems = staging(1)
    (
        inner_grad, outer_grad, weight_grad, aff_scale_grad, aff_shift_grad, bias_grad,
        scale_grad, mixer_aff_scale_grad, mixer_aff_shift_grad, inner_bias_grad,
        outer_bias_grad, mixer_scale_grad, magnitudes,
    ) = call(
        functools.partial(unpack_rest, mesh_shape, images_all),
        "unpack_rest",
        (*in_vmem((held0, late0, other_held0, other_late0)), *grads),
        (
            inner_out, outer_out, hbm(patches, layers, patches), row, row,
            hbm(layers, patches), row, row, row, hbm(layers, columns), row, row,
            hbm(layers, 2, 2),
        ),
        [stage, vmem(layers, padded, LANES, dtype=F32), vectors, sems],
        in_specs=[VMEM] * 4 + [HBM] * 2,
        out_specs=[HBM] * 2 + [VMEM] * 11,
        aliases={4: 0, 5: 1},
        us=2,
    )
    return (
        jnp.transpose(output, (0, 2, 1, 3)),
        jnp.transpose(input_grad, (0, 2, 1, 3)),
        aff_scale_grad,
        aff_shift_grad,
        jnp.transpose(weight_grad, (1, 0, 2)),
        bias_grad,
        scale_grad,
        mixer_aff_scale_grad,
        mixer_aff_shift_grad,
        inner_grad,
        inner_bias_grad,
        outer_grad,
        outer_bias_grad,
        mixer_scale_grad,
        magnitudes,
    )


def solution(mesh):
    split = P(None, "dp", None, None)
    owned = P("pipe", "dp", None, None)
    return jax.shard_map(
        functools.partial(on_device, dict(mesh.shape)),
        mesh=mesh,
        in_specs=(split,) * 3 + (P(),) * 12,
        out_specs=(owned,) * 2 + (P(),) * 13,
        check_vma=False,
    )
```

```python
import functools

import jax
import jax.numpy as jnp
from jax import lax
from jax.experimental import pallas as pl
from jax.experimental.pallas import tpu as pltpu
from jax.sharding import PartitionSpec as P

SQRT_HALF = 0.7071067811865476
INV_ROOT_TAU = 0.3989422804014327
AXES = ("dp", "pipe")
BLOCKS = 32
HALF = BLOCKS // 2
SCATTERED = 5
LANES = 384
VECTOR_ROWS = 16
BF = jnp.bfloat16
F32 = jnp.float32
VMEM = pl.BlockSpec(memory_space=pltpu.VMEM)
HBM = pl.BlockSpec(memory_space=pltpu.HBM)
VMEM_LIMIT = 28 * 2**20

CROSS_AFF_SCALE, CROSS_AFF_SHIFT, CROSS_SCALE, CROSS_BIAS = 0, 1, 2, 3
MIXER_AFF_SCALE, MIXER_AFF_SHIFT, MIXER_OUT_BIAS, MIXER_SCALE = 4, 5, 6, 7
MIXER_IN_BIAS = 8
SQUARES = 12


def dot(a, b, a_dim=1, b_dim=0):
    return lax.dot_general(
        a, b, (((a_dim,), (b_dim,)), ((), ())), preferred_element_type=F32
    )


def row_sum(values):
    return jnp.sum(values, axis=0, keepdims=True)


def phase_bits(mesh_shape):
    pipe_bits = [1 << b for b in range(mesh_shape["pipe"].bit_length() - 1)]
    dp_bits = [mesh_shape["pipe"] << b for b in range(mesh_shape["dp"].bit_length() - 1)]
    even = [pipe_bits[0], *pipe_bits[1:], *dp_bits]
    odd = list(even)
    odd[1], odd[2] = even[2], even[1]
    return even, odd


def block_code(mesh_shape, place):
    even, odd = phase_bits(mesh_shape)
    odd_place = place & 1
    code = jnp.int32(0)
    for even_bit, odd_bit in zip(even[:SCATTERED], odd[:SCATTERED]):
        bit = jnp.where(odd_place == 1, (place & odd_bit) != 0, (place & even_bit) != 0)
        code = 2 * code + bit.astype(jnp.int32)
    return code


def own_codes(mesh_shape):
    place = lax.axis_index("dp") * mesh_shape["pipe"] + lax.axis_index("pipe")
    return block_code(mesh_shape, place), block_code(mesh_shape, place ^ 1)


def kept_block(codes, slot):
    return codes[0] ^ slot


def sent_block(codes, slot):
    return codes[1] ^ slot


def inner_spot(block, rows, columns):
    across = columns // LANES
    row_at = pl.multiple_of((block // across) * rows, rows)
    return row_at, pl.multiple_of((block % across) * LANES, LANES)


def pack_halves(codes, block_at, kept_ref, sent_ref):
    @pl.loop(0, HALF)
    def _(slot):
        for block, out_ref in ((sent_block(codes, slot), sent_ref), (kept_block(codes, slot), kept_ref)):
            at = 0
            for piece in block_at(block):
                out_ref[slot, at : at + piece.shape[0], :] = piece
                at += piece.shape[0]


def pack_products(codes, inner_ref, outer_ref, kept_ref, sent_ref):
    depth = outer_ref.shape[0] // BLOCKS

    def block_at(block):
        row_at, column_at = inner_spot(block, depth, inner_ref.shape[1])
        outer_at = pl.multiple_of(block * depth, depth)
        return (
            inner_ref[pl.ds(row_at, depth), pl.ds(column_at, LANES)],
            outer_ref[pl.ds(outer_at, depth), :],
        )

    pack_halves(codes, block_at, kept_ref, sent_ref)


def read(ref, rows):
    return jnp.concatenate([ref[plane, rows, :] for plane in range(ref.shape[0])], axis=1)


def write(ref, rows, values):
    for plane in range(ref.shape[0]):
        ref[plane, rows, :] = values[:, plane * 128 : (plane + 1) * 128]


def rounded(values):
    return values.astype(BF).astype(F32)


def spread_rows(source_ref, target_ref):
    parts, patches, each, _ = source_ref.shape
    for part in range(parts):
        for patch in range(patches):
            base = (part * patches + patch) * each
            write(target_ref, slice(base, base + each), source_ref[part, patch].astype(F32))


def gather_rows(source_ref, target_ref):
    parts, patches, each, _ = target_ref.shape
    for part in range(parts):
        for patch in range(patches):
            base = (part * patches + patch) * each
            target_ref[part, patch] = read(source_ref, slice(base, base + each)).astype(BF)


def image_rows(image, patches, each):
    return pl.ds((image // each) * patches * each + image % each, patches, stride=each)


def row_tiles(rows):
    tile = max(t for t in range(16, 209, 16) if rows % t == 0)
    return [slice(at, at + tile) for at in range(0, rows, tile)]


def row_halves(rows):
    middle = -(-rows // 32) * 16
    return [slice(0, middle), slice(middle, rows)]


def cross_setup(mask_ref, weight_ref, bias_ref, kept_ref, keep_ref, bias_columns_ref, rows_ref):
    patches, layers, _ = weight_ref.shape
    padded = kept_ref.shape[2]
    for patch in range(patches):
        base = patch * layers
        weight = weight_ref[patch].astype(F32)
        rows_ref[0, base : base + layers, :] = weight[:, 0:128]
        rows_ref[1, base : base + layers, 0 : patches - 128] = weight[:, 128:]
    keep_ref[...] = jnp.zeros_like(keep_ref)
    kept_ref[...] = jnp.zeros_like(kept_ref)
    for layer in range(layers):
        weight = read(rows_ref, pl.ds(layer, patches, stride=layers))[:, 0:patches]
        for image in range(mask_ref.shape[0]):
            keep_row = mask_ref[image, layer : layer + 1, :].astype(F32)
            keep_ref[image, layer : layer + 1, 0:patches] = keep_row
            kept_ref[layer, image, 0:patches, 0:patches] = (weight * keep_row).astype(BF)
    bias_rows = jnp.concatenate([bias_ref[...], jnp.zeros((8 - layers, patches), F32)], axis=0)
    bias_rows = jnp.concatenate([bias_rows, jnp.zeros((8, 256 - patches), F32)], axis=1)
    bias_columns_ref[...] = jnp.transpose(bias_rows)[0:padded]


def cross_forward(
    layer, source_ref, target_ref, vectors_ref, kept_ref, bias_ref,
    aff_scale_ref, aff_shift_ref, scale_ref, low_ref, patches, each,
):
    aff_scale = aff_scale_ref[layer : layer + 1, :]
    aff_shift = aff_shift_ref[layer : layer + 1, :]
    scale = scale_ref[layer : layer + 1, :]
    branch_squares = jnp.zeros((1, LANES), F32)
    normed_squares = jnp.zeros((1, LANES), F32)
    for image in range(kept_ref.shape[1]):
        rows = image_rows(image, patches, each)
        stream = read(source_ref, rows)
        normed = aff_scale * stream + aff_shift
        low_ref[image, 0:patches, :] = normed.astype(BF)
        mixing = dot(kept_ref[layer, image], low_ref[image])
        branch = scale * (mixing + bias_ref[:, layer : layer + 1])[0:patches]
        write(target_ref, rows, rounded(stream + branch))
        branch_squares += row_sum(branch * branch)
        normed_squares += row_sum(normed * normed)
    vectors_ref[layer, SQUARES : SQUARES + 1, :] = branch_squares
    vectors_ref[layer, SQUARES + 1 : SQUARES + 2, :] = normed_squares


def mixer_hidden(
    layer, stream_ref, low_ref, fired_ref, slope_ref, vectors_ref,
    aff_scale_ref, aff_shift_ref, inner_ref, inner_bias_ref,
):
    aff_scale = aff_scale_ref[layer : layer + 1, :]
    aff_shift = aff_shift_ref[layer : layer + 1, :]
    tiles = row_tiles(stream_ref.shape[1])
    squares = jnp.zeros((1, LANES), F32)
    for rows in tiles:
        normed = aff_scale * read(stream_ref, rows) + aff_shift
        low_ref[rows, :] = normed.astype(BF)
        squares += row_sum(normed * normed)
    vectors_ref[layer, SQUARES + 3 : SQUARES + 4, :] = squares
    step = inner_ref.shape[1] // 3
    for part in range(3):
        at = slice(part * step, (part + 1) * step)
        for rows in tiles:
            hidden = dot(low_ref[rows, :], inner_ref[:, at]) + inner_bias_ref[layer : layer + 1, at]
            normal_cdf = 0.5 * (1.0 + lax.erf(hidden * SQRT_HALF))
            density = INV_ROOT_TAU * jnp.exp(-0.5 * hidden * hidden)
            fired_ref[rows, at] = (hidden * normal_cdf).astype(BF)
            slope_ref[rows, at] = (normal_cdf + hidden * density).astype(BF)


def mixer_backward(
    layer, upper_ref, low_ref, fired_ref, slope_ref, scaled_ref, inner_ref, outer_ref,
    inner_grad_ref, outer_grad_ref, vectors_ref, scale_ref,
):
    scale = scale_ref[layer : layer + 1, :]
    tiles = row_tiles(upper_ref.shape[1])
    bias = jnp.zeros((1, LANES), F32)
    for rows in tiles:
        result_grad = read(upper_ref, rows) * scale
        bias += row_sum(result_grad)
        scaled_ref[rows, :] = result_grad.astype(BF)
    vectors_ref[layer, MIXER_OUT_BIAS : MIXER_OUT_BIAS + 1, :] = bias
    columns = inner_ref.shape[1]
    step = 2 * LANES
    tiles = row_halves(upper_ref.shape[1])
    for part in range(columns // step):
        at = slice(part * step, (part + 1) * step)
        outer_grad_ref[at, :] = dot(fired_ref[:, at], scaled_ref[...], 0, 0).astype(BF)
        inner_bias = jnp.zeros((1, step), F32)
        for rows in tiles:
            hidden_grad = dot(scaled_ref[rows, :], outer_ref[at, :], 1, 1) * slope_ref[
                rows, at
            ].astype(F32)
            inner_bias += row_sum(hidden_grad)
            slope_ref[rows, at] = hidden_grad.astype(BF)
        for piece in range(step // LANES):
            row = MIXER_IN_BIAS + part * (step // LANES) + piece
            vectors_ref[layer, row : row + 1, :] = inner_bias[:, piece * LANES : (piece + 1) * LANES]
        inner_grad_ref[:, at] = dot(low_ref[...], slope_ref[:, at], 0, 0).astype(BF)


def mixer_input_grad(
    layer, upper_ref, stream_ref, hidden_grad_ref, target_ref, inner_ref, vectors_ref,
    aff_scale_ref,
):
    aff_scale = aff_scale_ref[layer : layer + 1, :]
    scale_grad = jnp.zeros((1, LANES), F32)
    shift_grad = jnp.zeros((1, LANES), F32)
    for rows in row_halves(upper_ref.shape[1]):
        normed_grad = dot(hidden_grad_ref[rows, :], inner_ref[...], 1, 1)
        scale_grad += row_sum(normed_grad * read(stream_ref, rows))
        shift_grad += row_sum(normed_grad)
        write(target_ref, rows, rounded(read(upper_ref, rows) + normed_grad * aff_scale))
    vectors_ref[layer, MIXER_AFF_SCALE : MIXER_AFF_SCALE + 1, :] = scale_grad
    vectors_ref[layer, MIXER_AFF_SHIFT : MIXER_AFF_SHIFT + 1, :] = shift_grad


def cross_backward(
    layer, stream_ref, upper_ref, target_ref, weight_grad_ref, vectors_ref, kept_ref, keep_ref,
    bias_ref, aff_scale_ref, aff_shift_ref, scale_ref, low_ref, mixing_low_ref, patches, each,
):
    padded = kept_ref.shape[2]
    aff_scale = aff_scale_ref[layer : layer + 1, :]
    aff_shift = aff_shift_ref[layer : layer + 1, :]
    scale = scale_ref[layer : layer + 1, :]
    aff_scale_grad = jnp.zeros((1, LANES), F32)
    aff_shift_grad = jnp.zeros((1, LANES), F32)
    scale_grad = jnp.zeros((1, LANES), F32)
    bias_grad = jnp.zeros((8, padded), F32)
    weight_grad = jnp.zeros((padded, padded), F32)
    ones = jnp.ones((8, LANES), BF)
    for image in range(kept_ref.shape[1]):
        rows = image_rows(image, patches, each)
        stream = read(stream_ref, rows)
        upper = read(upper_ref, rows)
        low_ref[image, 0:patches, :] = (aff_scale * stream + aff_shift).astype(BF)
        mixing_low_ref[image, 0:patches, :] = (upper * scale).astype(BF)
        kept = kept_ref[layer, image]
        shifted = dot(kept, low_ref[image]) + bias_ref[:, layer : layer + 1]
        scale_grad += row_sum(upper * shifted[0:patches])
        mixing_low = mixing_low_ref[image]
        bias_grad += dot(ones, mixing_low, 1, 1)
        weight_grad += (
            dot(mixing_low, low_ref[image], 1, 1) * keep_ref[image, layer : layer + 1, :]
        )
        normed_grad = dot(kept, mixing_low, 0, 0)[0:patches]
        aff_scale_grad += row_sum(normed_grad * stream)
        aff_shift_grad += row_sum(normed_grad)
        write(target_ref, rows, rounded(upper + normed_grad * aff_scale))
    weight_grad_ref[...] = weight_grad
    vectors_ref[layer, CROSS_AFF_SCALE : CROSS_AFF_SCALE + 1, :] = aff_scale_grad
    vectors_ref[layer, CROSS_AFF_SHIFT : CROSS_AFF_SHIFT + 1, :] = aff_shift_grad
    vectors_ref[layer, CROSS_SCALE : CROSS_SCALE + 1, :] = scale_grad
    vectors_ref[layer, CROSS_BIAS : CROSS_BIAS + 1, 0:padded] = bias_grad[0:1]


def clear_padding(*padded_refs, patches):
    for ref in padded_refs:
        images, padded, width = ref.shape
        for image in range(images):
            ref[image, padded - 16 :, :] = jnp.zeros((16, width), BF)


def first_kernel(
    mesh_shape,
    x_hbm, mask_hbm, g_hbm, inner_hbm, outer_hbm, cross_weight_hbm, cross_bias_hbm,
    inner_bias_hbm, mixer_aff_shift_hbm, *parameters_hbm_and_rest,
):
    parameters_hbm, rest = parameters_hbm_and_rest[:6], parameters_hbm_and_rest[6:]
    parameters, rest = rest[:6], rest[6:]
    cross_aff_scale, cross_aff_shift, cross_scale, mixer_aff_scale, outer_bias, mixer_scale = parameters
    (
    kept, sent, vectors, s0, s1, s2, s3, g_rows, low0, fired0, slope0, result0, fired1, slope1,
    inner0, outer0, inner1, outer1, kept_weight, keep, bias_columns,
    x_in, mask_in, g_in, cross_weight, cross_bias, inner_bias, mixer_aff_shift, weight_rows, padded_low,
    low1, scaled, inner_grad, outer_grad, sems,
    ) = rest
    _, patches, each, _ = x_in.shape
    per = x_in.shape[0]
    own = lax.axis_index("pipe") * per
    sources = (
        (cross_weight_hbm, cross_weight),
        (cross_bias_hbm, cross_bias),
        (inner_bias_hbm, inner_bias),
        (mixer_aff_shift_hbm, mixer_aff_shift),
        *zip(parameters_hbm, parameters),
        (mask_hbm.at[pl.ds(own, per)], mask_in),
        (x_hbm.at[pl.ds(own, per)], x_in),
        (inner_hbm.at[0], inner0),
        (outer_hbm.at[0], outer0),
        (inner_hbm.at[1], inner1),
        (g_hbm.at[pl.ds(own, per)], g_in),
        (outer_hbm.at[1], outer1),
    )
    copies = [
        pltpu.make_async_copy(source, target, sems.at[number])
        for number, (source, target) in enumerate(sources)
    ]
    for copy in copies:
        copy.start()
    vectors[...] = jnp.zeros_like(vectors)
    clear_padding(padded_low, patches=patches)
    for copy in copies[:-6]:
        copy.wait()
    copies = copies[-7:]
    masks = mask_in[...].reshape((per * each,) + mask_in.shape[2:])
    cross_setup(masks, cross_weight, cross_bias, kept_weight, keep, bias_columns, weight_rows)
    copies[1].wait()
    spread_rows(x_in, s0)
    cross = (kept_weight, bias_columns, cross_aff_scale, cross_aff_shift, cross_scale, padded_low)
    cross_forward(0, s0, s1, vectors, *cross, patches, each)
    copies[2].wait()
    mixer = (mixer_aff_scale, mixer_aff_shift)
    mixer_hidden(0, s1, low0, fired0, slope0, vectors, *mixer, inner0, inner_bias)
    copies[3].wait()
    squares = jnp.zeros((1, LANES), F32)
    for rows in row_halves(s1.shape[1]):
        result = dot(fired0[rows, :], outer0[...]) + outer_bias[0:1, :]
        result0[rows, :] = result.astype(BF)
        branch = mixer_scale[0:1, :] * result
        write(s2, rows, rounded(read(s1, rows) + branch))
        squares += row_sum(branch * branch)
    vectors[0, SQUARES + 2 : SQUARES + 3, :] = squares
    cross_forward(1, s2, s3, vectors, *cross, patches, each)
    copies[4].wait()
    mixer_hidden(1, s3, low1, fired1, slope1, vectors, *mixer, inner1, inner_bias)
    copies[5].wait()
    spread_rows(g_in, g_rows)
    copies[6].wait()
    mixer_backward(
        1, g_rows, low1, fired1, slope1, scaled, inner1, outer1, inner_grad, outer_grad,
        vectors, mixer_scale,
    )
    pack_products(own_codes(mesh_shape), inner_grad, outer_grad, kept, sent)


def second_kernel(
    s2, s3, g_rows, hidden_grad, inner1, kept_weight, keep, bias_columns, vectors_in,
    cross_aff_scale, cross_aff_shift, cross_scale, mixer_aff_scale,
    g2, weight_grad, vectors,
    g1, padded_low, padded_mixing, *, each,
):
    patches = s2.shape[1] // padded_low.shape[0]
    vectors[...] = vectors_in[...]
    clear_padding(padded_low, padded_mixing, patches=patches)
    mixer_input_grad(1, g_rows, s3, hidden_grad, g1, inner1, vectors, mixer_aff_scale)
    cross_backward(
        1, s2, g1, g2, weight_grad, vectors, kept_weight, keep, bias_columns,
        cross_aff_scale, cross_aff_shift, cross_scale, padded_low, padded_mixing, patches, each,
    )


def third_kernel(
    mesh_shape,
    s1, g2, low0, fired0, slope0, result0, inner0, outer0, s3, g_rows, fired1, outer1, vectors_in,
    mixer_aff_scale, outer_bias, mixer_scale,
    kept, sent, g1, vectors, output,
    hidden_grad, scaled, inner_grad, outer_grad, leaving,
):
    vectors[...] = vectors_in[...]
    hidden_grad[...] = slope0[...]
    mixer_backward(
        0, g2, low0, fired0, hidden_grad, scaled, inner0, outer0, inner_grad, outer_grad,
        vectors, mixer_scale,
    )
    pack_products(own_codes(mesh_shape), inner_grad, outer_grad, kept, sent)
    scale_grad = jnp.zeros((1, LANES), F32)
    for rows in row_tiles(g2.shape[1]):
        scale_grad += row_sum(read(g2, rows) * result0[rows, :].astype(F32))
    vectors[0, MIXER_SCALE : MIXER_SCALE + 1, :] = scale_grad
    mixer_input_grad(0, g2, s1, hidden_grad, g1, inner0, vectors, mixer_aff_scale)
    squares = jnp.zeros((1, LANES), F32)
    scale_grad = jnp.zeros((1, LANES), F32)
    for rows in row_halves(s3.shape[1]):
        result = dot(fired1[rows, :], outer1[...]) + outer_bias[1:2, :]
        scale_grad += row_sum(read(g_rows, rows) * result)
        branch = mixer_scale[1:2, :] * result
        write(leaving, rows, read(s3, rows) + branch)
        squares += row_sum(branch * branch)
    vectors[1, SQUARES + 2 : SQUARES + 3, :] = squares
    vectors[1, MIXER_SCALE : MIXER_SCALE + 1, :] = scale_grad
    gather_rows(leaving, output)


def fourth_kernel(
    mesh_shape,
    s0, g1, kept_weight, keep, bias_columns, weight_grad1, vectors_in,
    cross_aff_scale, cross_aff_shift, cross_scale,
    input_grad, kept, sent,
    g0, weight_grad0, vectors, small, padded_low, padded_mixing,
):
    _, patches, each, _ = input_grad.shape
    vectors[...] = vectors_in[...]
    clear_padding(padded_low, padded_mixing, patches=patches)
    cross_backward(
        0, s0, g1, g0, weight_grad0, vectors, kept_weight, keep, bias_columns,
        cross_aff_scale, cross_aff_shift, cross_scale, padded_low, padded_mixing, patches, each,
    )
    layers, padded = kept_weight.shape[0], kept_weight.shape[2]
    groups = padded // VECTOR_ROWS
    small[...] = jnp.zeros_like(small)
    for layer, weight_grad in enumerate((weight_grad0, weight_grad1)):
        for group in range(groups):
            rows = slice(group * VECTOR_ROWS, (group + 1) * VECTOR_ROWS)
            small[layer * groups + group, :, 0:padded] = weight_grad[rows, :].astype(BF)
        small[layers * groups + layer] = vectors[layer].astype(BF)
    pack_halves(own_codes(mesh_shape), lambda block: (small[block],), kept, sent)
    gather_rows(g0, input_grad)


def exchange_bits(values, mesh_shape, phases):
    even, odd = phase_bits(mesh_shape)
    places = range(mesh_shape["dp"] * mesh_shape["pipe"])

    def partner(place):
        for phase in phases:
            place ^= (odd if place & 1 else even)[phase]
        return place

    return lax.ppermute(values, AXES, [(i, partner(i)) for i in places])


def across(slot):
    return [phase for phase, bit in ((SCATTERED - 2, 2), (SCATTERED - 1, 1)) if slot & bit]


def part_sum(terms, start, stop):
    return sum(t[start:stop].astype(F32) for t in terms)


def joint_sum(families, start, stop):
    sums = [part_sum(terms, start, stop).astype(BF) for terms in families]
    return sums[0] if len(sums) == 1 else jnp.concatenate(sums, axis=1)


def halve(terms, width, mesh_shape, phase):
    half = width // 2
    leaving = part_sum(terms, half, width).astype(BF)
    return leaving, terms + [exchange_bits(leaving, mesh_shape, [phase])]


def halve_all(families, width, mesh_shape, phase):
    half = width // 2
    arrived = exchange_bits(joint_sum(families, half, width), mesh_shape, [phase])
    grown, at = [], 0
    for terms in families:
        rows = terms[0].shape[1]
        grown.append(terms + [arrived[:, at : at + rows]])
        at += rows
    return arrived, grown


LAST_SLOTS = (2, 3, 1)


def send_last(families, mesh_shape):
    leaving = [joint_sum(families, slot, slot + 1) for slot in LAST_SLOTS]
    return leaving, [
        exchange_bits(block, mesh_shape, across(slot)) for slot, block in zip(LAST_SLOTS, leaving)
    ]


def sum_last(families, arrived, mesh_shape):
    sums = [part_sum(terms, 0, 1) for terms in families]
    total = sums[0] if len(sums) == 1 else jnp.concatenate(sums, axis=1)
    total = total + sum(a.astype(F32) for a in arrived)
    for phase in range(SCATTERED, len(phase_bits(mesh_shape)[0])):
        total = total.astype(BF)
        total = total.astype(F32) + exchange_bits(total, mesh_shape, [phase]).astype(F32)
    return total.astype(BF)


def gather_last(own, mesh_shape):
    return {slot: exchange_bits(own, mesh_shape, across(slot)) for slot in LAST_SLOTS}


def join(own, arrived):
    return jnp.concatenate([own, arrived[1], arrived[2], arrived[3]], axis=0)


def double(held, mesh_shape, phase):
    return jnp.concatenate([held, exchange_bits(held, mesh_shape, [phase])], axis=0)


def after(values, *others):
    return lax.optimization_barrier((values, *others))[0]


def unpack_quarters(mesh_shape, images_all, layer, plan, quarters, inner_out, outer_out, stage, sems):
    codes = own_codes(mesh_shape)
    quarter, depth = HALF // 2, stage.shape[2]
    columns = inner_out.shape[2]

    def copies(number, slot):
        block_of, base = plan[number]
        block = block_of(codes, slot + base)
        row_at, column_at = inner_spot(block, depth, columns)
        outer_at = pl.multiple_of(block * depth, depth)
        index = number * quarter + slot
        return (
            pltpu.make_async_copy(
                stage.at[0, index],
                inner_out.at[layer, pl.ds(row_at, depth), pl.ds(column_at, LANES)],
                sems.at[0, index],
            ),
            pltpu.make_async_copy(
                stage.at[1, index], outer_out.at[layer, pl.ds(outer_at, depth), :], sems.at[1, index]
            ),
        )

    for number, values in enumerate(quarters):

        @pl.loop(0, quarter)
        def _(slot):
            for kind, copy in enumerate(copies(number, slot)):
                block = values[slot, kind * depth : (kind + 1) * depth, :]
                stage[kind, number * quarter + slot] = block.astype(F32) / images_all
                copy.start()

    for number in range(len(quarters)):

        @pl.loop(0, quarter)
        def _(slot):
            for copy in copies(number, slot):
                copy.wait()


QUARTERS = ((kept_block, 0), (kept_block, HALF // 2), (sent_block, 0), (sent_block, HALF // 2))


def unpack_first(mesh_shape, images_all, layer, numbers, *refs):
    quarters, outs = refs[: len(numbers)], refs[len(numbers) :]
    unpack_quarters(mesh_shape, images_all, layer, [QUARTERS[n] for n in numbers], quarters, *outs)


def unpack_more(mesh_shape, images_all, layer, numbers, *refs):
    quarters, outs = refs[: len(numbers)], refs[len(numbers) + 2 :]
    unpack_quarters(mesh_shape, images_all, layer, [QUARTERS[n] for n in numbers], quarters, *outs)


def unpack_rest(
    mesh_shape, images_all, held, late, other_held, other_late, inner_in, outer_in,
    inner_out, outer_out, weight_out, aff_scale_out, aff_shift_out, cross_bias_out,
    cross_scale_out, mixer_aff_scale_out, mixer_aff_shift_out, inner_bias_out, outer_bias_out,
    mixer_scale_out, magnitudes_out,
    stage, weight_rows, vectors, sems,
):
    patches, layers, _ = weight_out.shape
    groups = weight_rows.shape[1] // VECTOR_ROWS
    codes = own_codes(mesh_shape)
    for values, (block_of, base) in zip((held, late, other_held, other_late), QUARTERS):

        @pl.loop(0, HALF // 2)
        def _(slot):
            block = block_of(codes, slot + base)
            small = values[slot, 2 * stage.shape[2] :, :].astype(F32) / images_all

            @pl.when(block < layers * groups)
            def _():
                at = pl.multiple_of((block % groups) * VECTOR_ROWS, VECTOR_ROWS)
                weight_rows[block // groups, pl.ds(at, VECTOR_ROWS), :] = small

            @pl.when((block >= layers * groups) & (block < layers * (groups + 1)))
            def _():
                vectors[block - layers * groups] = small

    for layer in range(layers):
        row = slice(layer, layer + 1)
        weight_out[:, layer, :] = weight_rows[layer, 0:patches, 0:patches]
        aff_scale_out[row, :] = vectors[layer, CROSS_AFF_SCALE : CROSS_AFF_SCALE + 1, :]
        aff_shift_out[row, :] = vectors[layer, CROSS_AFF_SHIFT : CROSS_AFF_SHIFT + 1, :]
        cross_bias_out[row, :] = vectors[layer, CROSS_BIAS : CROSS_BIAS + 1, 0:patches]
        cross_scale_out[row, :] = vectors[layer, CROSS_SCALE : CROSS_SCALE + 1, :]
        mixer_aff_scale_out[row, :] = vectors[layer, MIXER_AFF_SCALE : MIXER_AFF_SCALE + 1, :]
        mixer_aff_shift_out[row, :] = vectors[layer, MIXER_AFF_SHIFT : MIXER_AFF_SHIFT + 1, :]
        outer_bias_out[row, :] = vectors[layer, MIXER_OUT_BIAS : MIXER_OUT_BIAS + 1, :]
        mixer_scale_out[row, :] = vectors[layer, MIXER_SCALE : MIXER_SCALE + 1, :]
        for piece in range(SQUARES - MIXER_IN_BIAS):
            at = slice(piece * LANES, (piece + 1) * LANES)
            inner_bias_out[row, at] = vectors[layer, MIXER_IN_BIAS + piece : MIXER_IN_BIAS + piece + 1, :]
        squares = vectors[layer, SQUARES : SQUARES + 4, :] / (patches * LANES)
        means = jnp.sqrt(jnp.sum(squares, axis=1, keepdims=True))
        for kind in range(2):
            for which in range(2):
                at = 2 * kind + which
                magnitudes_out[layer, kind : kind + 1, which : which + 1] = means[at : at + 1]
    unpack_quarters(
        mesh_shape, images_all, 0, [QUARTERS[3]], (other_late,), inner_out, outer_out, stage, sems
    )


def call(kernel, name, args, outs, scratch, in_specs=None, out_specs=None, aliases=None, us=1):
    return pl.pallas_call(
        kernel,
        out_shape=outs,
        in_specs=[VMEM] * len(args) if in_specs is None else in_specs,
        out_specs=[VMEM] * len(outs) if out_specs is None else out_specs,
        scratch_shapes=scratch,
        input_output_aliases=aliases or {},
        compiler_params=pltpu.CompilerParams(vmem_limit_bytes=VMEM_LIMIT),
        cost_estimate=pl.CostEstimate(
            flops=int(us * 1e9), bytes_accessed=int(us * 3e6), transcendentals=0
        ),
        name=name,
    )(*args)


def in_vmem(arrays):
    return [pltpu.with_memory_space_constraint(a, pltpu.VMEM) for a in arrays]


def in_hbm(arrays):
    return [pltpu.with_memory_space_constraint(a, pltpu.HBM) for a in arrays]


def on_device(
    mesh_shape,
    inputs,
    patch_masks,
    out_grad,
    cross_aff_scale,
    cross_aff_shift,
    cross_weight,
    cross_bias,
    cross_scale,
    mixer_aff_scale,
    mixer_aff_shift,
    mixer_in,
    mixer_in_bias,
    mixer_out,
    mixer_out_bias,
    mixer_scale,
):
    micros, each, patches, width = inputs.shape
    layers, _, columns = mixer_in.shape
    per = micros // mesh_shape["pipe"]
    images = per * each
    padded = -(-patches // 16) * 16
    rows = images * patches
    depth = width * columns // (BLOCKS * LANES)
    images_all = micros * each * mesh_shape["dp"]
    x_rows = jnp.transpose(inputs, (0, 2, 1, 3))
    g_rows = jnp.transpose(out_grad, (0, 2, 1, 3))
    weight_rows = jnp.transpose(cross_weight, (1, 0, 2))

    def vmem(*shape, dtype=BF):
        return pltpu.VMEM(shape, dtype)

    def hbm(*shape, dtype=F32):
        return jax.ShapeDtypeStruct(shape, dtype)

    stream = vmem(width // 128, rows, 128, dtype=F32)
    hidden = vmem(rows, columns)
    inner, outer = vmem(width, columns), vmem(columns, width)
    vectors = vmem(layers, VECTOR_ROWS, LANES, dtype=F32)
    padded_images = vmem(images, padded, width)
    local = (per, patches, each, width)
    first = call(
        functools.partial(first_kernel, mesh_shape),
        "forward",
        in_hbm((
            x_rows, patch_masks, g_rows, mixer_in, mixer_out, weight_rows, cross_bias,
            mixer_in_bias, mixer_aff_shift, cross_aff_scale, cross_aff_shift, cross_scale,
            mixer_aff_scale, mixer_out_bias, mixer_scale,
        )),
        (
            *[vmem(layers, width, dtype=F32)] * 6,
            vmem(HALF, 2 * depth, LANES),
            vmem(HALF, 2 * depth, LANES),
            vectors,
            *[stream] * 5,
            vmem(rows, width),
            hidden,
            hidden,
            vmem(rows, width),
            hidden,
            hidden,
            inner,
            outer,
            inner,
            outer,
            vmem(layers, images, padded, padded),
            vmem(images, 8, padded, dtype=F32),
            vmem(padded, 8, dtype=F32),
        ),
        [
            vmem(*local),
            vmem(per, each, layers, patches, dtype=jnp.int32),
            vmem(*local),
            vmem(patches, layers, patches),
            vmem(layers, patches, dtype=F32),
            vmem(layers, columns, dtype=F32),
            vmem(layers, width, dtype=F32),
            vmem(2, layers * patches, 128, dtype=F32),
            padded_images,
            vmem(rows, width),
            vmem(rows, width),
            inner,
            outer,
            pltpu.SemaphoreType.DMA((17,)),
        ],
        in_specs=[HBM] * 15,
        us=18,
    )
    aff_scale, aff_shift, scale, mixer_aff, result_bias, result_scale = in_vmem(first[:6])
    (
        kept1, sent1, sums, s0, s1, s2, s3, upper, low0, fired0, slope0, result0, fired1,
        hidden_grad1, inner0, outer0, inner1, outer1, kept_weight, keep, bias_columns,
    ) = first[6:]
    g2, weight_grad1, sums = call(
        functools.partial(second_kernel, each=each),
        "last_layer",
        (
            *in_vmem((
                s2, s3, upper, hidden_grad1, inner1, kept_weight, keep, bias_columns, sums,
            )),
            aff_scale, aff_shift, scale, mixer_aff,
        ),
        (stream, vmem(padded, padded, dtype=F32), vectors),
        [stream, padded_images, padded_images],
        us=4,
    )
    main1 = [kept1, exchange_bits(sent1, mesh_shape, [0])]
    leaving1, main1 = halve(main1, HALF, mesh_shape, 1)
    g2 = after(g2, leaving1)
    halves = vmem(HALF, 2 * depth, LANES)
    kept0, sent0, g1, sums, output = call(
        functools.partial(third_kernel, mesh_shape),
        "first_feed_forward",
        (
            *in_vmem((
                s1, g2, low0, fired0, slope0, result0, inner0, outer0, s3, upper, fired1, outer1,
                sums,
            )),
            mixer_aff, result_bias, result_scale,
        ),
        (halves, halves, stream, vectors, hbm(*local, dtype=BF)),
        [hidden, vmem(rows, width), inner, outer, stream],
        us=9,
    )
    sent0, sums = lax.optimization_barrier((sent0, sums, main1[-1]))[:2]
    main0 = [kept0, exchange_bits(sent0, mesh_shape, [0])]
    leaving1, main1 = halve(main1, HALF // 2, mesh_shape, 2)
    sums = after(sums, leaving1)
    halves = vmem(HALF, VECTOR_ROWS, LANES)
    input_grad, kept_small, sent_small = call(
        functools.partial(fourth_kernel, mesh_shape),
        "first_cross",
        (
            *in_vmem((s0, g1, kept_weight, keep, bias_columns, weight_grad1, sums)),
            aff_scale, aff_shift, scale,
        ),
        (hbm(*local, dtype=BF), halves, halves),
        [
            stream,
            vmem(padded, padded, dtype=F32),
            vectors,
            vmem(BLOCKS, VECTOR_ROWS, LANES),
            padded_images,
            padded_images,
        ],
        us=5,
    )
    small = [kept_small, exchange_bits(sent_small, mesh_shape, [0])]
    _, main0 = halve(main0, HALF, mesh_shape, 1)
    _, small = halve(small, HALF, mesh_shape, 1)
    own1 = sum_last([main1], send_last([main1], mesh_shape)[1], mesh_shape)
    main0[-1], small[-1], own1 = lax.optimization_barrier((main0[-1], small[-1], own1))
    width0 = HALF // 2
    terms0 = [[t[:width0] for t in main0], [t[:width0] for t in small]]
    _, terms0 = halve_all(terms0, width0, mesh_shape, 2)
    peers1 = gather_last(own1, mesh_shape)
    leaving0, arrived0 = send_last(terms0, mesh_shape)
    four1 = join(own1, after(peers1, leaving0))
    own0 = sum_last(terms0, arrived0, mesh_shape)
    more1 = exchange_bits(four1, mesh_shape, [2])
    peers0 = gather_last(own0, mesh_shape)
    more1 = after(more1, own0)
    held1 = jnp.concatenate([four1, more1], axis=0)
    four0 = join(own0, peers0)
    late1 = exchange_bits(held1, mesh_shape, [1])
    other_held1 = exchange_bits(held1, mesh_shape, [0])
    late1 = after(late1, four0)
    held0 = double(four0, mesh_shape, 2)
    other_late1 = exchange_bits(late1, mesh_shape, [0])
    other_late1 = after(other_late1, held0)
    late0 = exchange_bits(held0, mesh_shape, [1])
    other_held0 = exchange_bits(held0, mesh_shape, [0])
    quarters1 = (held1, late1, other_held1, other_late1)
    inner_out, outer_out = hbm(layers, width, columns), hbm(layers, columns, width)
    quarter = HALF // 2

    def staging(quarters):
        return [
            vmem(2, quarters * quarter, depth, LANES, dtype=F32),
            pltpu.SemaphoreType.DMA((2, quarters * quarter)),
        ]

    grads = call(
        functools.partial(unpack_first, mesh_shape, images_all, 1, (0, 1, 2, 3)),
        "unpack_last_layer",
        in_vmem(quarters1),
        (inner_out, outer_out),
        staging(4),
        out_specs=[HBM] * 2,
        us=3,
    )
    grads = call(
        functools.partial(unpack_more, mesh_shape, images_all, 0, (0, 2)),
        "unpack_held",
        (*in_vmem((held0, other_held0)), *grads),
        (inner_out, outer_out),
        staging(2),
        in_specs=[VMEM] * 2 + [HBM] * 2,
        out_specs=[HBM] * 2,
        aliases={2: 0, 3: 1},
        us=2,
    )
    late0, grads = lax.optimization_barrier((late0, grads))
    other_late0 = exchange_bits(late0, mesh_shape, [0])
    grads = call(
        functools.partial(unpack_more, mesh_shape, images_all, 0, (1,)),
        "unpack_late",
        (*in_vmem((late0,)), *grads),
        (inner_out, outer_out),
        staging(1),
        in_specs=[VMEM] + [HBM] * 2,
        out_specs=[HBM] * 2,
        aliases={1: 0, 2: 1},
        us=1,
    )
    row = hbm(layers, width)
    stage, sems = staging(1)
    (
        inner_grad, outer_grad, weight_grad, aff_scale_grad, aff_shift_grad, bias_grad,
        scale_grad, mixer_aff_scale_grad, mixer_aff_shift_grad, inner_bias_grad,
        outer_bias_grad, mixer_scale_grad, magnitudes,
    ) = call(
        functools.partial(unpack_rest, mesh_shape, images_all),
        "unpack_rest",
        (*in_vmem((held0, late0, other_held0, other_late0)), *grads),
        (
            inner_out, outer_out, hbm(patches, layers, patches), row, row,
            hbm(layers, patches), row, row, row, hbm(layers, columns), row, row,
            hbm(layers, 2, 2),
        ),
        [stage, vmem(layers, padded, LANES, dtype=F32), vectors, sems],
        in_specs=[VMEM] * 4 + [HBM] * 2,
        out_specs=[HBM] * 2 + [VMEM] * 11,
        aliases={4: 0, 5: 1},
        us=2,
    )
    return (
        jnp.transpose(output, (0, 2, 1, 3)),
        jnp.transpose(input_grad, (0, 2, 1, 3)),
        aff_scale_grad,
        aff_shift_grad,
        jnp.transpose(weight_grad, (1, 0, 2)),
        bias_grad,
        scale_grad,
        mixer_aff_scale_grad,
        mixer_aff_shift_grad,
        inner_grad,
        inner_bias_grad,
        outer_grad,
        outer_bias_grad,
        mixer_scale_grad,
        magnitudes,
    )


def solution(mesh):
    split = P(None, "dp", None, None)
    owned = P("pipe", "dp", None, None)
    return jax.shard_map(
        functools.partial(on_device, dict(mesh.shape)),
        mesh=mesh,
        in_specs=(split,) * 3 + (P(),) * 12,
        out_specs=(owned,) * 2 + (P(),) * 13,
        check_vma=False,
    )
```

```python
import functools

import jax
import jax.numpy as jnp
from jax import lax
from jax.experimental import pallas as pl
from jax.experimental.pallas import tpu as pltpu
from jax.sharding import PartitionSpec as P

SQRT_HALF = 0.7071067811865476
INV_ROOT_TAU = 0.3989422804014327
AXES = ("dp", "pipe")
BLOCKS = 32
HALF = BLOCKS // 2
SCATTERED = 5
LANES = 384
SMALL_ROWS = 8
VECTOR_ROWS = 24
BF = jnp.bfloat16
F32 = jnp.float32
VMEM = pl.BlockSpec(memory_space=pltpu.VMEM)
HBM = pl.BlockSpec(memory_space=pltpu.HBM)
VMEM_LIMIT = 28 * 2**20

CROSS_AFF_SCALE, CROSS_AFF_SHIFT, CROSS_SCALE, CROSS_BIAS = 0, 1, 2, 3
MIXER_AFF_SCALE, MIXER_AFF_SHIFT, MIXER_OUT_BIAS, MIXER_SCALE = 4, 5, 6, 7
MIXER_IN_BIAS = 8
SQUARES = 12
CROSS_REST = 16


def dot(a, b, a_dim=1, b_dim=0):
    return lax.dot_general(
        a, b, (((a_dim,), (b_dim,)), ((), ())), preferred_element_type=F32
    )


def row_sum(values):
    return jnp.sum(values, axis=0, keepdims=True)


def phase_bits(mesh_shape):
    pipe_bits = [1 << b for b in range(mesh_shape["pipe"].bit_length() - 1)]
    dp_bits = [mesh_shape["pipe"] << b for b in range(mesh_shape["dp"].bit_length() - 1)]
    even = [pipe_bits[0], *pipe_bits[1:], *dp_bits]
    odd = list(even)
    odd[1], odd[2] = even[2], even[1]
    return even, odd


def block_code(mesh_shape, place):
    even, odd = phase_bits(mesh_shape)
    odd_place = place & 1
    code = jnp.int32(0)
    for even_bit, odd_bit in zip(even[:SCATTERED], odd[:SCATTERED]):
        bit = jnp.where(odd_place == 1, (place & odd_bit) != 0, (place & even_bit) != 0)
        code = 2 * code + bit.astype(jnp.int32)
    return code


def own_codes(mesh_shape):
    place = lax.axis_index("dp") * mesh_shape["pipe"] + lax.axis_index("pipe")
    return block_code(mesh_shape, place), block_code(mesh_shape, place ^ 1)


def kept_block(codes, slot):
    return codes[0] ^ slot


def sent_block(codes, slot):
    return codes[1] ^ slot


def inner_spot(block, rows, columns):
    across = columns // LANES
    row_at = pl.multiple_of((block // across) * rows, rows)
    return row_at, pl.multiple_of((block % across) * LANES, LANES)


def pack_halves(codes, block_at, kept_ref, sent_ref):
    @pl.loop(0, HALF)
    def _(slot):
        for block, out_ref in ((sent_block(codes, slot), sent_ref), (kept_block(codes, slot), kept_ref)):
            at = 0
            for piece in block_at(block):
                out_ref[slot, at : at + piece.shape[0], :] = piece
                at += piece.shape[0]


def pack_products(codes, inner_ref, outer_ref, kept_ref, sent_ref):
    depth = outer_ref.shape[0] // BLOCKS

    def block_at(block):
        row_at, column_at = inner_spot(block, depth, inner_ref.shape[1])
        outer_at = pl.multiple_of(block * depth, depth)
        return (
            inner_ref[pl.ds(row_at, depth), pl.ds(column_at, LANES)],
            outer_ref[pl.ds(outer_at, depth), :],
        )

    pack_halves(codes, block_at, kept_ref, sent_ref)


def read(ref, rows):
    return jnp.concatenate([ref[plane, rows, :] for plane in range(ref.shape[0])], axis=1)


def write(ref, rows, values):
    for plane in range(ref.shape[0]):
        ref[plane, rows, :] = values[:, plane * 128 : (plane + 1) * 128]


def rounded(values):
    return values.astype(BF).astype(F32)


def spread_rows(source_ref, target_ref):
    parts, patches, each, _ = source_ref.shape
    for part in range(parts):
        for patch in range(patches):
            base = (part * patches + patch) * each
            write(target_ref, slice(base, base + each), source_ref[part, patch].astype(F32))


def gather_rows(source_ref, target_ref):
    parts, patches, each, _ = target_ref.shape
    for part in range(parts):
        for patch in range(patches):
            base = (part * patches + patch) * each
            target_ref[part, patch] = read(source_ref, slice(base, base + each)).astype(BF)


def image_rows(image, patches, each):
    return pl.ds((image // each) * patches * each + image % each, patches, stride=each)


def row_tiles(rows):
    tile = max(t for t in range(16, 209, 16) if rows % t == 0)
    return [slice(at, at + tile) for at in range(0, rows, tile)]


def row_halves(rows):
    middle = -(-rows // 32) * 16
    return [slice(0, middle), slice(middle, rows)]


def cross_setup(mask_ref, weight_ref, bias_ref, kept_ref, keep_ref, bias_columns_ref, rows_ref):
    patches, layers, _ = weight_ref.shape
    padded = kept_ref.shape[2]
    for patch in range(patches):
        base = patch * layers
        weight = weight_ref[patch].astype(F32)
        rows_ref[0, base : base + layers, :] = weight[:, 0:128]
        rows_ref[1, base : base + layers, 0 : patches - 128] = weight[:, 128:]
    keep_ref[...] = jnp.zeros_like(keep_ref)
    kept_ref[...] = jnp.zeros_like(kept_ref)
    for layer in range(layers):
        weight = read(rows_ref, pl.ds(layer, patches, stride=layers))[:, 0:patches]
        for image in range(mask_ref.shape[0]):
            keep_row = mask_ref[image, layer : layer + 1, :].astype(F32)
            keep_ref[image, layer : layer + 1, 0:patches] = keep_row
            kept_ref[layer, image, 0:patches, 0:patches] = (weight * keep_row).astype(BF)
    bias_rows = jnp.concatenate([bias_ref[...], jnp.zeros((8 - layers, patches), F32)], axis=0)
    bias_rows = jnp.concatenate([bias_rows, jnp.zeros((8, 256 - patches), F32)], axis=1)
    bias_columns_ref[...] = jnp.transpose(bias_rows)[0:padded]


def cross_forward(
    layer, source_ref, target_ref, vectors_ref, kept_ref, bias_ref,
    aff_scale_ref, aff_shift_ref, scale_ref, low_ref, patches, each,
):
    aff_scale = aff_scale_ref[layer : layer + 1, :]
    aff_shift = aff_shift_ref[layer : layer + 1, :]
    scale = scale_ref[layer : layer + 1, :]
    branch_squares = jnp.zeros((1, LANES), F32)
    normed_squares = jnp.zeros((1, LANES), F32)
    for image in range(kept_ref.shape[1]):
        rows = image_rows(image, patches, each)
        stream = read(source_ref, rows)
        normed = aff_scale * stream + aff_shift
        low_ref[image, 0:patches, :] = normed.astype(BF)
        mixing = dot(kept_ref[layer, image], low_ref[image])
        branch = scale * (mixing + bias_ref[:, layer : layer + 1])[0:patches]
        write(target_ref, rows, rounded(stream + branch))
        branch_squares += row_sum(branch * branch)
        normed_squares += row_sum(normed * normed)
    vectors_ref[layer, SQUARES : SQUARES + 1, :] = branch_squares
    vectors_ref[layer, SQUARES + 1 : SQUARES + 2, :] = normed_squares


def mixer_hidden(
    layer, stream_ref, low_ref, fired_ref, slope_ref, vectors_ref,
    aff_scale_ref, aff_shift_ref, inner_ref, inner_bias_ref,
):
    aff_scale = aff_scale_ref[layer : layer + 1, :]
    aff_shift = aff_shift_ref[layer : layer + 1, :]
    tiles = row_tiles(stream_ref.shape[1])
    squares = jnp.zeros((1, LANES), F32)
    for rows in tiles:
        normed = aff_scale * read(stream_ref, rows) + aff_shift
        low_ref[rows, :] = normed.astype(BF)
        squares += row_sum(normed * normed)
    vectors_ref[layer, SQUARES + 3 : SQUARES + 4, :] = squares
    step = inner_ref.shape[1] // 3
    for part in range(3):
        at = slice(part * step, (part + 1) * step)
        for rows in tiles:
            hidden = dot(low_ref[rows, :], inner_ref[:, at]) + inner_bias_ref[layer : layer + 1, at]
            normal_cdf = 0.5 * (1.0 + lax.erf(hidden * SQRT_HALF))
            density = INV_ROOT_TAU * jnp.exp(-0.5 * hidden * hidden)
            fired_ref[rows, at] = (hidden * normal_cdf).astype(BF)
            slope_ref[rows, at] = (normal_cdf + hidden * density).astype(BF)


def mixer_backward(
    layer, upper_ref, low_ref, fired_ref, slope_ref, scaled_ref, inner_ref, outer_ref,
    inner_grad_ref, outer_grad_ref, vectors_ref, scale_ref,
):
    scale = scale_ref[layer : layer + 1, :]
    tiles = row_tiles(upper_ref.shape[1])
    bias = jnp.zeros((1, LANES), F32)
    for rows in tiles:
        result_grad = read(upper_ref, rows) * scale
        bias += row_sum(result_grad)
        scaled_ref[rows, :] = result_grad.astype(BF)
    vectors_ref[layer, MIXER_OUT_BIAS : MIXER_OUT_BIAS + 1, :] = bias
    columns = inner_ref.shape[1]
    step = 2 * LANES
    tiles = row_halves(upper_ref.shape[1])
    for part in range(columns // step):
        at = slice(part * step, (part + 1) * step)
        outer_grad_ref[at, :] = dot(fired_ref[:, at], scaled_ref[...], 0, 0).astype(BF)
        inner_bias = jnp.zeros((1, step), F32)
        for rows in tiles:
            hidden_grad = dot(scaled_ref[rows, :], outer_ref[at, :], 1, 1) * slope_ref[
                rows, at
            ].astype(F32)
            inner_bias += row_sum(hidden_grad)
            slope_ref[rows, at] = hidden_grad.astype(BF)
        for piece in range(step // LANES):
            row = MIXER_IN_BIAS + part * (step // LANES) + piece
            vectors_ref[layer, row : row + 1, :] = inner_bias[:, piece * LANES : (piece + 1) * LANES]
        inner_grad_ref[:, at] = dot(low_ref[...], slope_ref[:, at], 0, 0).astype(BF)


def mixer_input_grad(
    layer, upper_ref, stream_ref, hidden_grad_ref, target_ref, inner_ref, vectors_ref,
    aff_scale_ref,
):
    aff_scale = aff_scale_ref[layer : layer + 1, :]
    scale_grad = jnp.zeros((1, LANES), F32)
    shift_grad = jnp.zeros((1, LANES), F32)
    for rows in row_halves(upper_ref.shape[1]):
        normed_grad = dot(hidden_grad_ref[rows, :], inner_ref[...], 1, 1)
        scale_grad += row_sum(normed_grad * read(stream_ref, rows))
        shift_grad += row_sum(normed_grad)
        write(target_ref, rows, rounded(read(upper_ref, rows) + normed_grad * aff_scale))
    vectors_ref[layer, MIXER_AFF_SCALE : MIXER_AFF_SCALE + 1, :] = scale_grad
    vectors_ref[layer, MIXER_AFF_SHIFT : MIXER_AFF_SHIFT + 1, :] = shift_grad


def cross_backward(
    layer, stream_ref, upper_ref, target_ref, weight_grad_ref, vectors_ref, kept_ref, keep_ref,
    bias_ref, aff_scale_ref, aff_shift_ref, scale_ref, low_ref, mixing_low_ref, patches, each,
):
    padded = kept_ref.shape[2]
    aff_scale = aff_scale_ref[layer : layer + 1, :]
    aff_shift = aff_shift_ref[layer : layer + 1, :]
    scale = scale_ref[layer : layer + 1, :]
    aff_scale_grad = jnp.zeros((1, LANES), F32)
    aff_shift_grad = jnp.zeros((1, LANES), F32)
    scale_grad = jnp.zeros((1, LANES), F32)
    bias_grad = jnp.zeros((8, padded), F32)
    weight_grad = jnp.zeros((padded, padded), F32)
    ones = jnp.ones((8, LANES), BF)
    for image in range(kept_ref.shape[1]):
        rows = image_rows(image, patches, each)
        stream = read(stream_ref, rows)
        upper = read(upper_ref, rows)
        low_ref[image, 0:patches, :] = (aff_scale * stream + aff_shift).astype(BF)
        mixing_low_ref[image, 0:patches, :] = (upper * scale).astype(BF)
        kept = kept_ref[layer, image]
        shifted = dot(kept, low_ref[image]) + bias_ref[:, layer : layer + 1]
        scale_grad += row_sum(upper * shifted[0:patches])
        mixing_low = mixing_low_ref[image]
        bias_grad += dot(ones, mixing_low, 1, 1)
        weight_grad += (
            dot(mixing_low, low_ref[image], 1, 1) * keep_ref[image, layer : layer + 1, :]
        )
        normed_grad = dot(kept, mixing_low, 0, 0)[0:patches]
        aff_scale_grad += row_sum(normed_grad * stream)
        aff_shift_grad += row_sum(normed_grad)
        write(target_ref, rows, rounded(upper + normed_grad * aff_scale))
    weight_grad_ref[0:padded, 0:padded] = weight_grad
    vectors_ref[layer, CROSS_AFF_SCALE : CROSS_AFF_SCALE + 1, :] = aff_scale_grad
    vectors_ref[layer, CROSS_AFF_SHIFT : CROSS_AFF_SHIFT + 1, :] = aff_shift_grad
    vectors_ref[layer, CROSS_SCALE : CROSS_SCALE + 1, :] = scale_grad
    vectors_ref[layer, CROSS_BIAS : CROSS_BIAS + 1, 0:padded] = bias_grad[0:1]


def clear_padding(*padded_refs, patches):
    for ref in padded_refs:
        images, padded, width = ref.shape
        for image in range(images):
            ref[image, padded - 16 :, :] = jnp.zeros((16, width), BF)


def first_kernel(
    mesh_shape,
    x_hbm, mask_hbm, g_hbm, inner_hbm, outer_hbm, cross_weight_hbm, cross_bias_hbm,
    inner_bias_hbm, mixer_aff_shift_hbm, *parameters_hbm_and_rest,
):
    parameters_hbm, rest = parameters_hbm_and_rest[:6], parameters_hbm_and_rest[6:]
    parameters, rest = rest[:6], rest[6:]
    cross_aff_scale, cross_aff_shift, cross_scale, mixer_aff_scale, outer_bias, mixer_scale = parameters
    (
    kept, sent, vectors, s0, s1, s2, s3, g_rows, low0, fired0, slope0, result0, fired1, slope1,
    inner0, outer0, inner1, outer1, kept_weight, keep, bias_columns,
    x_in, mask_in, g_in, cross_weight, cross_bias, inner_bias, mixer_aff_shift, weight_rows, padded_low,
    low1, scaled, inner_grad, outer_grad, sems,
    ) = rest
    _, patches, each, _ = x_in.shape
    per = x_in.shape[0]
    own = lax.axis_index("pipe") * per
    sources = (
        (cross_weight_hbm, cross_weight),
        (cross_bias_hbm, cross_bias),
        (inner_bias_hbm, inner_bias),
        (mixer_aff_shift_hbm, mixer_aff_shift),
        *zip(parameters_hbm, parameters),
        (mask_hbm.at[pl.ds(own, per)], mask_in),
        (x_hbm.at[pl.ds(own, per)], x_in),
        (inner_hbm.at[0], inner0),
        (outer_hbm.at[0], outer0),
        (inner_hbm.at[1], inner1),
        (g_hbm.at[pl.ds(own, per)], g_in),
        (outer_hbm.at[1], outer1),
    )
    copies = [
        pltpu.make_async_copy(source, target, sems.at[number])
        for number, (source, target) in enumerate(sources)
    ]
    for copy in copies:
        copy.start()
    vectors[...] = jnp.zeros_like(vectors)
    clear_padding(padded_low, patches=patches)
    for copy in copies[:-6]:
        copy.wait()
    copies = copies[-7:]
    masks = mask_in[...].reshape((per * each,) + mask_in.shape[2:])
    cross_setup(masks, cross_weight, cross_bias, kept_weight, keep, bias_columns, weight_rows)
    copies[1].wait()
    spread_rows(x_in, s0)
    cross = (kept_weight, bias_columns, cross_aff_scale, cross_aff_shift, cross_scale, padded_low)
    cross_forward(0, s0, s1, vectors, *cross, patches, each)
    copies[2].wait()
    mixer = (mixer_aff_scale, mixer_aff_shift)
    mixer_hidden(0, s1, low0, fired0, slope0, vectors, *mixer, inner0, inner_bias)
    copies[3].wait()
    squares = jnp.zeros((1, LANES), F32)
    for rows in row_halves(s1.shape[1]):
        result = dot(fired0[rows, :], outer0[...]) + outer_bias[0:1, :]
        result0[rows, :] = result.astype(BF)
        branch = mixer_scale[0:1, :] * result
        write(s2, rows, rounded(read(s1, rows) + branch))
        squares += row_sum(branch * branch)
    vectors[0, SQUARES + 2 : SQUARES + 3, :] = squares
    cross_forward(1, s2, s3, vectors, *cross, patches, each)
    copies[4].wait()
    mixer_hidden(1, s3, low1, fired1, slope1, vectors, *mixer, inner1, inner_bias)
    copies[5].wait()
    spread_rows(g_in, g_rows)
    copies[6].wait()
    mixer_backward(
        1, g_rows, low1, fired1, slope1, scaled, inner1, outer1, inner_grad, outer_grad,
        vectors, mixer_scale,
    )
    pack_products(own_codes(mesh_shape), inner_grad, outer_grad, kept, sent)


def second_kernel(
    s2, s3, g_rows, hidden_grad, inner1, kept_weight, keep, bias_columns, vectors_in,
    cross_aff_scale, cross_aff_shift, cross_scale, mixer_aff_scale,
    g2, weight_grad, vectors,
    g1, padded_low, padded_mixing, *, each,
):
    patches = s2.shape[1] // padded_low.shape[0]
    vectors[...] = vectors_in[...]
    clear_padding(padded_low, padded_mixing, patches=patches)
    mixer_input_grad(1, g_rows, s3, hidden_grad, g1, inner1, vectors, mixer_aff_scale)
    cross_backward(
        1, s2, g1, g2, weight_grad, vectors, kept_weight, keep, bias_columns,
        cross_aff_scale, cross_aff_shift, cross_scale, padded_low, padded_mixing, patches, each,
    )


def third_kernel(
    mesh_shape,
    s1, g2, low0, fired0, slope0, result0, inner0, outer0, s3, g_rows, fired1, outer1, vectors_in,
    mixer_aff_scale, outer_bias, mixer_scale,
    kept, sent, g1, vectors, output,
    hidden_grad, scaled, inner_grad, outer_grad, leaving,
):
    vectors[...] = vectors_in[...]
    hidden_grad[...] = slope0[...]
    mixer_backward(
        0, g2, low0, fired0, hidden_grad, scaled, inner0, outer0, inner_grad, outer_grad,
        vectors, mixer_scale,
    )
    pack_products(own_codes(mesh_shape), inner_grad, outer_grad, kept, sent)
    scale_grad = jnp.zeros((1, LANES), F32)
    for rows in row_tiles(g2.shape[1]):
        scale_grad += row_sum(read(g2, rows) * result0[rows, :].astype(F32))
    vectors[0, MIXER_SCALE : MIXER_SCALE + 1, :] = scale_grad
    mixer_input_grad(0, g2, s1, hidden_grad, g1, inner0, vectors, mixer_aff_scale)
    squares = jnp.zeros((1, LANES), F32)
    scale_grad = jnp.zeros((1, LANES), F32)
    for rows in row_halves(s3.shape[1]):
        result = dot(fired1[rows, :], outer1[...]) + outer_bias[1:2, :]
        scale_grad += row_sum(read(g_rows, rows) * result)
        branch = mixer_scale[1:2, :] * result
        write(leaving, rows, read(s3, rows) + branch)
        squares += row_sum(branch * branch)
    vectors[1, SQUARES + 2 : SQUARES + 3, :] = squares
    vectors[1, MIXER_SCALE : MIXER_SCALE + 1, :] = scale_grad
    gather_rows(leaving, output)


def pack_small(weight_grads, vectors_ref, small_ref, patches):
    groups = -(-patches // SMALL_ROWS)
    rows = groups * SMALL_ROWS
    first, second = (grad[0:rows, 128:256] for grad in weight_grads)
    lane = lax.broadcasted_iota(jnp.int32, (rows, 128), 1)
    shared = jnp.where(lane < 64, first, pltpu.roll(second, 64, 1))
    blocks = [grad[0:rows, 0:128] for grad in weight_grads] + [shared]
    small_ref[...] = jnp.zeros_like(small_ref)
    for part, block in enumerate(blocks):
        small_ref[0:groups, :, part * 128 : (part + 1) * 128] = block.astype(BF).reshape(
            groups, SMALL_ROWS, 128
        )
    for layer, grad in enumerate(weight_grads):
        rest = jnp.transpose(grad[:, 128:256])[64 : 64 + SMALL_ROWS]
        vectors_ref[layer, CROSS_REST : CROSS_REST + SMALL_ROWS, 0:256] = rest
        for piece in range(VECTOR_ROWS // SMALL_ROWS):
            at = groups + layer * (VECTOR_ROWS // SMALL_ROWS) + piece
            small_ref[at] = vectors_ref[
                layer, piece * SMALL_ROWS : (piece + 1) * SMALL_ROWS, :
            ].astype(BF)


def fourth_kernel(
    mesh_shape,
    s0, g1, kept_weight, keep, bias_columns, weight_grad1, vectors_in,
    cross_aff_scale, cross_aff_shift, cross_scale,
    input_grad, kept, sent,
    g0, weight_grad0, vectors, small, padded_low, padded_mixing,
):
    _, patches, each, _ = input_grad.shape
    vectors[...] = vectors_in[...]
    clear_padding(padded_low, padded_mixing, patches=patches)
    cross_backward(
        0, s0, g1, g0, weight_grad0, vectors, kept_weight, keep, bias_columns,
        cross_aff_scale, cross_aff_shift, cross_scale, padded_low, padded_mixing, patches, each,
    )
    pack_small((weight_grad0, weight_grad1), vectors, small, patches)
    pack_halves(own_codes(mesh_shape), lambda block: (small[block],), kept, sent)
    gather_rows(g0, input_grad)


def exchange_bits(values, mesh_shape, phases):
    even, odd = phase_bits(mesh_shape)
    places = range(mesh_shape["dp"] * mesh_shape["pipe"])

    def partner(place):
        for phase in phases:
            place ^= (odd if place & 1 else even)[phase]
        return place

    return lax.ppermute(values, AXES, [(i, partner(i)) for i in places])


def across(slot):
    return [phase for phase, bit in ((SCATTERED - 2, 2), (SCATTERED - 1, 1)) if slot & bit]


def part_sum(terms, start, stop):
    return sum(t[start:stop].astype(F32) for t in terms)


def joint_sum(families, start, stop):
    sums = [part_sum(terms, start, stop).astype(BF) for terms in families]
    return sums[0] if len(sums) == 1 else jnp.concatenate(sums, axis=1)


def halve(terms, width, mesh_shape, phase):
    half = width // 2
    leaving = part_sum(terms, half, width).astype(BF)
    return leaving, terms + [exchange_bits(leaving, mesh_shape, [phase])]


def halve_all(families, width, mesh_shape, phase):
    half = width // 2
    arrived = exchange_bits(joint_sum(families, half, width), mesh_shape, [phase])
    grown, at = [], 0
    for terms in families:
        rows = terms[0].shape[1]
        grown.append(terms + [arrived[:, at : at + rows]])
        at += rows
    return arrived, grown


LAST_SLOTS = (2, 3, 1)


def send_last(families, mesh_shape):
    leaving = [joint_sum(families, slot, slot + 1) for slot in LAST_SLOTS]
    return leaving, [
        exchange_bits(block, mesh_shape, across(slot)) for slot, block in zip(LAST_SLOTS, leaving)
    ]


def sum_last(families, arrived, mesh_shape):
    sums = [part_sum(terms, 0, 1) for terms in families]
    total = sums[0] if len(sums) == 1 else jnp.concatenate(sums, axis=1)
    total = total + sum(a.astype(F32) for a in arrived)
    for phase in range(SCATTERED, len(phase_bits(mesh_shape)[0])):
        total = total.astype(BF)
        total = total.astype(F32) + exchange_bits(total, mesh_shape, [phase]).astype(F32)
    return total.astype(BF)


def gather_last(own, mesh_shape):
    return {slot: exchange_bits(own, mesh_shape, across(slot)) for slot in LAST_SLOTS}


def join(own, arrived):
    return jnp.concatenate([own, arrived[1], arrived[2], arrived[3]], axis=0)


def double(held, mesh_shape, phase):
    return jnp.concatenate([held, exchange_bits(held, mesh_shape, [phase])], axis=0)


def after(values, *others):
    return lax.optimization_barrier((values, *others))[0]


def unpack_quarters(
    mesh_shape, images_all, layer, plan, quarters, inner_out, outer_out, stage, sems, meanwhile=None
):
    codes = own_codes(mesh_shape)
    quarter, depth = HALF // 2, stage.shape[2]
    columns = inner_out.shape[2]

    def copies(number, slot):
        block_of, base = plan[number]
        block = block_of(codes, slot + base)
        row_at, column_at = inner_spot(block, depth, columns)
        outer_at = pl.multiple_of(block * depth, depth)
        index = number * quarter + slot
        return (
            pltpu.make_async_copy(
                stage.at[0, index],
                inner_out.at[layer, pl.ds(row_at, depth), pl.ds(column_at, LANES)],
                sems.at[0, index],
            ),
            pltpu.make_async_copy(
                stage.at[1, index], outer_out.at[layer, pl.ds(outer_at, depth), :], sems.at[1, index]
            ),
        )

    for number, values in enumerate(quarters):

        @pl.loop(0, quarter)
        def _(slot):
            for kind, copy in enumerate(copies(number, slot)):
                block = values[slot, kind * depth : (kind + 1) * depth, :]
                stage[kind, number * quarter + slot] = block.astype(F32) / images_all
                copy.start()

    if meanwhile is not None:
        meanwhile()
    for number in range(len(quarters)):

        @pl.loop(0, quarter)
        def _(slot):
            for copy in copies(number, slot):
                copy.wait()


QUARTERS = ((kept_block, 0), (kept_block, HALF // 2), (sent_block, 0), (sent_block, HALF // 2))


def unpack_small(mesh_shape, plan, quarters, small_rows, depth):
    codes = own_codes(mesh_shape)
    for (block_of, base), values in zip(plan, quarters):

        @pl.loop(0, HALF // 2)
        def _(slot):
            small_rows[block_of(codes, slot + base)] = values[slot, 2 * depth :, :].astype(F32)


def unpack_last_layer(mesh_shape, images_all, *refs):
    unpack_quarters(mesh_shape, images_all, 1, QUARTERS, refs[:4], *refs[4:])


def unpack_held(
    mesh_shape, images_all, held, other_held, inner_in, outer_in,
    inner_out, outer_out, small_rows, stage, sems,
):
    plan, quarters = (QUARTERS[0], QUARTERS[2]), (held, other_held)
    unpack_quarters(mesh_shape, images_all, 0, plan, quarters, inner_out, outer_out, stage, sems)
    unpack_small(mesh_shape, plan, quarters, small_rows, stage.shape[2])


def unpack_late(
    mesh_shape, images_all, late, inner_in, outer_in, small_in,
    inner_out, outer_out, small_rows, stage, sems,
):
    plan, quarters = QUARTERS[1:2], (late,)
    unpack_quarters(mesh_shape, images_all, 0, plan, quarters, inner_out, outer_out, stage, sems)
    unpack_small(mesh_shape, plan, quarters, small_rows, stage.shape[2])


def unpack_rest(
    mesh_shape, images_all, other_late, inner_in, outer_in, small_in,
    inner_out, outer_out, small_rows, weight_out, aff_scale_out, aff_shift_out, cross_bias_out,
    cross_scale_out, mixer_aff_scale_out, mixer_aff_shift_out, inner_bias_out, outer_bias_out,
    mixer_scale_out, magnitudes_out,
    stage, rest_rows, sems,
):
    patches, layers, _ = weight_out.shape
    plan, quarters = QUARTERS[3:], (other_late,)

    def small_gradients():
        unpack_small(mesh_shape, plan, quarters, small_rows, stage.shape[2])
        groups = -(-patches // SMALL_ROWS)
        weights = (small_rows[0:groups] / images_all).reshape(groups * SMALL_ROWS, LANES)[0:patches]
        pieces = VECTOR_ROWS // SMALL_ROWS
        lane = lax.broadcasted_iota(jnp.int32, (patches, 128), 1)
        for layer in range(layers):
            row = slice(layer, layer + 1)
            at = groups + layer * pieces
            vectors = (small_rows[at : at + pieces] / images_all).reshape(VECTOR_ROWS, LANES)
            rest_rows[...] = jnp.zeros_like(rest_rows)
            rest_rows[64 : 64 + SMALL_ROWS, :] = vectors[CROSS_REST:, 0:256]
            rest = jnp.transpose(rest_rows[...])[0:patches]
            shared = weights[:, 256:384]
            if layer:
                shared = pltpu.roll(shared, 64, 1)
            last = jnp.where(lane < 64, shared, rest)
            weight_out[:, layer, 0:128] = weights[:, layer * 128 : (layer + 1) * 128]
            weight_out[:, layer, 128:] = last[:, 0 : patches - 128]
            for out, index in (
                (aff_scale_out, CROSS_AFF_SCALE),
                (aff_shift_out, CROSS_AFF_SHIFT),
                (cross_scale_out, CROSS_SCALE),
                (mixer_aff_scale_out, MIXER_AFF_SCALE),
                (mixer_aff_shift_out, MIXER_AFF_SHIFT),
                (outer_bias_out, MIXER_OUT_BIAS),
                (mixer_scale_out, MIXER_SCALE),
            ):
                out[row, :] = vectors[index : index + 1]
            cross_bias_out[row, :] = vectors[CROSS_BIAS : CROSS_BIAS + 1, 0:patches]
            for piece in range(SQUARES - MIXER_IN_BIAS):
                index = MIXER_IN_BIAS + piece
                inner_bias_out[row, piece * LANES : (piece + 1) * LANES] = vectors[index : index + 1]
            squares = vectors[SQUARES : SQUARES + 4] / (patches * LANES)
            means = jnp.sqrt(jnp.sum(squares, axis=1, keepdims=True))
            for kind in range(2):
                for which in range(2):
                    index = 2 * kind + which
                    magnitudes_out[layer, kind : kind + 1, which : which + 1] = means[index : index + 1]

    unpack_quarters(
        mesh_shape, images_all, 0, plan, quarters, inner_out, outer_out, stage, sems, small_gradients
    )


def call(kernel, name, args, outs, scratch, in_specs=None, out_specs=None, aliases=None, us=1):
    return pl.pallas_call(
        kernel,
        out_shape=outs,
        in_specs=[VMEM] * len(args) if in_specs is None else in_specs,
        out_specs=[VMEM] * len(outs) if out_specs is None else out_specs,
        scratch_shapes=scratch,
        input_output_aliases=aliases or {},
        compiler_params=pltpu.CompilerParams(vmem_limit_bytes=VMEM_LIMIT),
        cost_estimate=pl.CostEstimate(
            flops=int(us * 1e9), bytes_accessed=int(us * 3e6), transcendentals=0
        ),
        name=name,
    )(*args)


def in_vmem(arrays):
    return [pltpu.with_memory_space_constraint(a, pltpu.VMEM) for a in arrays]


def in_hbm(arrays):
    return [pltpu.with_memory_space_constraint(a, pltpu.HBM) for a in arrays]


def on_device(
    mesh_shape,
    inputs,
    patch_masks,
    out_grad,
    cross_aff_scale,
    cross_aff_shift,
    cross_weight,
    cross_bias,
    cross_scale,
    mixer_aff_scale,
    mixer_aff_shift,
    mixer_in,
    mixer_in_bias,
    mixer_out,
    mixer_out_bias,
    mixer_scale,
):
    micros, each, patches, width = inputs.shape
    layers, _, columns = mixer_in.shape
    per = micros // mesh_shape["pipe"]
    images = per * each
    padded = -(-patches // 16) * 16
    rows = images * patches
    depth = width * columns // (BLOCKS * LANES)
    images_all = micros * each * mesh_shape["dp"]
    x_rows = jnp.transpose(inputs, (0, 2, 1, 3))
    g_rows = jnp.transpose(out_grad, (0, 2, 1, 3))
    weight_rows = jnp.transpose(cross_weight, (1, 0, 2))

    def vmem(*shape, dtype=BF):
        return pltpu.VMEM(shape, dtype)

    def hbm(*shape, dtype=F32):
        return jax.ShapeDtypeStruct(shape, dtype)

    stream = vmem(width // 128, rows, 128, dtype=F32)
    hidden = vmem(rows, columns)
    inner, outer = vmem(width, columns), vmem(columns, width)
    vectors = vmem(layers, VECTOR_ROWS, LANES, dtype=F32)
    padded_images = vmem(images, padded, width)
    local = (per, patches, each, width)
    first = call(
        functools.partial(first_kernel, mesh_shape),
        "forward",
        in_hbm((
            x_rows, patch_masks, g_rows, mixer_in, mixer_out, weight_rows, cross_bias,
            mixer_in_bias, mixer_aff_shift, cross_aff_scale, cross_aff_shift, cross_scale,
            mixer_aff_scale, mixer_out_bias, mixer_scale,
        )),
        (
            *[vmem(layers, width, dtype=F32)] * 6,
            vmem(HALF, 2 * depth, LANES),
            vmem(HALF, 2 * depth, LANES),
            vectors,
            *[stream] * 5,
            vmem(rows, width),
            hidden,
            hidden,
            vmem(rows, width),
            hidden,
            hidden,
            inner,
            outer,
            inner,
            outer,
            vmem(layers, images, padded, padded),
            vmem(images, 8, padded, dtype=F32),
            vmem(padded, 8, dtype=F32),
        ),
        [
            vmem(*local),
            vmem(per, each, layers, patches, dtype=jnp.int32),
            vmem(*local),
            vmem(patches, layers, patches),
            vmem(layers, patches, dtype=F32),
            vmem(layers, columns, dtype=F32),
            vmem(layers, width, dtype=F32),
            vmem(2, layers * patches, 128, dtype=F32),
            padded_images,
            vmem(rows, width),
            vmem(rows, width),
            inner,
            outer,
            pltpu.SemaphoreType.DMA((17,)),
        ],
        in_specs=[HBM] * 15,
        us=18,
    )
    aff_scale, aff_shift, scale, mixer_aff, result_bias, result_scale = in_vmem(first[:6])
    (
        kept1, sent1, sums, s0, s1, s2, s3, upper, low0, fired0, slope0, result0, fired1,
        hidden_grad1, inner0, outer0, inner1, outer1, kept_weight, keep, bias_columns,
    ) = first[6:]
    g2, weight_grad1, sums = call(
        functools.partial(second_kernel, each=each),
        "last_layer",
        (
            *in_vmem((
                s2, s3, upper, hidden_grad1, inner1, kept_weight, keep, bias_columns, sums,
            )),
            aff_scale, aff_shift, scale, mixer_aff,
        ),
        (stream, vmem(256, 256, dtype=F32), vectors),
        [stream, padded_images, padded_images],
        us=4,
    )
    main1 = [kept1, exchange_bits(sent1, mesh_shape, [0])]
    leaving1, main1 = halve(main1, HALF, mesh_shape, 1)
    g2 = after(g2, leaving1)
    halves = vmem(HALF, 2 * depth, LANES)
    kept0, sent0, g1, sums, output = call(
        functools.partial(third_kernel, mesh_shape),
        "first_feed_forward",
        (
            *in_vmem((
                s1, g2, low0, fired0, slope0, result0, inner0, outer0, s3, upper, fired1, outer1,
                sums,
            )),
            mixer_aff, result_bias, result_scale,
        ),
        (halves, halves, stream, vectors, hbm(*local, dtype=BF)),
        [hidden, vmem(rows, width), inner, outer, stream],
        us=9,
    )
    sent0, sums = lax.optimization_barrier((sent0, sums, main1[-1]))[:2]
    main0 = [kept0, exchange_bits(sent0, mesh_shape, [0])]
    leaving1, main1 = halve(main1, HALF // 2, mesh_shape, 2)
    sums = after(sums, leaving1)
    halves = vmem(HALF, SMALL_ROWS, LANES)
    input_grad, kept_small, sent_small = call(
        functools.partial(fourth_kernel, mesh_shape),
        "first_cross",
        (
            *in_vmem((s0, g1, kept_weight, keep, bias_columns, weight_grad1, sums)),
            aff_scale, aff_shift, scale,
        ),
        (hbm(*local, dtype=BF), halves, halves),
        [
            stream,
            vmem(256, 256, dtype=F32),
            vectors,
            vmem(BLOCKS, SMALL_ROWS, LANES),
            padded_images,
            padded_images,
        ],
        us=5,
    )
    small = [kept_small, exchange_bits(sent_small, mesh_shape, [0])]
    _, main0 = halve(main0, HALF, mesh_shape, 1)
    _, small = halve(small, HALF, mesh_shape, 1)
    own1 = sum_last([main1], send_last([main1], mesh_shape)[1], mesh_shape)
    main0[-1], small[-1], own1 = lax.optimization_barrier((main0[-1], small[-1], own1))
    width0 = HALF // 2
    terms0 = [[t[:width0] for t in main0], [t[:width0] for t in small]]
    _, terms0 = halve_all(terms0, width0, mesh_shape, 2)
    peers1 = gather_last(own1, mesh_shape)
    leaving0, arrived0 = send_last(terms0, mesh_shape)
    four1 = join(own1, after(peers1, leaving0))
    own0 = sum_last(terms0, arrived0, mesh_shape)
    more1 = exchange_bits(four1, mesh_shape, [2])
    late1 = exchange_bits(four1, mesh_shape, [1])
    peers0 = gather_last(own0, mesh_shape)
    more1 = after(more1, own0)
    latest1 = exchange_bits(more1, mesh_shape, [1])
    four0 = join(own0, after(peers0, more1))
    held1 = jnp.concatenate([four1, more1], axis=0)
    other_held1 = exchange_bits(held1, mesh_shape, [0])
    more0 = exchange_bits(four0, mesh_shape, [2])
    late1, latest1 = after((late1, latest1), more0)
    late1 = jnp.concatenate([late1, latest1], axis=0)
    held0 = jnp.concatenate([four0, more0], axis=0)
    other_late1 = exchange_bits(late1, mesh_shape, [0])
    late0 = exchange_bits(held0, mesh_shape, [1])
    other_held0 = exchange_bits(held0, mesh_shape, [0])
    quarters1 = (held1, late1, other_held1, other_late1)
    inner_out, outer_out = hbm(layers, width, columns), hbm(layers, columns, width)
    quarter = HALF // 2

    def staging(quarters):
        return [
            vmem(2, quarters * quarter, depth, LANES, dtype=F32),
            pltpu.SemaphoreType.DMA((2, quarters * quarter)),
        ]

    small_rows = vmem(BLOCKS, SMALL_ROWS, LANES, dtype=F32)
    grads = call(
        functools.partial(unpack_last_layer, mesh_shape, images_all),
        "unpack_last_layer",
        in_vmem(quarters1),
        (inner_out, outer_out),
        staging(4),
        out_specs=[HBM] * 2,
        us=3,
    )
    *grads, rows_held = call(
        functools.partial(unpack_held, mesh_shape, images_all),
        "unpack_held",
        (*in_vmem((held0, other_held0)), *grads),
        (inner_out, outer_out, small_rows),
        staging(2),
        in_specs=[VMEM] * 2 + [HBM] * 2,
        out_specs=[HBM] * 2 + [VMEM],
        aliases={2: 0, 3: 1},
        us=2,
    )
    late0, grads = lax.optimization_barrier((late0, grads))
    other_late0 = exchange_bits(late0, mesh_shape, [0])
    *grads, rows_held = call(
        functools.partial(unpack_late, mesh_shape, images_all),
        "unpack_late",
        (*in_vmem((late0,)), *grads, *in_vmem((rows_held,))),
        (inner_out, outer_out, small_rows),
        staging(1),
        in_specs=[VMEM] + [HBM] * 2 + [VMEM],
        out_specs=[HBM] * 2 + [VMEM],
        aliases={1: 0, 2: 1, 3: 2},
        us=1,
    )
    row = hbm(layers, width)
    stage, sems = staging(1)
    (
        inner_grad, outer_grad, _, weight_grad, aff_scale_grad, aff_shift_grad, bias_grad,
        scale_grad, mixer_aff_scale_grad, mixer_aff_shift_grad, inner_bias_grad,
        outer_bias_grad, mixer_scale_grad, magnitudes,
    ) = call(
        functools.partial(unpack_rest, mesh_shape, images_all),
        "unpack_rest",
        (*in_vmem((other_late0,)), *grads, *in_vmem((rows_held,))),
        (
            inner_out, outer_out, small_rows, hbm(patches, layers, patches), row, row,
            hbm(layers, patches), row, row, row, hbm(layers, columns), row, row,
            hbm(layers, 2, 2),
        ),
        [stage, vmem(128, 256, dtype=F32), sems],
        in_specs=[VMEM] + [HBM] * 2 + [VMEM],
        out_specs=[HBM] * 2 + [VMEM] * 12,
        aliases={1: 0, 2: 1, 3: 2},
        us=2,
    )
    return (
        jnp.transpose(output, (0, 2, 1, 3)),
        jnp.transpose(input_grad, (0, 2, 1, 3)),
        aff_scale_grad,
        aff_shift_grad,
        jnp.transpose(weight_grad, (1, 0, 2)),
        bias_grad,
        scale_grad,
        mixer_aff_scale_grad,
        mixer_aff_shift_grad,
        inner_grad,
        inner_bias_grad,
        outer_grad,
        outer_bias_grad,
        mixer_scale_grad,
        magnitudes,
    )


def solution(mesh):
    split = P(None, "dp", None, None)
    owned = P("pipe", "dp", None, None)
    return jax.shard_map(
        functools.partial(on_device, dict(mesh.shape)),
        mesh=mesh,
        in_specs=(split,) * 3 + (P(),) * 12,
        out_specs=(owned,) * 2 + (P(),) * 13,
        check_vma=False,
    )
```

```python
import functools

import jax
import jax.numpy as jnp
from jax import lax
from jax.experimental import pallas as pl
from jax.experimental.pallas import tpu as pltpu
from jax.sharding import PartitionSpec as P

SQRT_HALF = 0.7071067811865476
INV_ROOT_TAU = 0.3989422804014327
AXES = ("dp", "pipe")
BLOCKS = 32
HALF = BLOCKS // 2
SCATTERED = 5
LANES = 384
SMALL_ROWS = 8
VECTOR_ROWS = 24
BF = jnp.bfloat16
F32 = jnp.float32
VMEM = pl.BlockSpec(memory_space=pltpu.VMEM)
HBM = pl.BlockSpec(memory_space=pltpu.HBM)
VMEM_LIMIT = 20 * 2**20

CROSS_AFF_SCALE, CROSS_AFF_SHIFT, CROSS_SCALE, CROSS_BIAS = 0, 1, 2, 3
MIXER_AFF_SCALE, MIXER_AFF_SHIFT, MIXER_OUT_BIAS, MIXER_SCALE = 4, 5, 6, 7
MIXER_IN_BIAS = 8
SQUARES = 12
CROSS_REST = 16


def dot(a, b, a_dim=1, b_dim=0):
    return lax.dot_general(
        a, b, (((a_dim,), (b_dim,)), ((), ())), preferred_element_type=F32
    )


def row_sum(values):
    return jnp.sum(values, axis=0, keepdims=True)


def phase_bits(mesh_shape):
    pipe_bits = [1 << b for b in range(mesh_shape["pipe"].bit_length() - 1)]
    dp_bits = [mesh_shape["pipe"] << b for b in range(mesh_shape["dp"].bit_length() - 1)]
    even = [pipe_bits[0], *pipe_bits[1:], *dp_bits]
    odd = list(even)
    odd[1], odd[2] = even[2], even[1]
    return even, odd


def block_code(mesh_shape, place):
    even, odd = phase_bits(mesh_shape)
    odd_place = place & 1
    code = jnp.int32(0)
    for even_bit, odd_bit in zip(even[:SCATTERED], odd[:SCATTERED]):
        bit = jnp.where(odd_place == 1, (place & odd_bit) != 0, (place & even_bit) != 0)
        code = 2 * code + bit.astype(jnp.int32)
    return code


def own_codes(mesh_shape):
    place = lax.axis_index("dp") * mesh_shape["pipe"] + lax.axis_index("pipe")
    return block_code(mesh_shape, place), block_code(mesh_shape, place ^ 1)


def kept_block(codes, slot):
    return codes[0] ^ slot


def sent_block(codes, slot):
    return codes[1] ^ slot


def inner_spot(block, rows, columns):
    across = columns // LANES
    row_at = pl.multiple_of((block // across) * rows, rows)
    return row_at, pl.multiple_of((block % across) * LANES, LANES)


def pack_halves(codes, block_at, kept_ref, sent_ref):
    @pl.loop(0, HALF)
    def _(slot):
        for block, out_ref in ((sent_block(codes, slot), sent_ref), (kept_block(codes, slot), kept_ref)):
            at = 0
            for piece in block_at(block):
                out_ref[slot, at : at + piece.shape[0], :] = piece
                at += piece.shape[0]


def pack_products(codes, inner_ref, outer_ref, kept_ref, sent_ref):
    depth = outer_ref.shape[0] // BLOCKS

    def block_at(block):
        row_at, column_at = inner_spot(block, depth, inner_ref.shape[1])
        outer_at = pl.multiple_of(block * depth, depth)
        return (
            inner_ref[pl.ds(row_at, depth), pl.ds(column_at, LANES)],
            outer_ref[pl.ds(outer_at, depth), :],
        )

    pack_halves(codes, block_at, kept_ref, sent_ref)


def read(ref, rows):
    return jnp.concatenate([ref[plane, rows, :] for plane in range(ref.shape[0])], axis=1)


def write(ref, rows, values):
    for plane in range(ref.shape[0]):
        ref[plane, rows, :] = values[:, plane * 128 : (plane + 1) * 128]


def rounded(values):
    return values.astype(BF).astype(F32)


def spread_rows(source_ref, target_ref):
    parts, patches, each, _ = source_ref.shape
    for part in range(parts):
        for patch in range(patches):
            base = (part * patches + patch) * each
            write(target_ref, slice(base, base + each), source_ref[part, patch].astype(F32))


def gather_rows(source_ref, target_ref):
    parts, patches, each, _ = target_ref.shape
    for part in range(parts):
        for patch in range(patches):
            base = (part * patches + patch) * each
            target_ref[part, patch] = read(source_ref, slice(base, base + each)).astype(BF)


def image_rows(image, patches, each):
    return pl.ds((image // each) * patches * each + image % each, patches, stride=each)


def row_tiles(rows):
    tile = max(t for t in range(16, 209, 16) if rows % t == 0)
    return [slice(at, at + tile) for at in range(0, rows, tile)]


def row_halves(rows):
    middle = -(-rows // 32) * 16
    return [slice(0, middle), slice(middle, rows)]


def cross_setup(mask_ref, weight_ref, bias_ref, kept_ref, keep_ref, bias_columns_ref, rows_ref):
    patches, layers, _ = weight_ref.shape
    padded = kept_ref.shape[2]
    for patch in range(patches):
        base = patch * layers
        weight = weight_ref[patch].astype(F32)
        rows_ref[0, base : base + layers, :] = weight[:, 0:128]
        rows_ref[1, base : base + layers, 0 : patches - 128] = weight[:, 128:]
    keep_ref[...] = jnp.zeros_like(keep_ref)
    kept_ref[...] = jnp.zeros_like(kept_ref)
    for layer in range(layers):
        weight = read(rows_ref, pl.ds(layer, patches, stride=layers))[:, 0:patches]
        for image in range(mask_ref.shape[0]):
            keep_row = mask_ref[image, layer : layer + 1, :].astype(F32)
            keep_ref[image, layer : layer + 1, 0:patches] = keep_row
            kept_ref[layer, image, 0:patches, 0:patches] = (weight * keep_row).astype(BF)
    bias_rows = jnp.concatenate([bias_ref[...], jnp.zeros((8 - layers, patches), F32)], axis=0)
    bias_rows = jnp.concatenate([bias_rows, jnp.zeros((8, 256 - patches), F32)], axis=1)
    bias_columns_ref[...] = jnp.transpose(bias_rows)[0:padded]


def cross_forward(
    layer, source_ref, target_ref, vectors_ref, kept_ref, bias_ref,
    aff_scale_ref, aff_shift_ref, scale_ref, low_ref, patches, each,
):
    aff_scale = aff_scale_ref[layer : layer + 1, :]
    aff_shift = aff_shift_ref[layer : layer + 1, :]
    scale = scale_ref[layer : layer + 1, :]
    branch_squares = jnp.zeros((1, LANES), F32)
    normed_squares = jnp.zeros((1, LANES), F32)
    for image in range(kept_ref.shape[1]):
        rows = image_rows(image, patches, each)
        stream = read(source_ref, rows)
        normed = aff_scale * stream + aff_shift
        low_ref[image, 0:patches, :] = normed.astype(BF)
        mixing = dot(kept_ref[layer, image], low_ref[image])
        branch = scale * (mixing + bias_ref[:, layer : layer + 1])[0:patches]
        write(target_ref, rows, rounded(stream + branch))
        branch_squares += row_sum(branch * branch)
        normed_squares += row_sum(normed * normed)
    vectors_ref[layer, SQUARES : SQUARES + 1, :] = branch_squares
    vectors_ref[layer, SQUARES + 1 : SQUARES + 2, :] = normed_squares


def mixer_hidden(
    layer, stream_ref, low_ref, fired_ref, slope_ref, vectors_ref,
    aff_scale_ref, aff_shift_ref, inner_ref, inner_bias_ref,
):
    aff_scale = aff_scale_ref[layer : layer + 1, :]
    aff_shift = aff_shift_ref[layer : layer + 1, :]
    tiles = row_tiles(stream_ref.shape[1])
    squares = jnp.zeros((1, LANES), F32)
    for rows in tiles:
        normed = aff_scale * read(stream_ref, rows) + aff_shift
        low_ref[rows, :] = normed.astype(BF)
        squares += row_sum(normed * normed)
    vectors_ref[layer, SQUARES + 3 : SQUARES + 4, :] = squares
    step = inner_ref.shape[1] // 3
    for part in range(3):
        at = slice(part * step, (part + 1) * step)
        for rows in tiles:
            hidden = dot(low_ref[rows, :], inner_ref[:, at]) + inner_bias_ref[layer : layer + 1, at]
            normal_cdf = 0.5 * (1.0 + lax.erf(hidden * SQRT_HALF))
            density = INV_ROOT_TAU * jnp.exp(-0.5 * hidden * hidden)
            fired_ref[rows, at] = (hidden * normal_cdf).astype(BF)
            slope_ref[rows, at] = (normal_cdf + hidden * density).astype(BF)


def mixer_backward(
    layer, upper_ref, low_ref, fired_ref, slope_ref, hidden_grad_ref, scaled_ref, inner_ref,
    outer_ref, inner_grad_ref, outer_grad_ref, vectors_ref, scale_ref,
):
    scale = scale_ref[layer : layer + 1, :]
    tiles = row_tiles(upper_ref.shape[1])
    bias = jnp.zeros((1, LANES), F32)
    for rows in tiles:
        result_grad = read(upper_ref, rows) * scale
        bias += row_sum(result_grad)
        scaled_ref[rows, :] = result_grad.astype(BF)
    vectors_ref[layer, MIXER_OUT_BIAS : MIXER_OUT_BIAS + 1, :] = bias
    columns = inner_ref.shape[1]
    step = 2 * LANES
    tiles = row_halves(upper_ref.shape[1])
    for part in range(columns // step):
        at = slice(part * step, (part + 1) * step)
        outer_grad_ref[at, :] = dot(fired_ref[:, at], scaled_ref[...], 0, 0).astype(BF)
        inner_bias = jnp.zeros((1, step), F32)
        for rows in tiles:
            hidden_grad = dot(scaled_ref[rows, :], outer_ref[at, :], 1, 1) * slope_ref[
                rows, at
            ].astype(F32)
            inner_bias += row_sum(hidden_grad)
            hidden_grad_ref[rows, at] = hidden_grad.astype(BF)
        for piece in range(step // LANES):
            row = MIXER_IN_BIAS + part * (step // LANES) + piece
            vectors_ref[layer, row : row + 1, :] = inner_bias[:, piece * LANES : (piece + 1) * LANES]
        inner_grad_ref[:, at] = dot(low_ref[...], hidden_grad_ref[:, at], 0, 0).astype(BF)


def mixer_input_grad(
    layer, upper_ref, stream_ref, hidden_grad_ref, target_ref, inner_ref, vectors_ref,
    aff_scale_ref,
):
    aff_scale = aff_scale_ref[layer : layer + 1, :]
    scale_grad = jnp.zeros((1, LANES), F32)
    shift_grad = jnp.zeros((1, LANES), F32)
    for rows in row_halves(upper_ref.shape[1]):
        normed_grad = dot(hidden_grad_ref[rows, :], inner_ref[...], 1, 1)
        scale_grad += row_sum(normed_grad * read(stream_ref, rows))
        shift_grad += row_sum(normed_grad)
        write(target_ref, rows, rounded(read(upper_ref, rows) + normed_grad * aff_scale))
    vectors_ref[layer, MIXER_AFF_SCALE : MIXER_AFF_SCALE + 1, :] = scale_grad
    vectors_ref[layer, MIXER_AFF_SHIFT : MIXER_AFF_SHIFT + 1, :] = shift_grad


def cross_backward(
    layer, stream_ref, upper_ref, target_ref, weight_grad_ref, vectors_ref, kept_ref, keep_ref,
    bias_ref, aff_scale_ref, aff_shift_ref, scale_ref, low_ref, mixing_low_ref, patches, each,
):
    padded = kept_ref.shape[2]
    aff_scale = aff_scale_ref[layer : layer + 1, :]
    aff_shift = aff_shift_ref[layer : layer + 1, :]
    scale = scale_ref[layer : layer + 1, :]
    aff_scale_grad = jnp.zeros((1, LANES), F32)
    aff_shift_grad = jnp.zeros((1, LANES), F32)
    scale_grad = jnp.zeros((1, LANES), F32)
    bias_grad = jnp.zeros((8, padded), F32)
    weight_grad = jnp.zeros((padded, padded), F32)
    ones = jnp.ones((8, LANES), BF)
    for image in range(kept_ref.shape[1]):
        rows = image_rows(image, patches, each)
        stream = read(stream_ref, rows)
        upper = read(upper_ref, rows)
        low_ref[image, 0:patches, :] = (aff_scale * stream + aff_shift).astype(BF)
        mixing_low_ref[image, 0:patches, :] = (upper * scale).astype(BF)
        kept = kept_ref[layer, image]
        shifted = dot(kept, low_ref[image]) + bias_ref[:, layer : layer + 1]
        scale_grad += row_sum(upper * shifted[0:patches])
        mixing_low = mixing_low_ref[image]
        bias_grad += dot(ones, mixing_low, 1, 1)
        weight_grad += (
            dot(mixing_low, low_ref[image], 1, 1) * keep_ref[image, layer : layer + 1, :]
        )
        normed_grad = dot(kept, mixing_low, 0, 0)[0:patches]
        aff_scale_grad += row_sum(normed_grad * stream)
        aff_shift_grad += row_sum(normed_grad)
        write(target_ref, rows, rounded(upper + normed_grad * aff_scale))
    weight_grad_ref[0:padded, 0:padded] = weight_grad
    vectors_ref[layer, CROSS_AFF_SCALE : CROSS_AFF_SCALE + 1, :] = aff_scale_grad
    vectors_ref[layer, CROSS_AFF_SHIFT : CROSS_AFF_SHIFT + 1, :] = aff_shift_grad
    vectors_ref[layer, CROSS_SCALE : CROSS_SCALE + 1, :] = scale_grad
    vectors_ref[layer, CROSS_BIAS : CROSS_BIAS + 1, 0:padded] = bias_grad[0:1]


def clear_padding(*padded_refs, patches):
    for ref in padded_refs:
        images, padded, width = ref.shape
        for image in range(images):
            ref[image, padded - 16 :, :] = jnp.zeros((16, width), BF)


def first_kernel(
    mesh_shape,
    x_hbm, mask_hbm, g_hbm, inner_hbm, outer_hbm, cross_weight_hbm, cross_bias_hbm,
    inner_bias_hbm, mixer_aff_shift_hbm, *parameters_hbm_and_rest,
):
    parameters_hbm, rest = parameters_hbm_and_rest[:6], parameters_hbm_and_rest[6:]
    parameters, rest = rest[:6], rest[6:]
    cross_aff_scale, cross_aff_shift, cross_scale, mixer_aff_scale, outer_bias, mixer_scale = parameters
    (
    kept, sent, vectors, s0, s1, s2, s3, g_rows, low0, fired0, slope0, result0, fired1, slope1,
    inner0, outer0, inner1, outer1, kept_weight, keep, bias_columns,
    x_in, mask_in, g_in, cross_weight, cross_bias, inner_bias, mixer_aff_shift, weight_rows, padded_low,
    low1, scaled, inner_grad, outer_grad, sems,
    ) = rest
    _, patches, each, _ = x_in.shape
    per = x_in.shape[0]
    own = lax.axis_index("pipe") * per
    mine = pl.ds(own, per)
    groups = (
        ((cross_weight_hbm, cross_weight), (mask_hbm.at[mine], mask_in), (cross_bias_hbm, cross_bias)),
        ((x_hbm.at[mine], x_in), *zip(parameters_hbm, parameters)),
        (
            (inner_hbm.at[0], inner0),
            (inner_bias_hbm, inner_bias),
            (mixer_aff_shift_hbm, mixer_aff_shift),
        ),
        ((outer_hbm.at[0], outer0),),
        ((inner_hbm.at[1], inner1),),
        ((g_hbm.at[mine], g_in), (outer_hbm.at[1], outer1)),
    )
    arrivals, number = [], 0
    for group in groups:
        arrivals.append([])
        for source, target in group:
            copy = pltpu.make_async_copy(source, target, sems.at[number])
            copy.start()
            arrivals[-1].append(copy)
            number += 1

    def wait_for(group):
        for copy in arrivals[group]:
            copy.wait()

    vectors[...] = jnp.zeros_like(vectors)
    clear_padding(padded_low, patches=patches)
    wait_for(0)
    masks = mask_in[...].reshape((per * each,) + mask_in.shape[2:])
    cross_setup(masks, cross_weight, cross_bias, kept_weight, keep, bias_columns, weight_rows)
    wait_for(1)
    spread_rows(x_in, s0)
    cross = (kept_weight, bias_columns, cross_aff_scale, cross_aff_shift, cross_scale, padded_low)
    cross_forward(0, s0, s1, vectors, *cross, patches, each)
    wait_for(2)
    mixer = (mixer_aff_scale, mixer_aff_shift)
    mixer_hidden(0, s1, low0, fired0, slope0, vectors, *mixer, inner0, inner_bias)
    wait_for(3)
    squares = jnp.zeros((1, LANES), F32)
    for rows in row_halves(s1.shape[1]):
        result = dot(fired0[rows, :], outer0[...]) + outer_bias[0:1, :]
        result0[rows, :] = result.astype(BF)
        branch = mixer_scale[0:1, :] * result
        write(s2, rows, rounded(read(s1, rows) + branch))
        squares += row_sum(branch * branch)
    vectors[0, SQUARES + 2 : SQUARES + 3, :] = squares
    cross_forward(1, s2, s3, vectors, *cross, patches, each)
    wait_for(4)
    mixer_hidden(1, s3, low1, fired1, slope1, vectors, *mixer, inner1, inner_bias)
    wait_for(5)
    spread_rows(g_in, g_rows)
    mixer_backward(
        1, g_rows, low1, fired1, slope1, slope1, scaled, inner1, outer1, inner_grad, outer_grad,
        vectors, mixer_scale,
    )
    pack_products(own_codes(mesh_shape), inner_grad, outer_grad, kept, sent)


def second_kernel(
    s2, s3, g_rows, hidden_grad, inner1, kept_weight, keep, bias_columns, vectors_in,
    cross_aff_scale, cross_aff_shift, cross_scale, mixer_aff_scale,
    g2, weight_grad, vectors,
    g1, padded_low, padded_mixing, *, each,
):
    patches = s2.shape[1] // padded_low.shape[0]
    vectors[...] = vectors_in[...]
    clear_padding(padded_low, padded_mixing, patches=patches)
    mixer_input_grad(1, g_rows, s3, hidden_grad, g1, inner1, vectors, mixer_aff_scale)
    cross_backward(
        1, s2, g1, g2, weight_grad, vectors, kept_weight, keep, bias_columns,
        cross_aff_scale, cross_aff_shift, cross_scale, padded_low, padded_mixing, patches, each,
    )


def third_kernel(
    mesh_shape,
    s1, g2, low0, fired0, slope0, inner0, outer0, s3, g_rows, fired1, outer1, vectors_in,
    mixer_aff_scale, outer_bias, mixer_scale,
    kept, sent, g1, vectors, leaving,
    hidden_grad, scaled, inner_grad, outer_grad,
):
    vectors[...] = vectors_in[...]
    mixer_backward(
        0, g2, low0, fired0, slope0, hidden_grad, scaled, inner0, outer0, inner_grad, outer_grad,
        vectors, mixer_scale,
    )
    pack_products(own_codes(mesh_shape), inner_grad, outer_grad, kept, sent)
    mixer_input_grad(0, g2, s1, hidden_grad, g1, inner0, vectors, mixer_aff_scale)
    squares = jnp.zeros((1, LANES), F32)
    scale_grad = jnp.zeros((1, LANES), F32)
    for rows in row_halves(s3.shape[1]):
        result = dot(fired1[rows, :], outer1[...]) + outer_bias[1:2, :]
        scale_grad += row_sum(read(g_rows, rows) * result)
        branch = mixer_scale[1:2, :] * result
        write(leaving, rows, read(s3, rows) + branch)
        squares += row_sum(branch * branch)
    vectors[1, SQUARES + 2 : SQUARES + 3, :] = squares
    vectors[1, MIXER_SCALE : MIXER_SCALE + 1, :] = scale_grad


def pack_small(weight_grads, vectors_ref, small_ref, patches):
    groups = -(-patches // SMALL_ROWS)
    rows = groups * SMALL_ROWS
    first, second = (grad[0:rows, 128:256] for grad in weight_grads)
    lane = lax.broadcasted_iota(jnp.int32, (rows, 128), 1)
    shared = jnp.where(lane < 64, first, pltpu.roll(second, 64, 1))
    blocks = [grad[0:rows, 0:128] for grad in weight_grads] + [shared]
    small_ref[...] = jnp.zeros_like(small_ref)
    for part, block in enumerate(blocks):
        small_ref[0:groups, :, part * 128 : (part + 1) * 128] = block.astype(BF).reshape(
            groups, SMALL_ROWS, 128
        )
    for layer, grad in enumerate(weight_grads):
        rest = jnp.transpose(grad[:, 128:256])[64 : 64 + SMALL_ROWS]
        vectors_ref[layer, CROSS_REST : CROSS_REST + SMALL_ROWS, 0:256] = rest
        for piece in range(VECTOR_ROWS // SMALL_ROWS):
            at = groups + layer * (VECTOR_ROWS // SMALL_ROWS) + piece
            small_ref[at] = vectors_ref[
                layer, piece * SMALL_ROWS : (piece + 1) * SMALL_ROWS, :
            ].astype(BF)


def fourth_kernel(
    mesh_shape,
    s0, g1, kept_weight, keep, bias_columns, weight_grad1, vectors_in, g2, result0, leaving,
    cross_aff_scale, cross_aff_shift, cross_scale,
    input_grad, output, kept, sent,
    g0, weight_grad0, vectors, small, padded_low, padded_mixing,
):
    _, patches, each, _ = input_grad.shape
    vectors[...] = vectors_in[...]
    clear_padding(padded_low, padded_mixing, patches=patches)
    cross_backward(
        0, s0, g1, g0, weight_grad0, vectors, kept_weight, keep, bias_columns,
        cross_aff_scale, cross_aff_shift, cross_scale, padded_low, padded_mixing, patches, each,
    )
    scale_grad = jnp.zeros((1, LANES), F32)
    for rows in row_tiles(g2.shape[1]):
        scale_grad += row_sum(read(g2, rows) * result0[rows, :].astype(F32))
    vectors[0, MIXER_SCALE : MIXER_SCALE + 1, :] = scale_grad
    pack_small((weight_grad0, weight_grad1), vectors, small, patches)
    pack_halves(own_codes(mesh_shape), lambda block: (small[block],), kept, sent)
    gather_rows(g0, input_grad)
    gather_rows(leaving, output)


def exchange_bits(values, mesh_shape, phases):
    even, odd = phase_bits(mesh_shape)
    places = range(mesh_shape["dp"] * mesh_shape["pipe"])

    def partner(place):
        for phase in phases:
            place ^= (odd if place & 1 else even)[phase]
        return place

    return lax.ppermute(values, AXES, [(i, partner(i)) for i in places])


def across(slot):
    return [phase for phase, bit in ((SCATTERED - 2, 2), (SCATTERED - 1, 1)) if slot & bit]


def part_sum(terms, start, stop):
    return sum(t[start:stop].astype(F32) for t in terms)


def joint_sum(families, start, stop):
    sums = [part_sum(terms, start, stop).astype(BF) for terms in families]
    return sums[0] if len(sums) == 1 else jnp.concatenate(sums, axis=1)


def halve(terms, width, mesh_shape, phase):
    half = width // 2
    leaving = part_sum(terms, half, width).astype(BF)
    return leaving, terms + [exchange_bits(leaving, mesh_shape, [phase])]


def halve_all(families, width, mesh_shape, phase):
    half = width // 2
    arrived = exchange_bits(joint_sum(families, half, width), mesh_shape, [phase])
    grown, at = [], 0
    for terms in families:
        rows = terms[0].shape[1]
        grown.append(terms + [arrived[:, at : at + rows]])
        at += rows
    return arrived, grown


def send_last(families, mesh_shape, slots):
    leaving = [joint_sum(families, slot, slot + 1) for slot in slots]
    return leaving, [
        exchange_bits(block, mesh_shape, across(slot)) for slot, block in zip(slots, leaving)
    ]


def sum_last(families, arrived, mesh_shape):
    sums = [part_sum(terms, 0, 1) for terms in families]
    total = sums[0] if len(sums) == 1 else jnp.concatenate(sums, axis=1)
    total = total + sum(a.astype(F32) for a in arrived)
    for phase in range(SCATTERED, len(phase_bits(mesh_shape)[0])):
        total = total.astype(BF)
        total = total.astype(F32) + exchange_bits(total, mesh_shape, [phase]).astype(F32)
    return total.astype(BF)


def gather_last(own, mesh_shape, slots):
    return {slot: exchange_bits(own, mesh_shape, across(slot)) for slot in slots}


def join(own, arrived):
    return jnp.concatenate([own, arrived[1], arrived[2], arrived[3]], axis=0)


def double(held, mesh_shape, phase):
    return jnp.concatenate([held, exchange_bits(held, mesh_shape, [phase])], axis=0)


def after(values, *others):
    return lax.optimization_barrier((values, *others))[0]


def unpack_pieces(
    mesh_shape, images_all, plan, pieces, inner_out, outer_out, stage, sems, meanwhile=None
):
    codes = own_codes(mesh_shape)
    depth = stage.shape[2]
    columns = inner_out.shape[2]
    first = [0]
    for values in pieces:
        first.append(first[-1] + values.shape[0])

    def copies(number, slot):
        layer, block_of, base = plan[number]
        block = block_of(codes, slot + base)
        row_at, column_at = inner_spot(block, depth, columns)
        outer_at = pl.multiple_of(block * depth, depth)
        index = first[number] + slot
        return (
            pltpu.make_async_copy(
                stage.at[0, index],
                inner_out.at[layer, pl.ds(row_at, depth), pl.ds(column_at, LANES)],
                sems.at[0, index],
            ),
            pltpu.make_async_copy(
                stage.at[1, index], outer_out.at[layer, pl.ds(outer_at, depth), :], sems.at[1, index]
            ),
        )

    for number, values in enumerate(pieces):

        @pl.loop(0, values.shape[0])
        def _(slot):
            for kind, copy in enumerate(copies(number, slot)):
                block = values[slot, kind * depth : (kind + 1) * depth, :]
                stage[kind, first[number] + slot] = block.astype(F32) / images_all
                copy.start()

    if meanwhile is not None:
        meanwhile()
    for number, values in enumerate(pieces):

        @pl.loop(0, values.shape[0])
        def _(slot):
            for copy in copies(number, slot):
                copy.wait()


QUARTER, EIGHTH = HALF // 2, HALF // 4
SMALL_OUTS = 11


def unpack_small(mesh_shape, plan, pieces, small_rows, depth):
    codes = own_codes(mesh_shape)
    for (layer, block_of, base), values in zip(plan, pieces):
        if layer == 0:

            @pl.loop(0, values.shape[0])
            def _(slot):
                small_rows[block_of(codes, slot + base)] = values[slot, 2 * depth :, :].astype(F32)


def unpack_some(mesh_shape, images_all, plan, *refs):
    inner_out, outer_out, small_rows, stage, sems = refs[-5:]
    pieces = refs[: len(plan)]
    unpack_pieces(mesh_shape, images_all, plan, pieces, inner_out, outer_out, stage, sems)
    unpack_small(mesh_shape, plan, pieces, small_rows, stage.shape[2])


def unpack_rest(
    mesh_shape, images_all, other_late, inner_in, outer_in, small_in,
    inner_out, outer_out, small_rows, *small_outs_and_rest,
):
    small_outs, rest = small_outs_and_rest[:SMALL_OUTS], small_outs_and_rest[SMALL_OUTS:]
    buffers, (stage, rest_rows, sems, small_sems) = rest[:SMALL_OUTS], rest[SMALL_OUTS:]
    (
        weight_out, aff_scale_out, aff_shift_out, cross_bias_out, cross_scale_out,
        mixer_aff_scale_out, mixer_aff_shift_out, inner_bias_out, outer_bias_out,
        mixer_scale_out, magnitudes_out,
    ) = buffers
    small_copies = [
        pltpu.make_async_copy(buffer, out, small_sems.at[number])
        for number, (buffer, out) in enumerate(zip(buffers, small_outs))
    ]
    patches, layers, _ = weight_out.shape
    plan, pieces = ((0, sent_block, QUARTER + EIGHTH),), (other_late,)

    def small_gradients():
        unpack_small(mesh_shape, plan, pieces, small_rows, stage.shape[2])
        groups = -(-patches // SMALL_ROWS)
        weights = (small_rows[0:groups] / images_all).reshape(groups * SMALL_ROWS, LANES)[0:patches]
        parts = VECTOR_ROWS // SMALL_ROWS
        lane = lax.broadcasted_iota(jnp.int32, (patches, 128), 1)
        for layer in range(layers):
            row = slice(layer, layer + 1)
            at = groups + layer * parts
            vectors = (small_rows[at : at + parts] / images_all).reshape(VECTOR_ROWS, LANES)
            rest_rows[...] = jnp.zeros_like(rest_rows)
            rest_rows[64 : 64 + SMALL_ROWS, :] = vectors[CROSS_REST:, 0:256]
            rest = jnp.transpose(rest_rows[...])[0:patches]
            shared = weights[:, 256:384]
            if layer:
                shared = pltpu.roll(shared, 64, 1)
            last = jnp.where(lane < 64, shared, rest)
            weight_out[:, layer, 0:128] = weights[:, layer * 128 : (layer + 1) * 128]
            weight_out[:, layer, 128:] = last[:, 0 : patches - 128]
            for out, index in (
                (aff_scale_out, CROSS_AFF_SCALE),
                (aff_shift_out, CROSS_AFF_SHIFT),
                (cross_scale_out, CROSS_SCALE),
                (mixer_aff_scale_out, MIXER_AFF_SCALE),
                (mixer_aff_shift_out, MIXER_AFF_SHIFT),
                (outer_bias_out, MIXER_OUT_BIAS),
                (mixer_scale_out, MIXER_SCALE),
            ):
                out[row, :] = vectors[index : index + 1]
            cross_bias_out[row, :] = vectors[CROSS_BIAS : CROSS_BIAS + 1, 0:patches]
            for piece in range(SQUARES - MIXER_IN_BIAS):
                index = MIXER_IN_BIAS + piece
                inner_bias_out[row, piece * LANES : (piece + 1) * LANES] = vectors[index : index + 1]
            squares = vectors[SQUARES : SQUARES + 4] / (patches * LANES)
            means = jnp.sqrt(jnp.sum(squares, axis=1, keepdims=True))
            for kind in range(2):
                for which in range(2):
                    index = 2 * kind + which
                    magnitudes_out[layer, kind : kind + 1, which : which + 1] = means[index : index + 1]
        for copy in small_copies:
            copy.start()

    unpack_pieces(
        mesh_shape, images_all, plan, pieces, inner_out, outer_out, stage, sems, small_gradients
    )
    for copy in small_copies:
        copy.wait()


def call(kernel, name, args, outs, scratch, in_specs=None, out_specs=None, aliases=None, us=1):
    return pl.pallas_call(
        kernel,
        out_shape=outs,
        in_specs=[VMEM] * len(args) if in_specs is None else in_specs,
        out_specs=[VMEM] * len(outs) if out_specs is None else out_specs,
        scratch_shapes=scratch,
        input_output_aliases=aliases or {},
        compiler_params=pltpu.CompilerParams(vmem_limit_bytes=VMEM_LIMIT),
        cost_estimate=pl.CostEstimate(
            flops=int(us * 1e9), bytes_accessed=int(us * 3e6), transcendentals=0
        ),
        name=name,
    )(*args)


def in_vmem(arrays):
    return [pltpu.with_memory_space_constraint(a, pltpu.VMEM) for a in arrays]


def in_hbm(arrays):
    return [pltpu.with_memory_space_constraint(a, pltpu.HBM) for a in arrays]


def on_device(
    mesh_shape,
    inputs,
    patch_masks,
    out_grad,
    cross_aff_scale,
    cross_aff_shift,
    cross_weight,
    cross_bias,
    cross_scale,
    mixer_aff_scale,
    mixer_aff_shift,
    mixer_in,
    mixer_in_bias,
    mixer_out,
    mixer_out_bias,
    mixer_scale,
):
    micros, each, patches, width = inputs.shape
    layers, _, columns = mixer_in.shape
    per = micros // mesh_shape["pipe"]
    images = per * each
    padded = -(-patches // 16) * 16
    rows = images * patches
    depth = width * columns // (BLOCKS * LANES)
    images_all = micros * each * mesh_shape["dp"]
    x_rows = jnp.transpose(inputs, (0, 2, 1, 3))
    g_rows = jnp.transpose(out_grad, (0, 2, 1, 3))
    weight_rows = jnp.transpose(cross_weight, (1, 0, 2))

    def vmem(*shape, dtype=BF):
        return pltpu.VMEM(shape, dtype)

    def hbm(*shape, dtype=F32):
        return jax.ShapeDtypeStruct(shape, dtype)

    stream = vmem(width // 128, rows, 128, dtype=F32)
    hidden = vmem(rows, columns)
    inner, outer = vmem(width, columns), vmem(columns, width)
    vectors = vmem(layers, VECTOR_ROWS, LANES, dtype=F32)
    padded_images = vmem(images, padded, width)
    local = (per, patches, each, width)
    first = call(
        functools.partial(first_kernel, mesh_shape),
        "forward",
        in_hbm((
            x_rows, patch_masks, g_rows, mixer_in, mixer_out, weight_rows, cross_bias,
            mixer_in_bias, mixer_aff_shift, cross_aff_scale, cross_aff_shift, cross_scale,
            mixer_aff_scale, mixer_out_bias, mixer_scale,
        )),
        (
            *[vmem(layers, width, dtype=F32)] * 6,
            vmem(HALF, 2 * depth, LANES),
            vmem(HALF, 2 * depth, LANES),
            vectors,
            *[stream] * 5,
            vmem(rows, width),
            hidden,
            hidden,
            vmem(rows, width),
            hidden,
            hidden,
            inner,
            outer,
            inner,
            outer,
            vmem(layers, images, padded, padded),
            vmem(images, 8, padded, dtype=F32),
            vmem(padded, 8, dtype=F32),
        ),
        [
            vmem(*local),
            vmem(per, each, layers, patches, dtype=jnp.int32),
            vmem(*local),
            vmem(patches, layers, patches),
            vmem(layers, patches, dtype=F32),
            vmem(layers, columns, dtype=F32),
            vmem(layers, width, dtype=F32),
            vmem(2, layers * patches, 128, dtype=F32),
            padded_images,
            vmem(rows, width),
            vmem(rows, width),
            inner,
            outer,
            pltpu.SemaphoreType.DMA((17,)),
        ],
        in_specs=[HBM] * 15,
        us=18,
    )
    aff_scale, aff_shift, scale, mixer_aff, result_bias, result_scale = in_vmem(first[:6])
    (
        kept1, sent1, sums, s0, s1, s2, s3, upper, low0, fired0, slope0, result0, fired1,
        hidden_grad1, inner0, outer0, inner1, outer1, kept_weight, keep, bias_columns,
    ) = first[6:]
    g2, weight_grad1, sums = call(
        functools.partial(second_kernel, each=each),
        "last_layer",
        (
            *in_vmem((
                s2, s3, upper, hidden_grad1, inner1, kept_weight, keep, bias_columns, sums,
            )),
            aff_scale, aff_shift, scale, mixer_aff,
        ),
        (stream, vmem(256, 256, dtype=F32), vectors),
        [stream, padded_images, padded_images],
        us=4,
    )
    main1 = [kept1, exchange_bits(sent1, mesh_shape, [0])]
    leaving1, main1 = halve(main1, HALF, mesh_shape, 1)
    g2 = after(g2, leaving1)
    halves = vmem(HALF, 2 * depth, LANES)
    kept0, sent0, g1, sums, leaving = call(
        functools.partial(third_kernel, mesh_shape),
        "first_feed_forward",
        (
            *in_vmem((
                s1, g2, low0, fired0, slope0, inner0, outer0, s3, upper, fired1, outer1, sums,
            )),
            mixer_aff, result_bias, result_scale,
        ),
        (halves, halves, stream, vectors, stream),
        [hidden, vmem(rows, width), inner, outer],
        us=9,
    )
    sent0, sums = lax.optimization_barrier((sent0, sums, main1[-1]))[:2]
    main0 = [kept0, exchange_bits(sent0, mesh_shape, [0])]
    leaving1, main1 = halve(main1, HALF // 2, mesh_shape, 2)
    sums = after(sums, leaving1)
    halves = vmem(HALF, SMALL_ROWS, LANES)
    input_grad, output, kept_small, sent_small = call(
        functools.partial(fourth_kernel, mesh_shape),
        "first_cross",
        (
            *in_vmem((
                s0, g1, kept_weight, keep, bias_columns, weight_grad1, sums, g2, result0, leaving,
            )),
            aff_scale, aff_shift, scale,
        ),
        (hbm(*local, dtype=BF), hbm(*local, dtype=BF), halves, halves),
        [
            stream,
            vmem(256, 256, dtype=F32),
            vectors,
            vmem(BLOCKS, SMALL_ROWS, LANES),
            padded_images,
            padded_images,
        ],
        us=5,
    )
    small = [kept_small, exchange_bits(sent_small, mesh_shape, [0])]
    _, main0 = halve(main0, HALF, mesh_shape, 1)
    _, small = halve(small, HALF, mesh_shape, 1)
    own1 = sum_last([main1], send_last([main1], mesh_shape, (1, 3, 2))[1], mesh_shape)
    main0[-1], small[-1], own1 = lax.optimization_barrier((main0[-1], small[-1], own1))
    width0 = HALF // 2
    terms0 = [[t[:width0] for t in main0], [t[:width0] for t in small]]
    _, terms0 = halve_all(terms0, width0, mesh_shape, 2)
    peers1 = gather_last(own1, mesh_shape, (1, 2, 3))
    leaving0, arrived0 = send_last(terms0, mesh_shape, (1, 3, 2))
    four1 = join(own1, after(peers1, leaving0))
    own0 = sum_last(terms0, arrived0, mesh_shape)
    more1 = exchange_bits(four1, mesh_shape, [2])
    late1 = exchange_bits(four1, mesh_shape, [1])
    peers0 = gather_last(own0, mesh_shape, (3, 1, 2))
    more1 = after(more1, own0)
    latest1 = exchange_bits(more1, mesh_shape, [1])
    four0 = join(own0, after(peers0, more1, late1))
    held1 = jnp.concatenate([four1, more1], axis=0)
    other_held1 = exchange_bits(held1, mesh_shape, [0])
    more0 = exchange_bits(four0, mesh_shape, [2])
    late0 = exchange_bits(four0, mesh_shape, [1])
    inner_out, outer_out = hbm(layers, width, columns), hbm(layers, columns, width)

    def staging(blocks):
        return [
            vmem(2, blocks, depth, LANES, dtype=F32),
            pltpu.SemaphoreType.DMA((2, blocks)),
        ]

    small_rows = vmem(BLOCKS, SMALL_ROWS, LANES, dtype=F32)

    def unpack(name, plan, pieces, grads=()):
        count, blocks = len(pieces), sum(p.shape[0] for p in pieces)
        return call(
            functools.partial(unpack_some, mesh_shape, images_all, plan),
            name,
            (*in_vmem(pieces), *grads[:2], *in_vmem(grads[2:])),
            (inner_out, outer_out, small_rows),
            staging(blocks),
            in_specs=[VMEM] * count + ([HBM, HBM, VMEM] if grads else []),
            out_specs=[HBM] * 2 + [VMEM],
            aliases={count + number: number for number in range(len(grads))},
            us=blocks / 8,
        )

    more0, late0 = lax.optimization_barrier((more0, late0))
    late1, latest1 = after((late1, latest1), more0)
    latest0 = exchange_bits(more0, mesh_shape, [1])
    late1 = jnp.concatenate([late1, latest1], axis=0)
    other_late1 = exchange_bits(late1, mesh_shape, [0])
    held0 = jnp.concatenate([four0, more0], axis=0)
    other_held0 = exchange_bits(held0, mesh_shape, [0])
    other_late0 = exchange_bits(late0, mesh_shape, [0])
    grads = unpack(
        "unpack_kept",
        (
            (1, kept_block, 0),
            (1, sent_block, 0),
            (1, kept_block, QUARTER),
            (0, kept_block, 0),
            (0, kept_block, QUARTER),
        ),
        (held1, other_held1, late1, held0, late0),
    )
    grads = unpack(
        "unpack_others",
        ((1, sent_block, QUARTER), (0, sent_block, 0), (0, sent_block, QUARTER)),
        (other_late1, other_held0, other_late0),
        grads,
    )
    latest0, grads = lax.optimization_barrier((latest0, grads))
    other_latest0 = exchange_bits(latest0, mesh_shape, [0])
    grads = unpack("unpack_latest", ((0, kept_block, QUARTER + EIGHTH),), (latest0,), grads)
    row = (layers, width)
    small_shapes = (
        (patches, layers, patches), row, row, (layers, patches), row, row, row,
        (layers, columns), row, row, (layers, 2, 2),
    )
    stage, sems = staging(EIGHTH)
    (
        inner_grad, outer_grad, _, weight_grad, aff_scale_grad, aff_shift_grad, bias_grad,
        scale_grad, mixer_aff_scale_grad, mixer_aff_shift_grad, inner_bias_grad,
        outer_bias_grad, mixer_scale_grad, magnitudes,
    ) = call(
        functools.partial(unpack_rest, mesh_shape, images_all),
        "unpack_rest",
        (*in_vmem((other_latest0,)), *grads[:2], *in_vmem(grads[2:])),
        (inner_out, outer_out, small_rows, *(hbm(*shape) for shape in small_shapes)),
        [
            *(vmem(*shape, dtype=F32) for shape in small_shapes),
            stage,
            vmem(128, 256, dtype=F32),
            sems,
            pltpu.SemaphoreType.DMA((SMALL_OUTS,)),
        ],
        in_specs=[VMEM] + [HBM] * 2 + [VMEM],
        out_specs=[HBM] * 2 + [VMEM] + [HBM] * SMALL_OUTS,
        aliases={1: 0, 2: 1, 3: 2},
        us=2,
    )
    return (
        jnp.transpose(output, (0, 2, 1, 3)),
        jnp.transpose(input_grad, (0, 2, 1, 3)),
        aff_scale_grad,
        aff_shift_grad,
        jnp.transpose(weight_grad, (1, 0, 2)),
        bias_grad,
        scale_grad,
        mixer_aff_scale_grad,
        mixer_aff_shift_grad,
        inner_grad,
        inner_bias_grad,
        outer_grad,
        outer_bias_grad,
        mixer_scale_grad,
        magnitudes,
    )


def solution(mesh):
    split = P(None, "dp", None, None)
    owned = P("pipe", "dp", None, None)
    return jax.shard_map(
        functools.partial(on_device, dict(mesh.shape)),
        mesh=mesh,
        in_specs=(split,) * 3 + (P(),) * 12,
        out_specs=(owned,) * 2 + (P(),) * 13,
        check_vma=False,
    )
```

```python
import functools

import jax
import jax.numpy as jnp
from jax import lax
from jax.experimental import pallas as pl
from jax.experimental.pallas import tpu as pltpu
from jax.sharding import PartitionSpec as P

SQRT_HALF = 0.7071067811865476
INV_ROOT_TAU = 0.3989422804014327
AXES = ("dp", "pipe")
BLOCKS = 32
HALF = BLOCKS // 2
SCATTERED = 5
LANES = 384
SMALL_ROWS = 8
VECTOR_ROWS = 24
BF = jnp.bfloat16
F32 = jnp.float32
VMEM = pl.BlockSpec(memory_space=pltpu.VMEM)
HBM = pl.BlockSpec(memory_space=pltpu.HBM)
VMEM_LIMIT = 20 * 2**20

CROSS_AFF_SCALE, CROSS_AFF_SHIFT, CROSS_SCALE, CROSS_BIAS = 0, 1, 2, 3
MIXER_AFF_SCALE, MIXER_AFF_SHIFT, MIXER_OUT_BIAS, MIXER_SCALE = 4, 5, 6, 7
MIXER_IN_BIAS = 8
SQUARES = 12
CROSS_REST = 16


def dot(a, b, a_dim=1, b_dim=0):
    return lax.dot_general(
        a, b, (((a_dim,), (b_dim,)), ((), ())), preferred_element_type=F32
    )


def row_sum(values):
    return jnp.sum(values, axis=0, keepdims=True)


def phase_bits(mesh_shape):
    pipe_bits = [1 << b for b in range(mesh_shape["pipe"].bit_length() - 1)]
    dp_bits = [mesh_shape["pipe"] << b for b in range(mesh_shape["dp"].bit_length() - 1)]
    even = [pipe_bits[0], *pipe_bits[1:], *dp_bits]
    odd = list(even)
    odd[1], odd[2] = even[2], even[1]
    return even, odd


def block_code(mesh_shape, place):
    even, odd = phase_bits(mesh_shape)
    odd_place = place & 1
    code = jnp.int32(0)
    for even_bit, odd_bit in zip(even[:SCATTERED], odd[:SCATTERED]):
        bit = jnp.where(odd_place == 1, (place & odd_bit) != 0, (place & even_bit) != 0)
        code = 2 * code + bit.astype(jnp.int32)
    return code


def own_codes(mesh_shape):
    place = lax.axis_index("dp") * mesh_shape["pipe"] + lax.axis_index("pipe")
    return block_code(mesh_shape, place), block_code(mesh_shape, place ^ 1)


def kept_block(codes, slot):
    return codes[0] ^ slot


def sent_block(codes, slot):
    return codes[1] ^ slot


def inner_spot(block, rows, columns):
    across = columns // LANES
    row_at = pl.multiple_of((block // across) * rows, rows)
    return row_at, pl.multiple_of((block % across) * LANES, LANES)


def pack_halves(codes, block_at, kept_ref, sent_ref):
    @pl.loop(0, HALF, unroll=4)
    def _(slot):
        for block, out_ref in ((sent_block(codes, slot), sent_ref), (kept_block(codes, slot), kept_ref)):
            at = 0
            for piece in block_at(block):
                out_ref[slot, at : at + piece.shape[0], :] = piece
                at += piece.shape[0]


def pack_products(codes, inner_ref, outer_ref, kept_ref, sent_ref):
    depth = outer_ref.shape[0] // BLOCKS

    def block_at(block):
        row_at, column_at = inner_spot(block, depth, inner_ref.shape[1])
        outer_at = pl.multiple_of(block * depth, depth)
        return (
            inner_ref[pl.ds(row_at, depth), pl.ds(column_at, LANES)],
            outer_ref[pl.ds(outer_at, depth), :],
        )

    pack_halves(codes, block_at, kept_ref, sent_ref)


def read(ref, rows):
    return jnp.concatenate([ref[plane, rows, :] for plane in range(ref.shape[0])], axis=1)


def write(ref, rows, values):
    for plane in range(ref.shape[0]):
        ref[plane, rows, :] = values[:, plane * 128 : (plane + 1) * 128]


def rounded(values):
    return values.astype(BF).astype(F32)


def spread_rows(source_ref, target_ref):
    parts, patches, each, _ = source_ref.shape
    for part in range(parts):
        for patch in range(patches):
            base = (part * patches + patch) * each
            write(target_ref, slice(base, base + each), source_ref[part, patch].astype(F32))


def gather_rows(source_ref, target_ref):
    parts, patches, each, _ = target_ref.shape
    for part in range(parts):
        for patch in range(patches):
            base = (part * patches + patch) * each
            target_ref[part, patch] = read(source_ref, slice(base, base + each)).astype(BF)


def image_rows(image, patches, each):
    return pl.ds((image // each) * patches * each + image % each, patches, stride=each)


def row_tiles(rows):
    tile = max(t for t in range(16, 209, 16) if rows % t == 0)
    return [slice(at, at + tile) for at in range(0, rows, tile)]


def row_halves(rows):
    middle = -(-rows // 32) * 16
    return [slice(0, middle), slice(middle, rows)]


def cross_setup(mask_ref, weight_ref, bias_ref, kept_ref, keep_ref, bias_columns_ref, rows_ref):
    patches, layers, _ = weight_ref.shape
    padded = kept_ref.shape[2]
    for patch in range(patches):
        base = patch * layers
        weight = weight_ref[patch].astype(F32)
        rows_ref[0, base : base + layers, :] = weight[:, 0:128]
        rows_ref[1, base : base + layers, 0 : patches - 128] = weight[:, 128:]
    keep_ref[...] = jnp.zeros_like(keep_ref)
    kept_ref[...] = jnp.zeros_like(kept_ref)
    for layer in range(layers):
        weight = read(rows_ref, pl.ds(layer, patches, stride=layers))[:, 0:patches]
        for image in range(mask_ref.shape[0]):
            keep_row = mask_ref[image, layer : layer + 1, :].astype(F32)
            keep_ref[image, layer : layer + 1, 0:patches] = keep_row
            kept_ref[layer, image, 0:patches, 0:patches] = (weight * keep_row).astype(BF)
    bias_rows = jnp.concatenate([bias_ref[...], jnp.zeros((8 - layers, patches), F32)], axis=0)
    bias_rows = jnp.concatenate([bias_rows, jnp.zeros((8, 256 - patches), F32)], axis=1)
    bias_columns_ref[...] = jnp.transpose(bias_rows)[0:padded]


def cross_forward(
    layer, source_ref, target_ref, vectors_ref, kept_ref, bias_ref,
    aff_scale_ref, aff_shift_ref, scale_ref, low_ref, patches, each,
):
    aff_scale = aff_scale_ref[layer : layer + 1, :]
    aff_shift = aff_shift_ref[layer : layer + 1, :]
    scale = scale_ref[layer : layer + 1, :]
    branch_squares = jnp.zeros((1, LANES), F32)
    normed_squares = jnp.zeros((1, LANES), F32)
    for image in range(kept_ref.shape[1]):
        rows = image_rows(image, patches, each)
        stream = read(source_ref, rows)
        normed = aff_scale * stream + aff_shift
        low_ref[image, 0:patches, :] = normed.astype(BF)
        mixing = dot(kept_ref[layer, image], low_ref[image])
        branch = scale * (mixing + bias_ref[:, layer : layer + 1])[0:patches]
        write(target_ref, rows, rounded(stream + branch))
        branch_squares += row_sum(branch * branch)
        normed_squares += row_sum(normed * normed)
    vectors_ref[layer, SQUARES : SQUARES + 1, :] = branch_squares
    vectors_ref[layer, SQUARES + 1 : SQUARES + 2, :] = normed_squares


def mixer_hidden(
    layer, stream_ref, low_ref, fired_ref, slope_ref, vectors_ref,
    aff_scale_ref, aff_shift_ref, inner_ref, inner_bias_ref,
):
    aff_scale = aff_scale_ref[layer : layer + 1, :]
    aff_shift = aff_shift_ref[layer : layer + 1, :]
    tiles = row_tiles(stream_ref.shape[1])
    squares = jnp.zeros((1, LANES), F32)
    for rows in tiles:
        normed = aff_scale * read(stream_ref, rows) + aff_shift
        low_ref[rows, :] = normed.astype(BF)
        squares += row_sum(normed * normed)
    vectors_ref[layer, SQUARES + 3 : SQUARES + 4, :] = squares
    step = inner_ref.shape[1] // 3
    for part in range(3):
        at = slice(part * step, (part + 1) * step)
        for rows in tiles:
            hidden = dot(low_ref[rows, :], inner_ref[:, at]) + inner_bias_ref[layer : layer + 1, at]
            normal_cdf = 0.5 * (1.0 + lax.erf(hidden * SQRT_HALF))
            density = INV_ROOT_TAU * jnp.exp(-0.5 * hidden * hidden)
            fired_ref[rows, at] = (hidden * normal_cdf).astype(BF)
            slope_ref[rows, at] = (normal_cdf + hidden * density).astype(BF)


def mixer_backward(
    layer, upper_ref, low_ref, fired_ref, slope_ref, hidden_grad_ref, scaled_ref, inner_ref,
    outer_ref, inner_grad_ref, outer_grad_ref, vectors_ref, scale_ref,
):
    scale = scale_ref[layer : layer + 1, :]
    tiles = row_tiles(upper_ref.shape[1])
    bias = jnp.zeros((1, LANES), F32)
    for rows in tiles:
        result_grad = read(upper_ref, rows) * scale
        bias += row_sum(result_grad)
        scaled_ref[rows, :] = result_grad.astype(BF)
    vectors_ref[layer, MIXER_OUT_BIAS : MIXER_OUT_BIAS + 1, :] = bias
    columns = inner_ref.shape[1]
    step = 2 * LANES
    tiles = row_halves(upper_ref.shape[1])
    for part in range(columns // step):
        at = slice(part * step, (part + 1) * step)
        outer_grad_ref[at, :] = dot(fired_ref[:, at], scaled_ref[...], 0, 0).astype(BF)
        inner_bias = jnp.zeros((1, step), F32)
        for rows in tiles:
            hidden_grad = dot(scaled_ref[rows, :], outer_ref[at, :], 1, 1) * slope_ref[
                rows, at
            ].astype(F32)
            inner_bias += row_sum(hidden_grad)
            hidden_grad_ref[rows, at] = hidden_grad.astype(BF)
        for piece in range(step // LANES):
            row = MIXER_IN_BIAS + part * (step // LANES) + piece
            vectors_ref[layer, row : row + 1, :] = inner_bias[:, piece * LANES : (piece + 1) * LANES]
        inner_grad_ref[:, at] = dot(low_ref[...], hidden_grad_ref[:, at], 0, 0).astype(BF)


def mixer_input_grad(
    layer, upper_ref, stream_ref, hidden_grad_ref, target_ref, inner_ref, vectors_ref,
    aff_scale_ref,
):
    aff_scale = aff_scale_ref[layer : layer + 1, :]
    scale_grad = jnp.zeros((1, LANES), F32)
    shift_grad = jnp.zeros((1, LANES), F32)
    for rows in row_halves(upper_ref.shape[1]):
        normed_grad = dot(hidden_grad_ref[rows, :], inner_ref[...], 1, 1)
        scale_grad += row_sum(normed_grad * read(stream_ref, rows))
        shift_grad += row_sum(normed_grad)
        write(target_ref, rows, rounded(read(upper_ref, rows) + normed_grad * aff_scale))
    vectors_ref[layer, MIXER_AFF_SCALE : MIXER_AFF_SCALE + 1, :] = scale_grad
    vectors_ref[layer, MIXER_AFF_SHIFT : MIXER_AFF_SHIFT + 1, :] = shift_grad


def cross_backward(
    layer, stream_ref, upper_ref, target_ref, weight_grad_ref, vectors_ref, kept_ref, keep_ref,
    bias_ref, aff_scale_ref, aff_shift_ref, scale_ref, low_ref, mixing_low_ref, patches, each,
):
    padded = kept_ref.shape[2]
    aff_scale = aff_scale_ref[layer : layer + 1, :]
    aff_shift = aff_shift_ref[layer : layer + 1, :]
    scale = scale_ref[layer : layer + 1, :]
    aff_scale_grad = jnp.zeros((1, LANES), F32)
    aff_shift_grad = jnp.zeros((1, LANES), F32)
    scale_grad = jnp.zeros((1, LANES), F32)
    bias_grad = jnp.zeros((8, padded), F32)
    weight_grad = jnp.zeros((padded, padded), F32)
    ones = jnp.ones((8, LANES), BF)
    for image in range(kept_ref.shape[1]):
        rows = image_rows(image, patches, each)
        stream = read(stream_ref, rows)
        upper = read(upper_ref, rows)
        low_ref[image, 0:patches, :] = (aff_scale * stream + aff_shift).astype(BF)
        mixing_low_ref[image, 0:patches, :] = (upper * scale).astype(BF)
        kept = kept_ref[layer, image]
        shifted = dot(kept, low_ref[image]) + bias_ref[:, layer : layer + 1]
        scale_grad += row_sum(upper * shifted[0:patches])
        mixing_low = mixing_low_ref[image]
        bias_grad += dot(ones, mixing_low, 1, 1)
        weight_grad += (
            dot(mixing_low, low_ref[image], 1, 1) * keep_ref[image, layer : layer + 1, :]
        )
        normed_grad = dot(kept, mixing_low, 0, 0)[0:patches]
        aff_scale_grad += row_sum(normed_grad * stream)
        aff_shift_grad += row_sum(normed_grad)
        write(target_ref, rows, rounded(upper + normed_grad * aff_scale))
    weight_grad_ref[0:padded, 0:padded] = weight_grad
    vectors_ref[layer, CROSS_AFF_SCALE : CROSS_AFF_SCALE + 1, :] = aff_scale_grad
    vectors_ref[layer, CROSS_AFF_SHIFT : CROSS_AFF_SHIFT + 1, :] = aff_shift_grad
    vectors_ref[layer, CROSS_SCALE : CROSS_SCALE + 1, :] = scale_grad
    vectors_ref[layer, CROSS_BIAS : CROSS_BIAS + 1, 0:padded] = bias_grad[0:1]


def clear_padding(*padded_refs, patches):
    for ref in padded_refs:
        images, padded, width = ref.shape
        for image in range(images):
            ref[image, padded - 16 :, :] = jnp.zeros((16, width), BF)


def first_kernel(
    mesh_shape,
    x_hbm, mask_hbm, g_hbm, inner_hbm, outer_hbm, cross_weight_hbm, cross_bias_hbm,
    inner_bias_hbm, mixer_aff_shift_hbm, *parameters_hbm_and_rest,
):
    parameters_hbm, rest = parameters_hbm_and_rest[:6], parameters_hbm_and_rest[6:]
    parameters, rest = rest[:6], rest[6:]
    cross_aff_scale, cross_aff_shift, cross_scale, mixer_aff_scale, outer_bias, mixer_scale = parameters
    (
    kept, sent, vectors, s0, s1, s2, s3, g_rows, low0, fired0, slope0, result0, fired1, slope1,
    inner0, outer0, inner1, outer1, kept_weight, keep, bias_columns,
    x_in, mask_in, g_in, cross_weight, cross_bias, inner_bias, mixer_aff_shift, weight_rows, padded_low,
    low1, scaled, inner_grad, outer_grad, sems,
    ) = rest
    _, patches, each, _ = x_in.shape
    per = x_in.shape[0]
    own = lax.axis_index("pipe") * per
    mine = pl.ds(own, per)
    groups = (
        ((cross_weight_hbm, cross_weight), (mask_hbm.at[mine], mask_in), (cross_bias_hbm, cross_bias)),
        ((x_hbm.at[mine], x_in), *zip(parameters_hbm, parameters)),
        (
            (inner_hbm.at[0], inner0),
            (inner_bias_hbm, inner_bias),
            (mixer_aff_shift_hbm, mixer_aff_shift),
        ),
        ((outer_hbm.at[0], outer0),),
        ((inner_hbm.at[1], inner1),),
        ((g_hbm.at[mine], g_in), (outer_hbm.at[1], outer1)),
    )
    arrivals, number = [], 0
    for group in groups:
        arrivals.append([])
        for source, target in group:
            copy = pltpu.make_async_copy(source, target, sems.at[number])
            copy.start()
            arrivals[-1].append(copy)
            number += 1

    def wait_for(group):
        for copy in arrivals[group]:
            copy.wait()

    vectors[...] = jnp.zeros_like(vectors)
    clear_padding(padded_low, patches=patches)
    wait_for(0)
    masks = mask_in[...].reshape((per * each,) + mask_in.shape[2:])
    cross_setup(masks, cross_weight, cross_bias, kept_weight, keep, bias_columns, weight_rows)
    wait_for(1)
    spread_rows(x_in, s0)
    cross = (kept_weight, bias_columns, cross_aff_scale, cross_aff_shift, cross_scale, padded_low)
    cross_forward(0, s0, s1, vectors, *cross, patches, each)
    wait_for(2)
    mixer = (mixer_aff_scale, mixer_aff_shift)
    mixer_hidden(0, s1, low0, fired0, slope0, vectors, *mixer, inner0, inner_bias)
    wait_for(3)
    squares = jnp.zeros((1, LANES), F32)
    for rows in row_halves(s1.shape[1]):
        result = dot(fired0[rows, :], outer0[...]) + outer_bias[0:1, :]
        result0[rows, :] = result.astype(BF)
        branch = mixer_scale[0:1, :] * result
        write(s2, rows, rounded(read(s1, rows) + branch))
        squares += row_sum(branch * branch)
    vectors[0, SQUARES + 2 : SQUARES + 3, :] = squares
    cross_forward(1, s2, s3, vectors, *cross, patches, each)
    wait_for(4)
    mixer_hidden(1, s3, low1, fired1, slope1, vectors, *mixer, inner1, inner_bias)
    wait_for(5)
    spread_rows(g_in, g_rows)
    mixer_backward(
        1, g_rows, low1, fired1, slope1, slope1, scaled, inner1, outer1, inner_grad, outer_grad,
        vectors, mixer_scale,
    )
    pack_products(own_codes(mesh_shape), inner_grad, outer_grad, kept, sent)


def second_kernel(
    s2, s3, g_rows, hidden_grad, inner1, kept_weight, keep, bias_columns, vectors_in,
    cross_aff_scale, cross_aff_shift, cross_scale, mixer_aff_scale,
    g2, weight_grad, vectors,
    g1, padded_low, padded_mixing, *, each,
):
    patches = s2.shape[1] // padded_low.shape[0]
    vectors[...] = vectors_in[...]
    clear_padding(padded_low, padded_mixing, patches=patches)
    mixer_input_grad(1, g_rows, s3, hidden_grad, g1, inner1, vectors, mixer_aff_scale)
    cross_backward(
        1, s2, g1, g2, weight_grad, vectors, kept_weight, keep, bias_columns,
        cross_aff_scale, cross_aff_shift, cross_scale, padded_low, padded_mixing, patches, each,
    )


def third_kernel(
    mesh_shape,
    s1, g2, low0, fired0, slope0, inner0, outer0, s3, g_rows, fired1, outer1, vectors_in,
    mixer_aff_scale, outer_bias, mixer_scale,
    kept, sent, g1, vectors, leaving,
    hidden_grad, scaled, inner_grad, outer_grad,
):
    vectors[...] = vectors_in[...]
    mixer_backward(
        0, g2, low0, fired0, slope0, hidden_grad, scaled, inner0, outer0, inner_grad, outer_grad,
        vectors, mixer_scale,
    )
    pack_products(own_codes(mesh_shape), inner_grad, outer_grad, kept, sent)
    mixer_input_grad(0, g2, s1, hidden_grad, g1, inner0, vectors, mixer_aff_scale)
    squares = jnp.zeros((1, LANES), F32)
    scale_grad = jnp.zeros((1, LANES), F32)
    for rows in row_halves(s3.shape[1]):
        result = dot(fired1[rows, :], outer1[...]) + outer_bias[1:2, :]
        scale_grad += row_sum(read(g_rows, rows) * result)
        branch = mixer_scale[1:2, :] * result
        write(leaving, rows, read(s3, rows) + branch)
        squares += row_sum(branch * branch)
    vectors[1, SQUARES + 2 : SQUARES + 3, :] = squares
    vectors[1, MIXER_SCALE : MIXER_SCALE + 1, :] = scale_grad


def pack_small(weight_grads, vectors_ref, small_ref, patches):
    groups = -(-patches // SMALL_ROWS)
    rows = groups * SMALL_ROWS
    first, second = (grad[0:rows, 128:256] for grad in weight_grads)
    lane = lax.broadcasted_iota(jnp.int32, (rows, 128), 1)
    shared = jnp.where(lane < 64, first, pltpu.roll(second, 64, 1))
    blocks = [grad[0:rows, 0:128] for grad in weight_grads] + [shared]
    small_ref[...] = jnp.zeros_like(small_ref)
    for part, block in enumerate(blocks):
        small_ref[0:groups, :, part * 128 : (part + 1) * 128] = block.astype(BF).reshape(
            groups, SMALL_ROWS, 128
        )
    for layer, grad in enumerate(weight_grads):
        rest = jnp.transpose(grad[:, 128:256])[64 : 64 + SMALL_ROWS]
        vectors_ref[layer, CROSS_REST : CROSS_REST + SMALL_ROWS, 0:256] = rest
        for piece in range(VECTOR_ROWS // SMALL_ROWS):
            at = groups + layer * (VECTOR_ROWS // SMALL_ROWS) + piece
            small_ref[at] = vectors_ref[
                layer, piece * SMALL_ROWS : (piece + 1) * SMALL_ROWS, :
            ].astype(BF)


def fourth_kernel(
    mesh_shape,
    s0, g1, kept_weight, keep, bias_columns, weight_grad1, vectors_in, g2, result0, leaving,
    cross_aff_scale, cross_aff_shift, cross_scale,
    input_grad, output, kept, sent,
    g0, weight_grad0, vectors, small, padded_low, padded_mixing,
):
    _, patches, each, _ = input_grad.shape
    vectors[...] = vectors_in[...]
    clear_padding(padded_low, padded_mixing, patches=patches)
    cross_backward(
        0, s0, g1, g0, weight_grad0, vectors, kept_weight, keep, bias_columns,
        cross_aff_scale, cross_aff_shift, cross_scale, padded_low, padded_mixing, patches, each,
    )
    scale_grad = jnp.zeros((1, LANES), F32)
    for rows in row_tiles(g2.shape[1]):
        scale_grad += row_sum(read(g2, rows) * result0[rows, :].astype(F32))
    vectors[0, MIXER_SCALE : MIXER_SCALE + 1, :] = scale_grad
    pack_small((weight_grad0, weight_grad1), vectors, small, patches)
    pack_halves(own_codes(mesh_shape), lambda block: (small[block],), kept, sent)
    gather_rows(g0, input_grad)
    gather_rows(leaving, output)


def exchange_bits(values, mesh_shape, phases):
    even, odd = phase_bits(mesh_shape)
    places = range(mesh_shape["dp"] * mesh_shape["pipe"])

    def partner(place):
        for phase in phases:
            place ^= (odd if place & 1 else even)[phase]
        return place

    return lax.ppermute(values, AXES, [(i, partner(i)) for i in places])


def across(slot):
    return [phase for phase, bit in ((SCATTERED - 2, 2), (SCATTERED - 1, 1)) if slot & bit]


def part_sum(terms, start, stop):
    return sum(t[start:stop].astype(F32) for t in terms)


def joint_sum(families, start, stop):
    sums = [part_sum(terms, start, stop).astype(BF) for terms in families]
    return sums[0] if len(sums) == 1 else jnp.concatenate(sums, axis=1)


def halve(terms, width, mesh_shape, phase):
    half = width // 2
    leaving = part_sum(terms, half, width).astype(BF)
    return leaving, terms + [exchange_bits(leaving, mesh_shape, [phase])]


def halve_all(families, width, mesh_shape, phase):
    half = width // 2
    arrived = exchange_bits(joint_sum(families, half, width), mesh_shape, [phase])
    grown, at = [], 0
    for terms in families:
        rows = terms[0].shape[1]
        grown.append(terms + [arrived[:, at : at + rows]])
        at += rows
    return arrived, grown


def send_last(families, mesh_shape, slots):
    leaving = [joint_sum(families, slot, slot + 1) for slot in slots]
    return leaving, [
        exchange_bits(block, mesh_shape, across(slot)) for slot, block in zip(slots, leaving)
    ]


def sum_last(families, arrived, mesh_shape):
    sums = [part_sum(terms, 0, 1) for terms in families]
    total = sums[0] if len(sums) == 1 else jnp.concatenate(sums, axis=1)
    total = total + sum(a.astype(F32) for a in arrived)
    for phase in range(SCATTERED, len(phase_bits(mesh_shape)[0])):
        total = total.astype(BF)
        total = total.astype(F32) + exchange_bits(total, mesh_shape, [phase]).astype(F32)
    return total.astype(BF)


def gather_last(own, mesh_shape, slots):
    return {slot: exchange_bits(own, mesh_shape, across(slot)) for slot in slots}


def join(own, arrived):
    return jnp.concatenate([own, arrived[1], arrived[2], arrived[3]], axis=0)


def double(held, mesh_shape, phase):
    return jnp.concatenate([held, exchange_bits(held, mesh_shape, [phase])], axis=0)


def after(values, *others):
    return lax.optimization_barrier((values, *others))[0]


def unpack_pieces(
    mesh_shape, images_all, plan, pieces, inner_out, outer_out, stage, sems, meanwhile=None
):
    codes = own_codes(mesh_shape)
    depth = stage.shape[2]
    columns = inner_out.shape[2]
    first = [0]
    for values in pieces:
        first.append(first[-1] + values.shape[0])

    def copies(number, slot):
        layer, block_of, base = plan[number]
        block = block_of(codes, slot + base)
        row_at, column_at = inner_spot(block, depth, columns)
        outer_at = pl.multiple_of(block * depth, depth)
        index = first[number] + slot
        return (
            pltpu.make_async_copy(
                stage.at[0, index],
                inner_out.at[layer, pl.ds(row_at, depth), pl.ds(column_at, LANES)],
                sems.at[0, index],
            ),
            pltpu.make_async_copy(
                stage.at[1, index], outer_out.at[layer, pl.ds(outer_at, depth), :], sems.at[1, index]
            ),
        )

    for number, values in enumerate(pieces):

        @pl.loop(0, values.shape[0])
        def _(slot):
            for kind, copy in enumerate(copies(number, slot)):
                block = values[slot, kind * depth : (kind + 1) * depth, :]
                stage[kind, first[number] + slot] = block.astype(F32) / images_all
                copy.start()

    if meanwhile is not None:
        meanwhile()
    for number, values in enumerate(pieces):

        @pl.loop(0, values.shape[0])
        def _(slot):
            for copy in copies(number, slot):
                copy.wait()


QUARTER, EIGHTH = HALF // 2, HALF // 4
SMALL_OUTS = 11


def unpack_small(mesh_shape, plan, pieces, small_rows, depth):
    codes = own_codes(mesh_shape)
    for (layer, block_of, base), values in zip(plan, pieces):
        if layer == 0:

            @pl.loop(0, values.shape[0])
            def _(slot):
                small_rows[block_of(codes, slot + base)] = values[slot, 2 * depth :, :].astype(F32)


def unpack_some(mesh_shape, images_all, plan, *refs):
    inner_out, outer_out, small_rows, stage, sems = refs[-5:]
    pieces = refs[: len(plan)]
    unpack_pieces(mesh_shape, images_all, plan, pieces, inner_out, outer_out, stage, sems)
    unpack_small(mesh_shape, plan, pieces, small_rows, stage.shape[2])


def unpack_rest(
    mesh_shape, images_all, other_late, inner_in, outer_in, small_in,
    inner_out, outer_out, small_rows, *small_outs_and_rest,
):
    small_outs, rest = small_outs_and_rest[:SMALL_OUTS], small_outs_and_rest[SMALL_OUTS:]
    buffers, (stage, rest_rows, sems, small_sems) = rest[:SMALL_OUTS], rest[SMALL_OUTS:]
    (
        weight_out, aff_scale_out, aff_shift_out, cross_bias_out, cross_scale_out,
        mixer_aff_scale_out, mixer_aff_shift_out, inner_bias_out, outer_bias_out,
        mixer_scale_out, magnitudes_out,
    ) = buffers
    small_copies = [
        pltpu.make_async_copy(buffer, out, small_sems.at[number])
        for number, (buffer, out) in enumerate(zip(buffers, small_outs))
    ]
    patches, layers, _ = weight_out.shape
    plan, pieces = ((0, sent_block, QUARTER + EIGHTH),), (other_late,)

    def small_gradients():
        unpack_small(mesh_shape, plan, pieces, small_rows, stage.shape[2])
        groups = -(-patches // SMALL_ROWS)
        weights = (small_rows[0:groups] / images_all).reshape(groups * SMALL_ROWS, LANES)[0:patches]
        parts = VECTOR_ROWS // SMALL_ROWS
        lane = lax.broadcasted_iota(jnp.int32, (patches, 128), 1)
        for layer in range(layers):
            row = slice(layer, layer + 1)
            at = groups + layer * parts
            vectors = (small_rows[at : at + parts] / images_all).reshape(VECTOR_ROWS, LANES)
            rest_rows[...] = jnp.zeros_like(rest_rows)
            rest_rows[64 : 64 + SMALL_ROWS, :] = vectors[CROSS_REST:, 0:256]
            rest = jnp.transpose(rest_rows[...])[0:patches]
            shared = weights[:, 256:384]
            if layer:
                shared = pltpu.roll(shared, 64, 1)
            last = jnp.where(lane < 64, shared, rest)
            weight_out[:, layer, 0:128] = weights[:, layer * 128 : (layer + 1) * 128]
            weight_out[:, layer, 128:] = last[:, 0 : patches - 128]
            for out, index in (
                (aff_scale_out, CROSS_AFF_SCALE),
                (aff_shift_out, CROSS_AFF_SHIFT),
                (cross_scale_out, CROSS_SCALE),
                (mixer_aff_scale_out, MIXER_AFF_SCALE),
                (mixer_aff_shift_out, MIXER_AFF_SHIFT),
                (outer_bias_out, MIXER_OUT_BIAS),
                (mixer_scale_out, MIXER_SCALE),
            ):
                out[row, :] = vectors[index : index + 1]
            cross_bias_out[row, :] = vectors[CROSS_BIAS : CROSS_BIAS + 1, 0:patches]
            for piece in range(SQUARES - MIXER_IN_BIAS):
                index = MIXER_IN_BIAS + piece
                inner_bias_out[row, piece * LANES : (piece + 1) * LANES] = vectors[index : index + 1]
            squares = vectors[SQUARES : SQUARES + 4] / (patches * LANES)
            means = jnp.sqrt(jnp.sum(squares, axis=1, keepdims=True))
            for kind in range(2):
                for which in range(2):
                    index = 2 * kind + which
                    magnitudes_out[layer, kind : kind + 1, which : which + 1] = means[index : index + 1]
        for copy in small_copies:
            copy.start()

    unpack_pieces(
        mesh_shape, images_all, plan, pieces, inner_out, outer_out, stage, sems, small_gradients
    )
    for copy in small_copies:
        copy.wait()


def call(kernel, name, args, outs, scratch, in_specs=None, out_specs=None, aliases=None, us=1):
    return pl.pallas_call(
        kernel,
        out_shape=outs,
        in_specs=[VMEM] * len(args) if in_specs is None else in_specs,
        out_specs=[VMEM] * len(outs) if out_specs is None else out_specs,
        scratch_shapes=scratch,
        input_output_aliases=aliases or {},
        compiler_params=pltpu.CompilerParams(vmem_limit_bytes=VMEM_LIMIT),
        cost_estimate=pl.CostEstimate(
            flops=int(us * 1e9), bytes_accessed=int(us * 3e6), transcendentals=0
        ),
        name=name,
    )(*args)


def in_vmem(arrays):
    return [pltpu.with_memory_space_constraint(a, pltpu.VMEM) for a in arrays]


def in_hbm(arrays):
    return [pltpu.with_memory_space_constraint(a, pltpu.HBM) for a in arrays]


def on_device(
    mesh_shape,
    inputs,
    patch_masks,
    out_grad,
    cross_aff_scale,
    cross_aff_shift,
    cross_weight,
    cross_bias,
    cross_scale,
    mixer_aff_scale,
    mixer_aff_shift,
    mixer_in,
    mixer_in_bias,
    mixer_out,
    mixer_out_bias,
    mixer_scale,
):
    micros, each, patches, width = inputs.shape
    layers, _, columns = mixer_in.shape
    per = micros // mesh_shape["pipe"]
    images = per * each
    padded = -(-patches // 16) * 16
    rows = images * patches
    depth = width * columns // (BLOCKS * LANES)
    images_all = micros * each * mesh_shape["dp"]
    x_rows = jnp.transpose(inputs, (0, 2, 1, 3))
    g_rows = jnp.transpose(out_grad, (0, 2, 1, 3))
    weight_rows = jnp.transpose(cross_weight, (1, 0, 2))

    def vmem(*shape, dtype=BF):
        return pltpu.VMEM(shape, dtype)

    def hbm(*shape, dtype=F32):
        return jax.ShapeDtypeStruct(shape, dtype)

    stream = vmem(width // 128, rows, 128, dtype=F32)
    hidden = vmem(rows, columns)
    inner, outer = vmem(width, columns), vmem(columns, width)
    vectors = vmem(layers, VECTOR_ROWS, LANES, dtype=F32)
    padded_images = vmem(images, padded, width)
    local = (per, patches, each, width)
    first = call(
        functools.partial(first_kernel, mesh_shape),
        "forward",
        in_hbm((
            x_rows, patch_masks, g_rows, mixer_in, mixer_out, weight_rows, cross_bias,
            mixer_in_bias, mixer_aff_shift, cross_aff_scale, cross_aff_shift, cross_scale,
            mixer_aff_scale, mixer_out_bias, mixer_scale,
        )),
        (
            *[vmem(layers, width, dtype=F32)] * 6,
            vmem(HALF, 2 * depth, LANES),
            vmem(HALF, 2 * depth, LANES),
            vectors,
            *[stream] * 5,
            vmem(rows, width),
            hidden,
            hidden,
            vmem(rows, width),
            hidden,
            hidden,
            inner,
            outer,
            inner,
            outer,
            vmem(layers, images, padded, padded),
            vmem(images, 8, padded, dtype=F32),
            vmem(padded, 8, dtype=F32),
        ),
        [
            vmem(*local),
            vmem(per, each, layers, patches, dtype=jnp.int32),
            vmem(*local),
            vmem(patches, layers, patches),
            vmem(layers, patches, dtype=F32),
            vmem(layers, columns, dtype=F32),
            vmem(layers, width, dtype=F32),
            vmem(2, layers * patches, 128, dtype=F32),
            padded_images,
            vmem(rows, width),
            vmem(rows, width),
            inner,
            outer,
            pltpu.SemaphoreType.DMA((17,)),
        ],
        in_specs=[HBM] * 15,
        us=18,
    )
    aff_scale, aff_shift, scale, mixer_aff, result_bias, result_scale = in_vmem(first[:6])
    (
        kept1, sent1, sums, s0, s1, s2, s3, upper, low0, fired0, slope0, result0, fired1,
        hidden_grad1, inner0, outer0, inner1, outer1, kept_weight, keep, bias_columns,
    ) = first[6:]
    g2, weight_grad1, sums = call(
        functools.partial(second_kernel, each=each),
        "last_layer",
        (
            *in_vmem((
                s2, s3, upper, hidden_grad1, inner1, kept_weight, keep, bias_columns, sums,
            )),
            aff_scale, aff_shift, scale, mixer_aff,
        ),
        (stream, vmem(256, 256, dtype=F32), vectors),
        [stream, padded_images, padded_images],
        us=4,
    )
    main1 = [kept1, exchange_bits(sent1, mesh_shape, [0])]
    leaving1, main1 = halve(main1, HALF, mesh_shape, 1)
    g2 = after(g2, leaving1)
    halves = vmem(HALF, 2 * depth, LANES)
    kept0, sent0, g1, sums, leaving = call(
        functools.partial(third_kernel, mesh_shape),
        "first_feed_forward",
        (
            *in_vmem((
                s1, g2, low0, fired0, slope0, inner0, outer0, s3, upper, fired1, outer1, sums,
            )),
            mixer_aff, result_bias, result_scale,
        ),
        (halves, halves, stream, vectors, stream),
        [hidden, vmem(rows, width), inner, outer],
        us=9,
    )
    sent0, sums = lax.optimization_barrier((sent0, sums, main1[-1]))[:2]
    main0 = [kept0, exchange_bits(sent0, mesh_shape, [0])]
    leaving1, main1 = halve(main1, HALF // 2, mesh_shape, 2)
    sums = after(sums, leaving1)
    halves = vmem(HALF, SMALL_ROWS, LANES)
    input_grad, output, kept_small, sent_small = call(
        functools.partial(fourth_kernel, mesh_shape),
        "first_cross",
        (
            *in_vmem((
                s0, g1, kept_weight, keep, bias_columns, weight_grad1, sums, g2, result0, leaving,
            )),
            aff_scale, aff_shift, scale,
        ),
        (hbm(*local, dtype=BF), hbm(*local, dtype=BF), halves, halves),
        [
            stream,
            vmem(256, 256, dtype=F32),
            vectors,
            vmem(BLOCKS, SMALL_ROWS, LANES),
            padded_images,
            padded_images,
        ],
        us=5,
    )
    small = [kept_small, exchange_bits(sent_small, mesh_shape, [0])]
    _, main0 = halve(main0, HALF, mesh_shape, 1)
    _, small = halve(small, HALF, mesh_shape, 1)
    own1 = sum_last([main1], send_last([main1], mesh_shape, (1, 3, 2))[1], mesh_shape)
    main0[-1], small[-1], own1 = lax.optimization_barrier((main0[-1], small[-1], own1))
    width0 = HALF // 2
    terms0 = [[t[:width0] for t in main0], [t[:width0] for t in small]]
    _, terms0 = halve_all(terms0, width0, mesh_shape, 2)
    peers1 = gather_last(own1, mesh_shape, (1, 2, 3))
    leaving0, arrived0 = send_last(terms0, mesh_shape, (1, 3, 2))
    four1 = join(own1, after(peers1, leaving0))
    own0 = sum_last(terms0, arrived0, mesh_shape)
    more1 = exchange_bits(four1, mesh_shape, [2])
    late1 = exchange_bits(four1, mesh_shape, [1])
    peers0 = gather_last(own0, mesh_shape, (3, 1, 2))
    more1 = after(more1, own0)
    latest1 = exchange_bits(more1, mesh_shape, [1])
    four0 = join(own0, after(peers0, more1, late1))
    held1 = jnp.concatenate([four1, more1], axis=0)
    other_held1 = exchange_bits(held1, mesh_shape, [0])
    more0 = exchange_bits(four0, mesh_shape, [2])
    late0 = exchange_bits(four0, mesh_shape, [1])
    inner_out, outer_out = hbm(layers, width, columns), hbm(layers, columns, width)

    def staging(blocks):
        return [
            vmem(2, blocks, depth, LANES, dtype=F32),
            pltpu.SemaphoreType.DMA((2, blocks)),
        ]

    small_rows = vmem(BLOCKS, SMALL_ROWS, LANES, dtype=F32)

    def unpack(name, plan, pieces, grads=()):
        count, blocks = len(pieces), sum(p.shape[0] for p in pieces)
        return call(
            functools.partial(unpack_some, mesh_shape, images_all, plan),
            name,
            (*in_vmem(pieces), *grads[:2], *in_vmem(grads[2:])),
            (inner_out, outer_out, small_rows),
            staging(blocks),
            in_specs=[VMEM] * count + ([HBM, HBM, VMEM] if grads else []),
            out_specs=[HBM] * 2 + [VMEM],
            aliases={count + number: number for number in range(len(grads))},
            us=blocks / 8,
        )

    more0, late0 = lax.optimization_barrier((more0, late0))
    late1, latest1 = after((late1, latest1), more0)
    latest0 = exchange_bits(more0, mesh_shape, [1])
    late1 = jnp.concatenate([late1, latest1], axis=0)
    other_late1 = exchange_bits(late1, mesh_shape, [0])
    held0 = jnp.concatenate([four0, more0], axis=0)
    other_held0 = exchange_bits(held0, mesh_shape, [0])
    other_late0 = exchange_bits(late0, mesh_shape, [0])
    grads = unpack(
        "unpack_kept",
        (
            (1, kept_block, 0),
            (1, sent_block, 0),
            (1, kept_block, QUARTER),
            (0, kept_block, 0),
            (0, kept_block, QUARTER),
        ),
        (held1, other_held1, late1, held0, late0),
    )
    grads = unpack(
        "unpack_others",
        ((1, sent_block, QUARTER), (0, sent_block, 0), (0, sent_block, QUARTER)),
        (other_late1, other_held0, other_late0),
        grads,
    )
    latest0, grads = lax.optimization_barrier((latest0, grads))
    other_latest0 = exchange_bits(latest0, mesh_shape, [0])
    grads = unpack("unpack_latest", ((0, kept_block, QUARTER + EIGHTH),), (latest0,), grads)
    row = (layers, width)
    small_shapes = (
        (patches, layers, patches), row, row, (layers, patches), row, row, row,
        (layers, columns), row, row, (layers, 2, 2),
    )
    stage, sems = staging(EIGHTH)
    (
        inner_grad, outer_grad, _, weight_grad, aff_scale_grad, aff_shift_grad, bias_grad,
        scale_grad, mixer_aff_scale_grad, mixer_aff_shift_grad, inner_bias_grad,
        outer_bias_grad, mixer_scale_grad, magnitudes,
    ) = call(
        functools.partial(unpack_rest, mesh_shape, images_all),
        "unpack_rest",
        (*in_vmem((other_latest0,)), *grads[:2], *in_vmem(grads[2:])),
        (inner_out, outer_out, small_rows, *(hbm(*shape) for shape in small_shapes)),
        [
            *(vmem(*shape, dtype=F32) for shape in small_shapes),
            stage,
            vmem(128, 256, dtype=F32),
            sems,
            pltpu.SemaphoreType.DMA((SMALL_OUTS,)),
        ],
        in_specs=[VMEM] + [HBM] * 2 + [VMEM],
        out_specs=[HBM] * 2 + [VMEM] + [HBM] * SMALL_OUTS,
        aliases={1: 0, 2: 1, 3: 2},
        us=2,
    )
    return (
        jnp.transpose(output, (0, 2, 1, 3)),
        jnp.transpose(input_grad, (0, 2, 1, 3)),
        aff_scale_grad,
        aff_shift_grad,
        jnp.transpose(weight_grad, (1, 0, 2)),
        bias_grad,
        scale_grad,
        mixer_aff_scale_grad,
        mixer_aff_shift_grad,
        inner_grad,
        inner_bias_grad,
        outer_grad,
        outer_bias_grad,
        mixer_scale_grad,
        magnitudes,
    )


def solution(mesh):
    split = P(None, "dp", None, None)
    owned = P("pipe", "dp", None, None)
    return jax.shard_map(
        functools.partial(on_device, dict(mesh.shape)),
        mesh=mesh,
        in_specs=(split,) * 3 + (P(),) * 12,
        out_specs=(owned,) * 2 + (P(),) * 13,
        check_vma=False,
    )
```

```python
import functools

import jax
import jax.numpy as jnp
from jax import lax
from jax.experimental import pallas as pl
from jax.experimental.pallas import tpu as pltpu
from jax.sharding import PartitionSpec as P

SQRT_HALF = 0.7071067811865476
INV_ROOT_TAU = 0.3989422804014327
AXES = ("dp", "pipe")
BLOCKS = 32
HALF = BLOCKS // 2
SCATTERED = 5
LANES = 384
SMALL_ROWS = 8
VECTOR_ROWS = 24
BF = jnp.bfloat16
F32 = jnp.float32
VMEM = pl.BlockSpec(memory_space=pltpu.VMEM)
HBM = pl.BlockSpec(memory_space=pltpu.HBM)
VMEM_LIMIT = 16 * 2**20

CROSS_AFF_SCALE, CROSS_AFF_SHIFT, CROSS_SCALE, CROSS_BIAS = 0, 1, 2, 3
MIXER_AFF_SCALE, MIXER_AFF_SHIFT, MIXER_OUT_BIAS, MIXER_SCALE = 4, 5, 6, 7
MIXER_IN_BIAS = 8
SQUARES = 12
CROSS_REST = 16


def dot(a, b, a_dim=1, b_dim=0):
    return lax.dot_general(
        a, b, (((a_dim,), (b_dim,)), ((), ())), preferred_element_type=F32
    )


def row_sum(values):
    return jnp.sum(values, axis=0, keepdims=True)


def phase_bits(mesh_shape):
    pipe_bits = [1 << b for b in range(mesh_shape["pipe"].bit_length() - 1)]
    dp_bits = [mesh_shape["pipe"] << b for b in range(mesh_shape["dp"].bit_length() - 1)]
    even = [pipe_bits[0], *pipe_bits[1:], *dp_bits]
    odd = list(even)
    odd[1], odd[2] = even[2], even[1]
    return even, odd


def block_code(mesh_shape, place):
    even, odd = phase_bits(mesh_shape)
    odd_place = place & 1
    code = jnp.int32(0)
    for even_bit, odd_bit in zip(even[:SCATTERED], odd[:SCATTERED]):
        bit = jnp.where(odd_place == 1, (place & odd_bit) != 0, (place & even_bit) != 0)
        code = 2 * code + bit.astype(jnp.int32)
    return code


def own_codes(mesh_shape):
    place = lax.axis_index("dp") * mesh_shape["pipe"] + lax.axis_index("pipe")
    return block_code(mesh_shape, place), block_code(mesh_shape, place ^ 1)


def kept_block(codes, slot):
    return codes[0] ^ slot


def sent_block(codes, slot):
    return codes[1] ^ slot


def inner_spot(block, rows, columns):
    across = columns // LANES
    row_at = pl.multiple_of((block // across) * rows, rows)
    return row_at, pl.multiple_of((block % across) * LANES, LANES)


def pack_halves(codes, block_at, kept_ref, sent_ref):
    @pl.loop(0, HALF)
    def _(slot):
        for block, out_ref in ((sent_block(codes, slot), sent_ref), (kept_block(codes, slot), kept_ref)):
            at = 0
            for piece in block_at(block):
                out_ref[slot, at : at + piece.shape[0], :] = piece
                at += piece.shape[0]


def pack_products(codes, inner_ref, outer_ref, kept_ref, sent_ref):
    depth = outer_ref.shape[0] // BLOCKS

    def block_at(block):
        row_at, column_at = inner_spot(block, depth, inner_ref.shape[1])
        outer_at = pl.multiple_of(block * depth, depth)
        return (
            inner_ref[pl.ds(row_at, depth), pl.ds(column_at, LANES)],
            outer_ref[pl.ds(outer_at, depth), :],
        )

    pack_halves(codes, block_at, kept_ref, sent_ref)


def read(ref, rows):
    return jnp.concatenate([ref[plane, rows, :] for plane in range(ref.shape[0])], axis=1)


def write(ref, rows, values):
    for plane in range(ref.shape[0]):
        ref[plane, rows, :] = values[:, plane * 128 : (plane + 1) * 128]


def rounded(values):
    return values.astype(BF).astype(F32)


def spread_rows(source_ref, target_ref):
    parts, patches, each, _ = source_ref.shape
    for part in range(parts):
        for patch in range(patches):
            base = (part * patches + patch) * each
            write(target_ref, slice(base, base + each), source_ref[part, patch].astype(F32))


def gather_rows(source_ref, target_ref):
    parts, patches, each, _ = target_ref.shape
    for part in range(parts):
        for patch in range(patches):
            base = (part * patches + patch) * each
            target_ref[part, patch] = read(source_ref, slice(base, base + each)).astype(BF)


def image_rows(image, patches, each):
    return pl.ds((image // each) * patches * each + image % each, patches, stride=each)


def row_tiles(rows):
    tile = max(t for t in range(16, 209, 16) if rows % t == 0)
    return [slice(at, at + tile) for at in range(0, rows, tile)]


def row_halves(rows):
    middle = -(-rows // 32) * 16
    return [slice(0, middle), slice(middle, rows)]


def cross_setup(mask_ref, weight_ref, bias_ref, kept_ref, keep_ref, bias_columns_ref, rows_ref):
    patches, layers, _ = weight_ref.shape
    padded = kept_ref.shape[2]
    for patch in range(patches):
        base = patch * layers
        weight = weight_ref[patch].astype(F32)
        rows_ref[0, base : base + layers, :] = weight[:, 0:128]
        rows_ref[1, base : base + layers, 0 : patches - 128] = weight[:, 128:]
    keep_ref[...] = jnp.zeros_like(keep_ref)
    kept_ref[...] = jnp.zeros_like(kept_ref)
    for layer in range(layers):
        weight = read(rows_ref, pl.ds(layer, patches, stride=layers))[:, 0:patches]
        for image in range(mask_ref.shape[0]):
            keep_row = mask_ref[image, layer : layer + 1, :].astype(F32)
            keep_ref[image, layer : layer + 1, 0:patches] = keep_row
            kept_ref[layer, image, 0:patches, 0:patches] = (weight * keep_row).astype(BF)
    bias_rows = jnp.concatenate([bias_ref[...], jnp.zeros((8 - layers, patches), F32)], axis=0)
    bias_rows = jnp.concatenate([bias_rows, jnp.zeros((8, 256 - patches), F32)], axis=1)
    bias_columns_ref[...] = jnp.transpose(bias_rows)[0:padded]


def cross_forward(
    layer, source_ref, target_ref, vectors_ref, kept_ref, bias_ref,
    aff_scale_ref, aff_shift_ref, scale_ref, low_ref, patches, each,
):
    aff_scale = aff_scale_ref[layer : layer + 1, :]
    aff_shift = aff_shift_ref[layer : layer + 1, :]
    scale = scale_ref[layer : layer + 1, :]
    branch_squares = jnp.zeros((1, LANES), F32)
    normed_squares = jnp.zeros((1, LANES), F32)
    for image in range(kept_ref.shape[1]):
        rows = image_rows(image, patches, each)
        stream = read(source_ref, rows)
        normed = aff_scale * stream + aff_shift
        low_ref[image, 0:patches, :] = normed.astype(BF)
        mixing = dot(kept_ref[layer, image], low_ref[image])
        branch = scale * (mixing + bias_ref[:, layer : layer + 1])[0:patches]
        write(target_ref, rows, rounded(stream + branch))
        branch_squares += row_sum(branch * branch)
        normed_squares += row_sum(normed * normed)
    vectors_ref[layer, SQUARES : SQUARES + 1, :] = branch_squares
    vectors_ref[layer, SQUARES + 1 : SQUARES + 2, :] = normed_squares


def mixer_hidden(
    layer, stream_ref, low_ref, fired_ref, slope_ref, vectors_ref,
    aff_scale_ref, aff_shift_ref, inner_ref, inner_bias_ref,
):
    aff_scale = aff_scale_ref[layer : layer + 1, :]
    aff_shift = aff_shift_ref[layer : layer + 1, :]
    tiles = row_tiles(stream_ref.shape[1])
    squares = jnp.zeros((1, LANES), F32)
    for rows in tiles:
        normed = aff_scale * read(stream_ref, rows) + aff_shift
        low_ref[rows, :] = normed.astype(BF)
        squares += row_sum(normed * normed)
    vectors_ref[layer, SQUARES + 3 : SQUARES + 4, :] = squares
    step = inner_ref.shape[1] // 3
    for part in range(3):
        at = slice(part * step, (part + 1) * step)
        for rows in tiles:
            hidden = dot(low_ref[rows, :], inner_ref[:, at]) + inner_bias_ref[layer : layer + 1, at]
            normal_cdf = 0.5 * (1.0 + lax.erf(hidden * SQRT_HALF))
            density = INV_ROOT_TAU * jnp.exp(-0.5 * hidden * hidden)
            fired_ref[rows, at] = (hidden * normal_cdf).astype(BF)
            slope_ref[rows, at] = (normal_cdf + hidden * density).astype(BF)


def mixer_backward(
    layer, upper_ref, low_ref, fired_ref, slope_ref, hidden_grad_ref, scaled_ref, inner_ref,
    outer_ref, inner_grad_ref, outer_grad_ref, vectors_ref, scale_ref,
):
    scale = scale_ref[layer : layer + 1, :]
    tiles = row_tiles(upper_ref.shape[1])
    bias = jnp.zeros((1, LANES), F32)
    for rows in tiles:
        result_grad = read(upper_ref, rows) * scale
        bias += row_sum(result_grad)
        scaled_ref[rows, :] = result_grad.astype(BF)
    vectors_ref[layer, MIXER_OUT_BIAS : MIXER_OUT_BIAS + 1, :] = bias
    columns = inner_ref.shape[1]
    step = 2 * LANES
    tiles = row_halves(upper_ref.shape[1])
    for part in range(columns // step):
        at = slice(part * step, (part + 1) * step)
        outer_grad_ref[at, :] = dot(fired_ref[:, at], scaled_ref[...], 0, 0).astype(BF)
        inner_bias = jnp.zeros((1, step), F32)
        for rows in tiles:
            hidden_grad = dot(scaled_ref[rows, :], outer_ref[at, :], 1, 1) * slope_ref[
                rows, at
            ].astype(F32)
            inner_bias += row_sum(hidden_grad)
            hidden_grad_ref[rows, at] = hidden_grad.astype(BF)
        for piece in range(step // LANES):
            row = MIXER_IN_BIAS + part * (step // LANES) + piece
            vectors_ref[layer, row : row + 1, :] = inner_bias[:, piece * LANES : (piece + 1) * LANES]
        inner_grad_ref[:, at] = dot(low_ref[...], hidden_grad_ref[:, at], 0, 0).astype(BF)


def mixer_input_grad(
    layer, upper_ref, stream_ref, hidden_grad_ref, target_ref, inner_ref, vectors_ref,
    aff_scale_ref,
):
    aff_scale = aff_scale_ref[layer : layer + 1, :]
    scale_grad = jnp.zeros((1, LANES), F32)
    shift_grad = jnp.zeros((1, LANES), F32)
    for rows in row_halves(upper_ref.shape[1]):
        normed_grad = dot(hidden_grad_ref[rows, :], inner_ref[...], 1, 1)
        scale_grad += row_sum(normed_grad * read(stream_ref, rows))
        shift_grad += row_sum(normed_grad)
        write(target_ref, rows, rounded(read(upper_ref, rows) + normed_grad * aff_scale))
    vectors_ref[layer, MIXER_AFF_SCALE : MIXER_AFF_SCALE + 1, :] = scale_grad
    vectors_ref[layer, MIXER_AFF_SHIFT : MIXER_AFF_SHIFT + 1, :] = shift_grad


def cross_backward(
    layer, stream_ref, upper_ref, target_ref, weight_grad_ref, vectors_ref, kept_ref, keep_ref,
    bias_ref, aff_scale_ref, aff_shift_ref, scale_ref, low_ref, mixing_low_ref, patches, each,
):
    padded = kept_ref.shape[2]
    aff_scale = aff_scale_ref[layer : layer + 1, :]
    aff_shift = aff_shift_ref[layer : layer + 1, :]
    scale = scale_ref[layer : layer + 1, :]
    aff_scale_grad = jnp.zeros((1, LANES), F32)
    aff_shift_grad = jnp.zeros((1, LANES), F32)
    scale_grad = jnp.zeros((1, LANES), F32)
    bias_grad = jnp.zeros((8, padded), F32)
    weight_grad = jnp.zeros((padded, padded), F32)
    ones = jnp.ones((8, LANES), BF)
    for image in range(kept_ref.shape[1]):
        rows = image_rows(image, patches, each)
        stream = read(stream_ref, rows)
        upper = read(upper_ref, rows)
        low_ref[image, 0:patches, :] = (aff_scale * stream + aff_shift).astype(BF)
        mixing_low_ref[image, 0:patches, :] = (upper * scale).astype(BF)
        kept = kept_ref[layer, image]
        shifted = dot(kept, low_ref[image]) + bias_ref[:, layer : layer + 1]
        scale_grad += row_sum(upper * shifted[0:patches])
        mixing_low = mixing_low_ref[image]
        bias_grad += dot(ones, mixing_low, 1, 1)
        weight_grad += (
            dot(mixing_low, low_ref[image], 1, 1) * keep_ref[image, layer : layer + 1, :]
        )
        normed_grad = dot(kept, mixing_low, 0, 0)[0:patches]
        aff_scale_grad += row_sum(normed_grad * stream)
        aff_shift_grad += row_sum(normed_grad)
        write(target_ref, rows, rounded(upper + normed_grad * aff_scale))
    weight_grad_ref[0:padded, 0:padded] = weight_grad
    vectors_ref[layer, CROSS_AFF_SCALE : CROSS_AFF_SCALE + 1, :] = aff_scale_grad
    vectors_ref[layer, CROSS_AFF_SHIFT : CROSS_AFF_SHIFT + 1, :] = aff_shift_grad
    vectors_ref[layer, CROSS_SCALE : CROSS_SCALE + 1, :] = scale_grad
    vectors_ref[layer, CROSS_BIAS : CROSS_BIAS + 1, 0:padded] = bias_grad[0:1]


def clear_padding(*padded_refs, patches):
    for ref in padded_refs:
        images, padded, width = ref.shape
        for image in range(images):
            ref[image, padded - 16 :, :] = jnp.zeros((16, width), BF)


def first_kernel(
    mesh_shape,
    x_hbm, mask_hbm, g_hbm, inner_hbm, outer_hbm, cross_weight_hbm, cross_bias_hbm,
    inner_bias_hbm, mixer_aff_shift_hbm, *parameters_hbm_and_rest,
):
    parameters_hbm, rest = parameters_hbm_and_rest[:6], parameters_hbm_and_rest[6:]
    parameters, rest = rest[:6], rest[6:]
    cross_aff_scale, cross_aff_shift, cross_scale, mixer_aff_scale, outer_bias, mixer_scale = parameters
    (
    kept, sent, vectors, s0, s1, s2, s3, g_rows, low0, fired0, slope0, result0, fired1, slope1,
    inner0, outer0, inner1, outer1, kept_weight, keep, bias_columns,
    x_in, mask_in, g_in, cross_weight, cross_bias, inner_bias, mixer_aff_shift, weight_rows, padded_low,
    low1, scaled, inner_grad, outer_grad, sems,
    ) = rest
    _, patches, each, _ = x_in.shape
    per = x_in.shape[0]
    own = lax.axis_index("pipe") * per
    mine = pl.ds(own, per)
    groups = (
        ((cross_weight_hbm, cross_weight), (mask_hbm.at[mine], mask_in), (cross_bias_hbm, cross_bias)),
        ((x_hbm.at[mine], x_in), *zip(parameters_hbm, parameters)),
        (
            (inner_hbm.at[0], inner0),
            (inner_bias_hbm, inner_bias),
            (mixer_aff_shift_hbm, mixer_aff_shift),
        ),
        ((outer_hbm.at[0], outer0),),
        ((inner_hbm.at[1], inner1),),
        ((g_hbm.at[mine], g_in), (outer_hbm.at[1], outer1)),
    )
    arrivals, number = [], 0
    for group in groups:
        arrivals.append([])
        for source, target in group:
            copy = pltpu.make_async_copy(source, target, sems.at[number])
            copy.start()
            arrivals[-1].append(copy)
            number += 1

    def wait_for(group):
        for copy in arrivals[group]:
            copy.wait()

    vectors[...] = jnp.zeros_like(vectors)
    clear_padding(padded_low, patches=patches)
    wait_for(0)
    masks = mask_in[...].reshape((per * each,) + mask_in.shape[2:])
    cross_setup(masks, cross_weight, cross_bias, kept_weight, keep, bias_columns, weight_rows)
    wait_for(1)
    spread_rows(x_in, s0)
    cross = (kept_weight, bias_columns, cross_aff_scale, cross_aff_shift, cross_scale, padded_low)
    cross_forward(0, s0, s1, vectors, *cross, patches, each)
    wait_for(2)
    mixer = (mixer_aff_scale, mixer_aff_shift)
    mixer_hidden(0, s1, low0, fired0, slope0, vectors, *mixer, inner0, inner_bias)
    wait_for(3)
    squares = jnp.zeros((1, LANES), F32)
    for rows in row_halves(s1.shape[1]):
        result = dot(fired0[rows, :], outer0[...]) + outer_bias[0:1, :]
        result0[rows, :] = result.astype(BF)
        branch = mixer_scale[0:1, :] * result
        write(s2, rows, rounded(read(s1, rows) + branch))
        squares += row_sum(branch * branch)
    vectors[0, SQUARES + 2 : SQUARES + 3, :] = squares
    cross_forward(1, s2, s3, vectors, *cross, patches, each)
    wait_for(4)
    mixer_hidden(1, s3, low1, fired1, slope1, vectors, *mixer, inner1, inner_bias)
    wait_for(5)
    spread_rows(g_in, g_rows)
    mixer_backward(
        1, g_rows, low1, fired1, slope1, slope1, scaled, inner1, outer1, inner_grad, outer_grad,
        vectors, mixer_scale,
    )
    pack_products(own_codes(mesh_shape), inner_grad, outer_grad, kept, sent)


def second_kernel(
    s2, s3, g_rows, hidden_grad, inner1, kept_weight, keep, bias_columns, vectors_in,
    cross_aff_scale, cross_aff_shift, cross_scale, mixer_aff_scale,
    g2, weight_grad, vectors,
    g1, padded_low, padded_mixing, *, each,
):
    patches = s2.shape[1] // padded_low.shape[0]
    vectors[...] = vectors_in[...]
    clear_padding(padded_low, padded_mixing, patches=patches)
    mixer_input_grad(1, g_rows, s3, hidden_grad, g1, inner1, vectors, mixer_aff_scale)
    cross_backward(
        1, s2, g1, g2, weight_grad, vectors, kept_weight, keep, bias_columns,
        cross_aff_scale, cross_aff_shift, cross_scale, padded_low, padded_mixing, patches, each,
    )


def third_kernel(
    mesh_shape,
    s1, g2, low0, fired0, slope0, inner0, outer0, s3, g_rows, fired1, outer1, vectors_in,
    mixer_aff_scale, outer_bias, mixer_scale,
    kept, sent, g1, vectors, leaving,
    hidden_grad, scaled, inner_grad, outer_grad,
):
    vectors[...] = vectors_in[...]
    mixer_backward(
        0, g2, low0, fired0, slope0, hidden_grad, scaled, inner0, outer0, inner_grad, outer_grad,
        vectors, mixer_scale,
    )
    pack_products(own_codes(mesh_shape), inner_grad, outer_grad, kept, sent)
    mixer_input_grad(0, g2, s1, hidden_grad, g1, inner0, vectors, mixer_aff_scale)
    squares = jnp.zeros((1, LANES), F32)
    scale_grad = jnp.zeros((1, LANES), F32)
    for rows in row_halves(s3.shape[1]):
        result = dot(fired1[rows, :], outer1[...]) + outer_bias[1:2, :]
        scale_grad += row_sum(read(g_rows, rows) * result)
        branch = mixer_scale[1:2, :] * result
        write(leaving, rows, read(s3, rows) + branch)
        squares += row_sum(branch * branch)
    vectors[1, SQUARES + 2 : SQUARES + 3, :] = squares
    vectors[1, MIXER_SCALE : MIXER_SCALE + 1, :] = scale_grad


def pack_small(weight_grads, vectors_ref, small_ref, patches):
    groups = -(-patches // SMALL_ROWS)
    rows = groups * SMALL_ROWS
    first, second = (grad[0:rows, 128:256] for grad in weight_grads)
    lane = lax.broadcasted_iota(jnp.int32, (rows, 128), 1)
    shared = jnp.where(lane < 64, first, pltpu.roll(second, 64, 1))
    blocks = [grad[0:rows, 0:128] for grad in weight_grads] + [shared]
    small_ref[...] = jnp.zeros_like(small_ref)
    for part, block in enumerate(blocks):
        small_ref[0:groups, :, part * 128 : (part + 1) * 128] = block.astype(BF).reshape(
            groups, SMALL_ROWS, 128
        )
    for layer, grad in enumerate(weight_grads):
        rest = jnp.transpose(grad[:, 128:256])[64 : 64 + SMALL_ROWS]
        vectors_ref[layer, CROSS_REST : CROSS_REST + SMALL_ROWS, 0:256] = rest
        for piece in range(VECTOR_ROWS // SMALL_ROWS):
            at = groups + layer * (VECTOR_ROWS // SMALL_ROWS) + piece
            small_ref[at] = vectors_ref[
                layer, piece * SMALL_ROWS : (piece + 1) * SMALL_ROWS, :
            ].astype(BF)


def fourth_kernel(
    mesh_shape,
    s0, g1, kept_weight, keep, bias_columns, weight_grad1, vectors_in, g2, result0, leaving,
    cross_aff_scale, cross_aff_shift, cross_scale,
    input_grad, output, kept, sent,
    g0, weight_grad0, vectors, small, padded_low, padded_mixing,
):
    _, patches, each, _ = input_grad.shape
    vectors[...] = vectors_in[...]
    clear_padding(padded_low, padded_mixing, patches=patches)
    cross_backward(
        0, s0, g1, g0, weight_grad0, vectors, kept_weight, keep, bias_columns,
        cross_aff_scale, cross_aff_shift, cross_scale, padded_low, padded_mixing, patches, each,
    )
    scale_grad = jnp.zeros((1, LANES), F32)
    for rows in row_tiles(g2.shape[1]):
        scale_grad += row_sum(read(g2, rows) * result0[rows, :].astype(F32))
    vectors[0, MIXER_SCALE : MIXER_SCALE + 1, :] = scale_grad
    pack_small((weight_grad0, weight_grad1), vectors, small, patches)
    pack_halves(own_codes(mesh_shape), lambda block: (small[block],), kept, sent)
    gather_rows(g0, input_grad)
    gather_rows(leaving, output)


def exchange_bits(values, mesh_shape, phases):
    even, odd = phase_bits(mesh_shape)
    places = range(mesh_shape["dp"] * mesh_shape["pipe"])

    def partner(place):
        for phase in phases:
            place ^= (odd if place & 1 else even)[phase]
        return place

    return lax.ppermute(values, AXES, [(i, partner(i)) for i in places])


def across(slot):
    return [phase for phase, bit in ((SCATTERED - 2, 2), (SCATTERED - 1, 1)) if slot & bit]


def part_sum(terms, start, stop):
    return sum(t[start:stop].astype(F32) for t in terms)


def joint_sum(families, start, stop):
    sums = [part_sum(terms, start, stop).astype(BF) for terms in families]
    return sums[0] if len(sums) == 1 else jnp.concatenate(sums, axis=1)


def halve(terms, width, mesh_shape, phase):
    half = width // 2
    leaving = part_sum(terms, half, width).astype(BF)
    return leaving, terms + [exchange_bits(leaving, mesh_shape, [phase])]


def halve_all(families, width, mesh_shape, phase):
    half = width // 2
    arrived = exchange_bits(joint_sum(families, half, width), mesh_shape, [phase])
    grown, at = [], 0
    for terms in families:
        rows = terms[0].shape[1]
        grown.append(terms + [arrived[:, at : at + rows]])
        at += rows
    return arrived, grown


def send_last(families, mesh_shape, slots):
    leaving = [joint_sum(families, slot, slot + 1) for slot in slots]
    return leaving, [
        exchange_bits(block, mesh_shape, across(slot)) for slot, block in zip(slots, leaving)
    ]


def sum_last(families, arrived, mesh_shape):
    sums = [part_sum(terms, 0, 1) for terms in families]
    total = sums[0] if len(sums) == 1 else jnp.concatenate(sums, axis=1)
    total = total + sum(a.astype(F32) for a in arrived)
    for phase in range(SCATTERED, len(phase_bits(mesh_shape)[0])):
        total = total.astype(BF)
        total = total.astype(F32) + exchange_bits(total, mesh_shape, [phase]).astype(F32)
    return total.astype(BF)


def gather_last(own, mesh_shape, slots):
    return {slot: exchange_bits(own, mesh_shape, across(slot)) for slot in slots}


def join(own, arrived):
    return jnp.concatenate([own, arrived[1], arrived[2], arrived[3]], axis=0)


def double(held, mesh_shape, phase):
    return jnp.concatenate([held, exchange_bits(held, mesh_shape, [phase])], axis=0)


def after(values, *others):
    return lax.optimization_barrier((values, *others))[0]


def unpack_pieces(
    mesh_shape, images_all, plan, pieces, inner_out, outer_out, stage, sems, meanwhile=None
):
    codes = own_codes(mesh_shape)
    depth = stage.shape[2]
    columns = inner_out.shape[2]
    first = [0]
    for values in pieces:
        first.append(first[-1] + values.shape[0])

    def copies(number, slot):
        layer, block_of, base = plan[number]
        block = block_of(codes, slot + base)
        row_at, column_at = inner_spot(block, depth, columns)
        outer_at = pl.multiple_of(block * depth, depth)
        index = first[number] + slot
        return (
            pltpu.make_async_copy(
                stage.at[0, index],
                inner_out.at[layer, pl.ds(row_at, depth), pl.ds(column_at, LANES)],
                sems.at[0, index],
            ),
            pltpu.make_async_copy(
                stage.at[1, index], outer_out.at[layer, pl.ds(outer_at, depth), :], sems.at[1, index]
            ),
        )

    for number, values in enumerate(pieces):

        @pl.loop(0, values.shape[0])
        def _(slot):
            for kind, copy in enumerate(copies(number, slot)):
                block = values[slot, kind * depth : (kind + 1) * depth, :]
                stage[kind, first[number] + slot] = block.astype(F32) / images_all
                copy.start()

    if meanwhile is not None:
        meanwhile()
    for number, values in enumerate(pieces):

        @pl.loop(0, values.shape[0])
        def _(slot):
            for copy in copies(number, slot):
                copy.wait()


QUARTER, EIGHTH = HALF // 2, HALF // 4
SMALL_OUTS = 11


def unpack_small(mesh_shape, plan, pieces, small_rows, depth):
    codes = own_codes(mesh_shape)
    for (layer, block_of, base), values in zip(plan, pieces):
        if layer == 0:

            @pl.loop(0, values.shape[0])
            def _(slot):
                small_rows[block_of(codes, slot + base)] = values[slot, 2 * depth :, :].astype(F32)


def unpack_some(mesh_shape, images_all, plan, *refs):
    inner_out, outer_out, small_rows, stage, sems = refs[-5:]
    pieces = refs[: len(plan)]
    unpack_pieces(mesh_shape, images_all, plan, pieces, inner_out, outer_out, stage, sems)
    unpack_small(mesh_shape, plan, pieces, small_rows, stage.shape[2])


def unpack_rest(
    mesh_shape, images_all, other_late, inner_in, outer_in, small_in,
    inner_out, outer_out, small_rows, *small_outs_and_rest,
):
    small_outs, rest = small_outs_and_rest[:SMALL_OUTS], small_outs_and_rest[SMALL_OUTS:]
    buffers, (stage, rest_rows, sems, small_sems) = rest[:SMALL_OUTS], rest[SMALL_OUTS:]
    (
        weight_out, aff_scale_out, aff_shift_out, cross_bias_out, cross_scale_out,
        mixer_aff_scale_out, mixer_aff_shift_out, inner_bias_out, outer_bias_out,
        mixer_scale_out, magnitudes_out,
    ) = buffers
    small_copies = [
        pltpu.make_async_copy(buffer, out, small_sems.at[number])
        for number, (buffer, out) in enumerate(zip(buffers, small_outs))
    ]
    patches, layers, _ = weight_out.shape
    plan, pieces = ((0, sent_block, QUARTER + EIGHTH),), (other_late,)

    def small_gradients():
        unpack_small(mesh_shape, plan, pieces, small_rows, stage.shape[2])
        groups = -(-patches // SMALL_ROWS)
        weights = (small_rows[0:groups] / images_all).reshape(groups * SMALL_ROWS, LANES)[0:patches]
        parts = VECTOR_ROWS // SMALL_ROWS
        lane = lax.broadcasted_iota(jnp.int32, (patches, 128), 1)
        for layer in range(layers):
            row = slice(layer, layer + 1)
            at = groups + layer * parts
            vectors = (small_rows[at : at + parts] / images_all).reshape(VECTOR_ROWS, LANES)
            rest_rows[...] = jnp.zeros_like(rest_rows)
            rest_rows[64 : 64 + SMALL_ROWS, :] = vectors[CROSS_REST:, 0:256]
            rest = jnp.transpose(rest_rows[...])[0:patches]
            shared = weights[:, 256:384]
            if layer:
                shared = pltpu.roll(shared, 64, 1)
            last = jnp.where(lane < 64, shared, rest)
            weight_out[:, layer, 0:128] = weights[:, layer * 128 : (layer + 1) * 128]
            weight_out[:, layer, 128:] = last[:, 0 : patches - 128]
            for out, index in (
                (aff_scale_out, CROSS_AFF_SCALE),
                (aff_shift_out, CROSS_AFF_SHIFT),
                (cross_scale_out, CROSS_SCALE),
                (mixer_aff_scale_out, MIXER_AFF_SCALE),
                (mixer_aff_shift_out, MIXER_AFF_SHIFT),
                (outer_bias_out, MIXER_OUT_BIAS),
                (mixer_scale_out, MIXER_SCALE),
            ):
                out[row, :] = vectors[index : index + 1]
            cross_bias_out[row, :] = vectors[CROSS_BIAS : CROSS_BIAS + 1, 0:patches]
            for piece in range(SQUARES - MIXER_IN_BIAS):
                index = MIXER_IN_BIAS + piece
                inner_bias_out[row, piece * LANES : (piece + 1) * LANES] = vectors[index : index + 1]
            squares = vectors[SQUARES : SQUARES + 4] / (patches * LANES)
            means = jnp.sqrt(jnp.sum(squares, axis=1, keepdims=True))
            for kind in range(2):
                for which in range(2):
                    index = 2 * kind + which
                    magnitudes_out[layer, kind : kind + 1, which : which + 1] = means[index : index + 1]
        for copy in small_copies:
            copy.start()

    unpack_pieces(
        mesh_shape, images_all, plan, pieces, inner_out, outer_out, stage, sems, small_gradients
    )
    for copy in small_copies:
        copy.wait()


def call(kernel, name, args, outs, scratch, in_specs=None, out_specs=None, aliases=None, us=1):
    return pl.pallas_call(
        kernel,
        out_shape=outs,
        in_specs=[VMEM] * len(args) if in_specs is None else in_specs,
        out_specs=[VMEM] * len(outs) if out_specs is None else out_specs,
        scratch_shapes=scratch,
        input_output_aliases=aliases or {},
        compiler_params=pltpu.CompilerParams(vmem_limit_bytes=VMEM_LIMIT),
        cost_estimate=pl.CostEstimate(
            flops=int(us * 1e9), bytes_accessed=int(us * 3e6), transcendentals=0
        ),
        name=name,
    )(*args)


def in_vmem(arrays):
    return [pltpu.with_memory_space_constraint(a, pltpu.VMEM) for a in arrays]


def in_hbm(arrays):
    return [pltpu.with_memory_space_constraint(a, pltpu.HBM) for a in arrays]


def on_device(
    mesh_shape,
    inputs,
    patch_masks,
    out_grad,
    cross_aff_scale,
    cross_aff_shift,
    cross_weight,
    cross_bias,
    cross_scale,
    mixer_aff_scale,
    mixer_aff_shift,
    mixer_in,
    mixer_in_bias,
    mixer_out,
    mixer_out_bias,
    mixer_scale,
):
    micros, each, patches, width = inputs.shape
    layers, _, columns = mixer_in.shape
    per = micros // mesh_shape["pipe"]
    images = per * each
    padded = -(-patches // 16) * 16
    rows = images * patches
    depth = width * columns // (BLOCKS * LANES)
    images_all = micros * each * mesh_shape["dp"]
    x_rows = jnp.transpose(inputs, (0, 2, 1, 3))
    g_rows = jnp.transpose(out_grad, (0, 2, 1, 3))
    weight_rows = jnp.transpose(cross_weight, (1, 0, 2))

    def vmem(*shape, dtype=BF):
        return pltpu.VMEM(shape, dtype)

    def hbm(*shape, dtype=F32):
        return jax.ShapeDtypeStruct(shape, dtype)

    stream = vmem(width // 128, rows, 128, dtype=F32)
    hidden = vmem(rows, columns)
    inner, outer = vmem(width, columns), vmem(columns, width)
    vectors = vmem(layers, VECTOR_ROWS, LANES, dtype=F32)
    padded_images = vmem(images, padded, width)
    local = (per, patches, each, width)
    first = call(
        functools.partial(first_kernel, mesh_shape),
        "forward",
        in_hbm((
            x_rows, patch_masks, g_rows, mixer_in, mixer_out, weight_rows, cross_bias,
            mixer_in_bias, mixer_aff_shift, cross_aff_scale, cross_aff_shift, cross_scale,
            mixer_aff_scale, mixer_out_bias, mixer_scale,
        )),
        (
            *[vmem(layers, width, dtype=F32)] * 6,
            vmem(HALF, 2 * depth, LANES),
            vmem(HALF, 2 * depth, LANES),
            vectors,
            *[stream] * 5,
            vmem(rows, width),
            hidden,
            hidden,
            vmem(rows, width),
            hidden,
            hidden,
            inner,
            outer,
            inner,
            outer,
            vmem(layers, images, padded, padded),
            vmem(images, 8, padded, dtype=F32),
            vmem(padded, 8, dtype=F32),
        ),
        [
            vmem(*local),
            vmem(per, each, layers, patches, dtype=jnp.int32),
            vmem(*local),
            vmem(patches, layers, patches),
            vmem(layers, patches, dtype=F32),
            vmem(layers, columns, dtype=F32),
            vmem(layers, width, dtype=F32),
            vmem(2, layers * patches, 128, dtype=F32),
            padded_images,
            vmem(rows, width),
            vmem(rows, width),
            inner,
            outer,
            pltpu.SemaphoreType.DMA((17,)),
        ],
        in_specs=[HBM] * 15,
        us=18,
    )
    aff_scale, aff_shift, scale, mixer_aff, result_bias, result_scale = in_vmem(first[:6])
    (
        kept1, sent1, sums, s0, s1, s2, s3, upper, low0, fired0, slope0, result0, fired1,
        hidden_grad1, inner0, outer0, inner1, outer1, kept_weight, keep, bias_columns,
    ) = first[6:]
    g2, weight_grad1, sums = call(
        functools.partial(second_kernel, each=each),
        "last_layer",
        (
            *in_vmem((
                s2, s3, upper, hidden_grad1, inner1, kept_weight, keep, bias_columns, sums,
            )),
            aff_scale, aff_shift, scale, mixer_aff,
        ),
        (stream, vmem(256, 256, dtype=F32), vectors),
        [stream, padded_images, padded_images],
        us=4,
    )
    main1 = [kept1, exchange_bits(sent1, mesh_shape, [0])]
    leaving1, main1 = halve(main1, HALF, mesh_shape, 1)
    g2 = after(g2, leaving1)
    halves = vmem(HALF, 2 * depth, LANES)
    kept0, sent0, g1, sums, leaving = call(
        functools.partial(third_kernel, mesh_shape),
        "first_feed_forward",
        (
            *in_vmem((
                s1, g2, low0, fired0, slope0, inner0, outer0, s3, upper, fired1, outer1, sums,
            )),
            mixer_aff, result_bias, result_scale,
        ),
        (halves, halves, stream, vectors, stream),
        [hidden, vmem(rows, width), inner, outer],
        us=9,
    )
    sent0, sums = lax.optimization_barrier((sent0, sums, main1[-1]))[:2]
    main0 = [kept0, exchange_bits(sent0, mesh_shape, [0])]
    leaving1, main1 = halve(main1, HALF // 2, mesh_shape, 2)
    sums = after(sums, leaving1)
    halves = vmem(HALF, SMALL_ROWS, LANES)
    input_grad, output, kept_small, sent_small = call(
        functools.partial(fourth_kernel, mesh_shape),
        "first_cross",
        (
            *in_vmem((
                s0, g1, kept_weight, keep, bias_columns, weight_grad1, sums, g2, result0, leaving,
            )),
            aff_scale, aff_shift, scale,
        ),
        (hbm(*local, dtype=BF), hbm(*local, dtype=BF), halves, halves),
        [
            stream,
            vmem(256, 256, dtype=F32),
            vectors,
            vmem(BLOCKS, SMALL_ROWS, LANES),
            padded_images,
            padded_images,
        ],
        us=5,
    )
    small = [kept_small, exchange_bits(sent_small, mesh_shape, [0])]
    _, main0 = halve(main0, HALF, mesh_shape, 1)
    _, small = halve(small, HALF, mesh_shape, 1)
    own1 = sum_last([main1], send_last([main1], mesh_shape, (1, 3, 2))[1], mesh_shape)
    main0[-1], small[-1], own1 = lax.optimization_barrier((main0[-1], small[-1], own1))
    width0 = HALF // 2
    terms0 = [[t[:width0] for t in main0], [t[:width0] for t in small]]
    _, terms0 = halve_all(terms0, width0, mesh_shape, 2)
    peers1 = gather_last(own1, mesh_shape, (1, 2, 3))
    leaving0, arrived0 = send_last(terms0, mesh_shape, (1, 3, 2))
    four1 = join(own1, after(peers1, leaving0))
    own0 = sum_last(terms0, arrived0, mesh_shape)
    more1 = exchange_bits(four1, mesh_shape, [2])
    late1 = exchange_bits(four1, mesh_shape, [1])
    peers0 = gather_last(own0, mesh_shape, (3, 1, 2))
    more1 = after(more1, own0)
    latest1 = exchange_bits(more1, mesh_shape, [1])
    four0 = join(own0, after(peers0, more1, late1))
    held1 = jnp.concatenate([four1, more1], axis=0)
    other_held1 = exchange_bits(held1, mesh_shape, [0])
    more0 = exchange_bits(four0, mesh_shape, [2])
    late0 = exchange_bits(four0, mesh_shape, [1])
    inner_out, outer_out = hbm(layers, width, columns), hbm(layers, columns, width)

    def staging(blocks):
        return [
            vmem(2, blocks, depth, LANES, dtype=F32),
            pltpu.SemaphoreType.DMA((2, blocks)),
        ]

    small_rows = vmem(BLOCKS, SMALL_ROWS, LANES, dtype=F32)

    def unpack(name, plan, pieces, grads=()):
        count, blocks = len(pieces), sum(p.shape[0] for p in pieces)
        return call(
            functools.partial(unpack_some, mesh_shape, images_all, plan),
            name,
            (*in_vmem(pieces), *grads[:2], *in_vmem(grads[2:])),
            (inner_out, outer_out, small_rows),
            staging(blocks),
            in_specs=[VMEM] * count + ([HBM, HBM, VMEM] if grads else []),
            out_specs=[HBM] * 2 + [VMEM],
            aliases={count + number: number for number in range(len(grads))},
            us=blocks / 8,
        )

    more0, late0 = lax.optimization_barrier((more0, late0))
    late1, latest1 = after((late1, latest1), more0)
    latest0 = exchange_bits(more0, mesh_shape, [1])
    late1 = jnp.concatenate([late1, latest1], axis=0)
    other_late1 = exchange_bits(late1, mesh_shape, [0])
    held0 = jnp.concatenate([four0, more0], axis=0)
    other_held0 = exchange_bits(held0, mesh_shape, [0])
    other_late0 = exchange_bits(late0, mesh_shape, [0])
    grads = unpack(
        "unpack_kept",
        (
            (1, kept_block, 0),
            (1, sent_block, 0),
            (1, kept_block, QUARTER),
            (0, kept_block, 0),
            (0, kept_block, QUARTER),
        ),
        (held1, other_held1, late1, held0, late0),
    )
    grads = unpack(
        "unpack_others",
        ((1, sent_block, QUARTER), (0, sent_block, 0), (0, sent_block, QUARTER)),
        (other_late1, other_held0, other_late0),
        grads,
    )
    latest0, grads = lax.optimization_barrier((latest0, grads))
    other_latest0 = exchange_bits(latest0, mesh_shape, [0])
    grads = unpack("unpack_latest", ((0, kept_block, QUARTER + EIGHTH),), (latest0,), grads)
    row = (layers, width)
    small_shapes = (
        (patches, layers, patches), row, row, (layers, patches), row, row, row,
        (layers, columns), row, row, (layers, 2, 2),
    )
    stage, sems = staging(EIGHTH)
    (
        inner_grad, outer_grad, _, weight_grad, aff_scale_grad, aff_shift_grad, bias_grad,
        scale_grad, mixer_aff_scale_grad, mixer_aff_shift_grad, inner_bias_grad,
        outer_bias_grad, mixer_scale_grad, magnitudes,
    ) = call(
        functools.partial(unpack_rest, mesh_shape, images_all),
        "unpack_rest",
        (*in_vmem((other_latest0,)), *grads[:2], *in_vmem(grads[2:])),
        (inner_out, outer_out, small_rows, *(hbm(*shape) for shape in small_shapes)),
        [
            *(vmem(*shape, dtype=F32) for shape in small_shapes),
            stage,
            vmem(128, 256, dtype=F32),
            sems,
            pltpu.SemaphoreType.DMA((SMALL_OUTS,)),
        ],
        in_specs=[VMEM] + [HBM] * 2 + [VMEM],
        out_specs=[HBM] * 2 + [VMEM] + [HBM] * SMALL_OUTS,
        aliases={1: 0, 2: 1, 3: 2},
        us=2,
    )
    return (
        jnp.transpose(output, (0, 2, 1, 3)),
        jnp.transpose(input_grad, (0, 2, 1, 3)),
        aff_scale_grad,
        aff_shift_grad,
        jnp.transpose(weight_grad, (1, 0, 2)),
        bias_grad,
        scale_grad,
        mixer_aff_scale_grad,
        mixer_aff_shift_grad,
        inner_grad,
        inner_bias_grad,
        outer_grad,
        outer_bias_grad,
        mixer_scale_grad,
        magnitudes,
    )


def solution(mesh):
    split = P(None, "dp", None, None)
    owned = P("pipe", "dp", None, None)
    return jax.shard_map(
        functools.partial(on_device, dict(mesh.shape)),
        mesh=mesh,
        in_specs=(split,) * 3 + (P(),) * 12,
        out_specs=(owned,) * 2 + (P(),) * 13,
        check_vma=False,
    )
```
